32 devices in a mesh: pitch: 8 (over z, x), span: 4 (over y, core).
Axes of the slice: x: 2, y: 2, z: 4, core: 2. Of those that a mesh axis runs over, the one named last changes fastest.
Arguments:
- stator_state: float32 [5, 16, 256, 2048], P(None, None, 'span', 'pitch'), may hold values from -6 to 6
- rotor_state: float32 [5, 16, 256, 2048], P(None, None, 'span', 'pitch'), may hold values from -6 to 6
- jacobians: float32 [3, 5, 5], replicated, may hold values from -2.5 to 2.5
- field_mix: float32 [5, 5], replicated, may hold values from -2.5 to 2.5
- mode_blend: float32 [5, 2048], replicated, may hold values from 0.1 to 0.9
- rotor_offset: int32 [1], replicated, may hold values from 0 to 2047
Outputs:
- stator_next: float32 [5, 16, 256, 2048], P(None, None, 'span', 'pitch')
- rotor_next: float32 [5, 16, 256, 2048], P(None, None, 'span', 'pitch')
The draws below stay inside these ranges and needn't reach their ends.
Inputs may be any that keep to these rules, and one draw needn't show every extreme that they name: `rotor_offset`: the rotor's rotation against the stator, in whole pitch cells.
All inputs are finite; a program needn't handle non-finite values.
Results may differ from the reference program's by a relative error of at most 0.0001.
Values sent between devices are 32-bit elements; how exact they have to be, the bound alone decides.
No kernel may reach another device: no remote copies, remote signals or barrier semaphores. Data moves between devices by JAX's collectives and lax.ppermute only.
A program may use at most 192 MiB of HBM per device.

```python
import jax
import jax.numpy as jnp
from jax import lax

NP = 2048
FIELDS = 5
AX = 16
NR = 256


def block_levels(key, extent, pieces, least, top_value):
    def one(position, shards_of):
        heights = jax.random.uniform(jax.random.fold_in(jax.random.fold_in(key, 6), position), (shards_of,), jnp.float32, least / len(pieces), top_value / len(pieces))
        return jnp.repeat(jnp.exp(heights), extent[position] // shards_of).reshape((-1,) + (1,) * (len(extent) - position - 1))

    factor_of = one(*pieces[0])
    for cut in pieces[1:]:
        factor_of = factor_of * one(*cut)
    return factor_of


def scatter_about(stream_key, shape, spread, reach, cuts=(), kind=jnp.bfloat16):
    level = block_levels(stream_key, shape, cuts, -0.22, 0.18) if cuts else 1.0
    array = jax.random.normal(stream_key, shape, jnp.float32) * spread * level
    return jnp.minimum(jnp.maximum(array, -reach), reach).astype(kind)


def setup_inputs(seed: int = 0) -> dict:
    key_list = jax.random.split(jax.random.key(seed), 7)
    return {
        "stator_state": scatter_about(key_list[0], (FIELDS, AX, NR, NP), 1.0, 6.0, ((2, 4), (3, 8)), jnp.float32),
        "rotor_state": scatter_about(key_list[1], (FIELDS, AX, NR, NP), 1.0, 6.0, ((2, 4), (3, 8)), jnp.float32),
        "jacobians": scatter_about(key_list[2], (3, FIELDS, FIELDS), FIELDS ** -0.5, 2.5, (), jnp.float32),
        "field_mix": scatter_about(key_list[3], (FIELDS, FIELDS), FIELDS ** -0.5, 2.5, (), jnp.float32),
        "mode_blend": jnp.clip(jax.random.uniform(key_list[4], (FIELDS, NP), jnp.float32, 0.1, 0.9), 0.1, 0.9),
        "rotor_offset": jax.random.randint(key_list[5], (1,), 0, NP).astype(jnp.int32),
    }


time_step = 0.5
damping = 1.0 / 32.0


def hartley(planes):
    spectrum = jnp.fft.fft(planes, axis=-1)
    return jnp.real(spectrum) - jnp.imag(spectrum)


def block_update(state, before, after, jacobians):
    extended = jnp.concatenate([before, state, after], axis=1)
    extended = jnp.pad(extended, ((0, 0), (0, 0), (2, 2), (0, 0)))
    extended = jnp.pad(extended, ((0, 0), (0, 0), (0, 0), (2, 2)), mode="wrap")

    def one_layer(layer):
        window = lax.dynamic_slice_in_dim(extended, layer, 5, 1)
        centre = window[:, 2, 2:-2, 2:-2]
        neighbours = (
            (window[:, 3, 2:-2, 2:-2], window[:, 1, 2:-2, 2:-2], window[:, 4, 2:-2, 2:-2], window[:, 0, 2:-2, 2:-2]),
            (window[:, 2, 3:-1, 2:-2], window[:, 2, 1:-3, 2:-2], window[:, 2, 4:, 2:-2], window[:, 2, :-4, 2:-2]),
            (window[:, 2, 2:-2, 3:-1], window[:, 2, 2:-2, 1:-3], window[:, 2, 2:-2, 4:], window[:, 2, 2:-2, :-4]),
        )
        totals = jnp.zeros_like(centre)
        for course in range(3):
            plus_one, minus_one, plus_two, minus_two = neighbours[course]
            slopes = 0.5 * (plus_one - minus_one)
            totals = totals - jnp.einsum("fg,gsp->fsp", jacobians[course], slopes, precision=lax.Precision.HIGHEST)
            totals = totals - damping * (plus_two - 4.0 * plus_one + 6.0 * centre - 4.0 * minus_one + minus_two)
        return totals

    changes = lax.map(one_layer, jnp.arange(state.shape[1], dtype=jnp.int32))
    return state + time_step * jnp.moveaxis(changes, 0, 1)


def reference(stator_state, rotor_state, jacobians, field_mix, mode_blend, rotor_offset):
    offset = rotor_offset[0]
    stator_planes = jnp.stack([stator_state[:, -1], stator_state[:, -2]], axis=1)
    rotor_planes = rotor_state[:, 0:2]
    stator_modes = hartley(stator_planes)
    rotor_modes = hartley(jnp.roll(rotor_planes, offset, axis=-1))
    blend = mode_blend[:, None, None, :]
    stator_blend = blend * rotor_modes + (1.0 - blend) * stator_modes
    rotor_blend = blend * stator_modes + (1.0 - blend) * rotor_modes
    stator_back = hartley(stator_blend) / NP
    rotor_back = jnp.roll(hartley(rotor_blend) / NP, -offset, axis=-1)
    stator_ghost = jnp.einsum("fg,glrp->flrp", field_mix, stator_back, precision=lax.Precision.HIGHEST)
    rotor_ghost = jnp.einsum("fg,glrp->flrp", field_mix, rotor_back, precision=lax.Precision.HIGHEST)
    no_inflow = jnp.zeros((FIELDS, 2, NR, NP), jnp.float32)
    stator_next = block_update(stator_state, no_inflow, stator_ghost, jacobians)
    rotor_next = block_update(rotor_state, rotor_ghost[:, ::-1], no_inflow, jacobians)
    return stator_next, rotor_next
```

```python
import functools
import math

import jax
import jax.numpy as jnp
import ml_dtypes
import numpy as np
from jax import lax
from jax.experimental import pallas as pl
from jax.experimental.pallas import tpu as pltpu
from jax.sharding import PartitionSpec as P

NP = 2048
LANES = 128
OUTER = NP // LANES
PAIRS = OUTER // 2
UNITS = 12

time_step = 0.5
damping = 1.0 / 32.0
VMEM_LIMIT = 56 * 1024 * 1024


def mode_tables():
    inner = np.arange(LANES)
    out = np.zeros((PAIRS, 2 * LANES, 2 * LANES))

    def angles(outer):
        return 2.0 * math.pi * (np.outer(inner, outer + OUTER * inner) % NP) / NP

    for m in range(PAIRS):
        first, second = (0, PAIRS) if m == 0 else (m, OUTER - m)
        a, b = angles(first), angles(second)
        if m == 0:
            out[m, :LANES, :LANES] = np.cos(a) + np.sin(a)
            out[m, LANES:, LANES:] = np.cos(b) + np.sin(b)
        else:
            out[m, :LANES, :LANES] = np.cos(a)
            out[m, LANES:, :LANES] = np.sin(a)
            out[m, :LANES, LANES:] = np.sin(b)
            out[m, LANES:, LANES:] = np.cos(b)
    high = out.astype(ml_dtypes.bfloat16)
    low = (out - high.astype(np.float64)).astype(ml_dtypes.bfloat16)
    return high, low


def outer_order():
    order = [(0, PAIRS)] + [(m, OUTER - m) for m in range(1, PAIRS)]
    return np.array(order)


def fast_hartley(parts):
    count = len(parts)
    if count == 1:
        return parts
    half = count // 2
    even = fast_hartley(parts[0::2])
    odd = fast_hartley(parts[1::2])
    turned = []
    for k in range(half):
        if k == 0:
            turned.append(odd[0])
        elif 4 * k == count:
            turned.append(odd[half - k])
        else:
            angle = 2.0 * math.pi * k / count
            turned.append(odd[k] * math.cos(angle) + odd[half - k] * math.sin(angle))
    return [even[k] + turned[k] for k in range(half)] + [even[k] - turned[k] for k in range(half)]


def split_dot(x, high, low, dims):
    x_high = x.astype(jnp.bfloat16)
    x_low = (x - x_high.astype(jnp.float32)).astype(jnp.bfloat16)
    dot = functools.partial(
        lax.dot_general, dimension_numbers=(dims, ((), ())), preferred_element_type=jnp.float32
    )
    return dot(x_high, high) + (dot(x_low, high) + dot(x_high, low))


def transform_kernel(fields, offset_ref, got_ref, blend_ref, high_ref, low_ref, out_ref, turn, work):
    rows, cols = got_ref.shape[2:]
    per = cols // LANES
    offset = offset_ref[0]
    whole, part = offset // LANES, offset % LANES
    chunk = 8 if rows % 8 == 0 else rows
    lane = lax.broadcasted_iota(jnp.int32, (chunk, LANES), 1)
    pairs = outer_order()

    def block(i):
        return i // per, slice((i % per) * LANES, (i % per + 1) * LANES)

    for i in range(OUTER):
        device, lanes = block(i)
        turn[i] = pltpu.roll(got_ref[device, 1, :, lanes], part, 1)
    for at in range(0, rows, chunk):
        span = slice(at, at + chunk)
        parts = []
        for i in range(OUTER):
            device, lanes = block(i)
            now = turn[(i - whole + OUTER) % OUTER, span, :]
            before = turn[(i - whole - 1 + OUTER) % OUTER, span, :]
            parts.append(jnp.where(lane >= part, now, before) - got_ref[device, 0, span, lanes])
        modes = fast_hartley(parts)
        for m in range(PAIRS):
            work[m, span, :LANES] = modes[pairs[m, 0]]
            work[m, span, LANES:] = modes[pairs[m, 1]]
    for m in range(PAIRS):
        got = split_dot(work[m], high_ref[m], low_ref[m], ((1,), (0,)))
        per_field = rows // fields
        got = jnp.concatenate(
            [
                got[f * per_field : (f + 1) * per_field] * blend_ref[m, f : f + 1, :]
                for f in range(fields)
            ],
            axis=0,
        )
        work[m] = split_dot(got, high_ref[m], low_ref[m], ((1,), (1,)))
    back = (LANES - part) % LANES
    for at in range(0, rows, chunk):
        span = slice(at, at + chunk)
        modes = [None] * OUTER
        for m in range(PAIRS):
            modes[pairs[m, 0]] = work[m, span, :LANES]
            modes[pairs[m, 1]] = work[m, span, LANES:]
        parts = fast_hartley(modes)
        for i in range(OUTER):
            device, lanes = block(i)
            out_ref[device, 0, span, lanes] = parts[i]
            turn[i, span, :] = pltpu.roll(parts[i], back, 1)
        for i in range(OUTER):
            device, lanes = block(i)
            now = turn[(i + whole) % OUTER, span, :]
            after = turn[(i + whole + 1) % OUTER, span, :]
            out_ref[device, 1, span, lanes] = jnp.where(lane < LANES - part, now, after)


def transform(received, offset, blend, fields):
    high, low = mode_tables()
    count, _, rows, cols = received.shape
    vmem = pl.BlockSpec(memory_space=pltpu.VMEM)
    return pl.pallas_call(
        functools.partial(transform_kernel, fields),
        out_shape=jax.ShapeDtypeStruct(received.shape, jnp.float32),
        in_specs=[pl.BlockSpec(memory_space=pltpu.SMEM)] + [vmem] * 4,
        out_specs=vmem,
        scratch_shapes=[
            pltpu.VMEM((OUTER, rows, LANES), jnp.float32),
            pltpu.VMEM((PAIRS, rows, 2 * LANES), jnp.float32),
        ],
        compiler_params=pltpu.CompilerParams(vmem_limit_bytes=VMEM_LIMIT),
        cost_estimate=pl.CostEstimate(
            flops=12 * rows * PAIRS * 4 * LANES * LANES, bytes_accessed=5_000_000, transcendentals=0
        ),
        name="modes",
    )(offset, received, blend, jnp.asarray(high), jnp.asarray(low))


def pack_kernel(stator_ref, rotor_ref, low_ref, high_ref, left_ref, right_ref):
    step = pl.program_id(0)
    fields, _, rows, cols = stator_ref.shape
    lane = lax.broadcasted_iota(jnp.int32, (rows, LANES), 1)
    for side, ref in enumerate((stator_ref, rotor_ref)):
        unit = 2 * step + side
        place, first = unit // UNITS, unit % UNITS * (2 * fields)
        left = jnp.zeros((rows, LANES), jnp.float32)
        right = jnp.zeros((rows, LANES), jnp.float32)
        for f in range(fields):
            low_ref[side, 0, f] = ref[f, 0, :2, :]
            high_ref[side, 0, f] = ref[f, 0, rows - 2 :, :]
            here = lane // 2 == f
            a, b = ref[f, 0, :, :LANES], ref[f, 0, :, cols - LANES :]
            left = jnp.where(here, pltpu.roll(a, 2 * f, 1) if f else a, left)
            right = jnp.where(here, pltpu.roll(b, 2 * f + 2, 1), right)
        left = pltpu.roll(left, first, 1)
        right = pltpu.roll(right, first, 1)

        fresh = (lane >= first) & (lane < first + 2 * fields)
        left_ref[place] = jnp.where(fresh, left, left_ref[place])
        right_ref[place] = jnp.where(fresh, right, right_ref[place])


def pack_edges(stator, rotor):
    fields, layers, rows, cols = stator.shape
    blocks = -(-2 * layers // UNITS)
    one = (fields, 1, rows, cols)
    edge = jax.ShapeDtypeStruct((2, layers, fields, 2, cols), jnp.float32)
    side = jax.ShapeDtypeStruct((blocks, rows, LANES), jnp.float32)
    edge_spec = pl.BlockSpec((2, 1, fields, 2, cols), lambda t: (0, t, 0, 0, 0))
    side_spec = pl.BlockSpec((blocks, rows, LANES), lambda t: (0, 0, 0))
    return pl.pallas_call(
        pack_kernel,
        grid=(layers,),
        out_shape=(edge, edge, side, side),
        in_specs=[
            pl.BlockSpec(one, lambda t: (0, t, 0, 0)),
            pl.BlockSpec(one, lambda t: (0, layers - 1 - t, 0, 0)),
        ],
        out_specs=(edge_spec, edge_spec, side_spec, side_spec),
        compiler_params=pltpu.CompilerParams(vmem_limit_bytes=VMEM_LIMIT),
        cost_estimate=pl.CostEstimate(
            flops=0, bytes_accessed=2 * 4 * stator.size, transcendentals=0
        ),
        name="edges",
    )(stator, rotor)


def stencil_kernel(
    layers, jac_ref, mix_ref, stator_hbm, rotor_hbm, low_ref, high_ref, left_ref, right_ref,
    stator_out, rotor_out, state, sems,
):
    t = pl.program_id(0)
    fields, _, rows, cols = stator_out.shape
    blocks = cols // LANES
    sources = (stator_hbm, rotor_hbm)

    def load(side, layer):
        taken = layer if side == 0 else layers - 1 - layer
        return pltpu.make_async_copy(
            sources[side].at[:, taken], state.at[side, :, layer + 2], sems.at[side, layer]
        )

    @pl.when(t == 0)
    def _():
        for layer in range(layers):
            for side in range(2):
                load(side, layer).start()
        state[:, :, 0:2] = jnp.zeros((2, fields, 2, rows, cols), jnp.float32)
        for layer in range(2):
            for side in range(2):
                load(side, layer).wait()

    @pl.when(t + 2 < layers)
    def _():
        for side in range(2):
            load(side, t + 2).wait()

    @pl.when(t == layers - 2)
    def _():
        for side in range(2):
            for ghost in range(2):
                for at in range(0, rows, 8):
                    span = slice(at, at + 8)
                    planes = [state[side, g, layers + 1 - ghost, span, :] for g in range(fields)]
                    for f in range(fields):
                        total = mix_ref[f * fields] * planes[0]
                        for g in range(1, fields):
                            total = total + mix_ref[f * fields + g] * planes[g]
                        state[side, f, layers + 2 + ghost, span, :] = total

    lane = lax.broadcasted_iota(jnp.int32, (8, LANES), 1)
    row = lax.broadcasted_iota(jnp.int32, (8, LANES), 0)
    here = t + 2
    pad = jnp.zeros((6, cols), jnp.float32)
    for side, out in ((0, stator_out), (1, rotor_out)):
        unit = 2 * t + side
        place, first = unit // UNITS, unit % UNITS * (2 * fields)
        turn = (LANES - first) % LANES
        for at in range(0, rows, 8):
            span = slice(at, at + 8)
            from_left = pltpu.roll(left_ref[place, span, :], turn, 1)
            from_right = pltpu.roll(right_ref[place, span, :], turn, 1)
            slopes, bases = [], []
            for f in range(fields):
                shift = (LANES - 2 * f) % LANES
                rim = jnp.where(
                    lane < LANES // 2,
                    pltpu.roll(from_right, shift, 1) if shift else from_right,
                    pltpu.roll(from_left, LANES - 2 * f - 2, 1),
                )
                if at == 0:
                    above = jnp.concatenate([pad, low_ref[side, 0, f]], axis=0)
                else:
                    above = state[side, f, here, at - 8 : at, :]
                if at + 8 == rows:
                    below = jnp.concatenate([high_ref[side, 0, f], pad], axis=0)
                else:
                    below = state[side, f, here, at + 8 : at + 16, :]
                centre = [state[side, f, here, span, b * LANES : (b + 1) * LANES] for b in range(blocks)]
                ring = centre + [rim]
                field_slopes, field_bases = [], []
                for b in range(blocks):
                    lanes = slice(b * LANES, (b + 1) * LANES)
                    now = centre[b]
                    nxt, prv = ring[b + 1], ring[b - 1]
                    up, down = above[:, lanes], below[:, lanes]
                    a_p1, a_m1 = state[side, f, here + 1, span, lanes], state[side, f, here - 1, span, lanes]
                    a_p2, a_m2 = state[side, f, here + 2, span, lanes], state[side, f, here - 2, span, lanes]
                    r_p1 = pltpu.roll(jnp.where(row < 1, down, now), 7, 0)
                    r_p2 = pltpu.roll(jnp.where(row < 2, down, now), 6, 0)
                    r_m1 = pltpu.roll(jnp.where(row >= 7, up, now), 1, 0)
                    r_m2 = pltpu.roll(jnp.where(row >= 6, up, now), 2, 0)
                    p_p1 = pltpu.roll(jnp.where(lane < 1, nxt, now), LANES - 1, 1)
                    p_p2 = pltpu.roll(jnp.where(lane < 2, nxt, now), LANES - 2, 1)
                    p_m1 = pltpu.roll(jnp.where(lane >= LANES - 1, prv, now), 1, 1)
                    p_m2 = pltpu.roll(jnp.where(lane >= LANES - 2, prv, now), 2, 1)
                    field_slopes.append((a_p1 - a_m1, r_p1 - r_m1, p_p1 - p_m1))
                    near = ((a_p1 + a_m1) + (r_p1 + r_m1)) + (p_p1 + p_m1)
                    far = ((a_p2 + a_m2) + (r_p2 + r_m2)) + (p_p2 + p_m2)
                    field_bases.append(
                        now * (1.0 - 18.0 * time_step * damping)
                        + (near * 4.0 - far) * (time_step * damping)
                    )
                slopes.append(field_slopes)
                bases.append(field_bases)
            for f in range(fields):
                totals = list(bases[f])
                for d in range(3):
                    for g in range(fields):
                        weight = jac_ref[((side * 3 + d) * fields + f) * fields + g]
                        for b in range(blocks):
                            totals[b] = totals[b] + weight * slopes[g][b][d]
                for b in range(blocks):
                    out[f, 0, span, b * LANES : (b + 1) * LANES] = totals[b]


def stencil(stator, rotor, low, high, left, right, weights, mix):
    fields, layers, rows, cols = stator.shape
    one = (fields, 1, rows, cols)
    smem = pl.BlockSpec(memory_space=pltpu.SMEM)
    hbm = pl.BlockSpec(memory_space=pl.ANY)
    edge_spec = pl.BlockSpec((2, 1, fields, 2, cols), lambda t: (0, t, 0, 0, 0))
    side_spec = pl.BlockSpec(left.shape, lambda t: (0, 0, 0))
    shape = jax.ShapeDtypeStruct(stator.shape, jnp.float32)
    return pl.pallas_call(
        functools.partial(stencil_kernel, layers),
        grid=(layers,),
        out_shape=(shape, shape),
        in_specs=[smem, smem, hbm, hbm, edge_spec, edge_spec, side_spec, side_spec],
        out_specs=(
            pl.BlockSpec(one, lambda t: (0, t, 0, 0)),
            pl.BlockSpec(one, lambda t: (0, layers - 1 - t, 0, 0)),
        ),
        scratch_shapes=[
            pltpu.VMEM((2, fields, layers + 4, rows, cols), jnp.float32),
            pltpu.SemaphoreType.DMA((2, layers)),
        ],
        compiler_params=pltpu.CompilerParams(vmem_limit_bytes=VMEM_LIMIT),
        cost_estimate=pl.CostEstimate(
            flops=60 * 2 * stator.size, bytes_accessed=16 * stator.size, transcendentals=0
        ),
        name="stencil",
    )(weights, mix, stator, rotor, low, high, left, right)


def close_kernel(weight_ref, modes_ref, stator_ref, rotor_ref, stator_out, rotor_out):
    fields, _, rows, cols = stator_ref.shape
    count = modes_ref.shape[0]
    step = modes_ref.shape[4]
    for side, (ref, out) in enumerate(((stator_ref, stator_out), (rotor_ref, rotor_out))):
        near, far = (1, 0) if side == 0 else (0, 1)
        for q in range(count):
            span = slice(q * step, (q + 1) * step)
            first = [modes_ref[q, side, g, 0] for g in range(fields)]
            second = [modes_ref[q, side, g, 1] for g in range(fields)]
            for f in range(fields):
                rim, inner = ref[f, near, span, :], ref[f, far, span, :]
                for g in range(fields):
                    at = (side * 2 * fields + f) * fields + g
                    weight_near = weight_ref[at]
                    weight_far = weight_ref[at + fields * fields]
                    rim = rim + (weight_near * first[g] + weight_far * second[g])
                    inner = inner + weight_far * first[g]
                out[f, near, span, :] = rim
                out[f, far, span, :] = inner


def close(modes, stator, rotor, weights):
    fields, layers, rows, cols = stator.shape
    count, _, _, _, step, _ = modes.shape
    group = max(1, count // 4)
    block = (fields, 2, rows // count * group, cols)
    specs = (
        pl.BlockSpec(block, lambda q: (0, layers // 2 - 1, q, 0)),
        pl.BlockSpec(block, lambda q: (0, 0, q, 0)),
    )
    shape = jax.ShapeDtypeStruct(stator.shape, jnp.float32)
    return pl.pallas_call(
        close_kernel,
        grid=(count // group,),
        out_shape=(shape, shape),
        in_specs=[
            pl.BlockSpec(memory_space=pltpu.SMEM),
            pl.BlockSpec((group,) + modes.shape[1:], lambda q: (q, 0, 0, 0, 0, 0)),
            *specs,
        ],
        out_specs=specs,
        input_output_aliases={2: 0, 3: 1},
        compiler_params=pltpu.CompilerParams(vmem_limit_bytes=VMEM_LIMIT),
        cost_estimate=pl.CostEstimate(
            flops=30 * modes.size, bytes_accessed=12 * modes.size, transcendentals=0
        ),
        name="interface",
    )(weights, modes, stator, rotor)


def exact_dot(a, b):
    return jnp.matmul(a, b, precision=lax.Precision.HIGHEST)


def shards(stator, rotor, jacobians, field_mix, mode_blend, rotor_offset):
    fields, layers, rows, cols = stator.shape
    count = lax.axis_size("pitch")
    spans = lax.axis_size("span")
    step = rows // count

    def by_owner(planes):
        return jnp.moveaxis(planes.reshape(fields, 2, count, step, cols), 2, 0)

    planes = jnp.stack([by_owner(stator[:, layers - 2 :][:, ::-1]), by_owner(rotor[:, :2])], axis=1)
    planes = planes.reshape(count, 2, fields * 2 * step, cols)
    received = lax.all_to_all(planes, "pitch", 0, 0, tiled=True)

    low, high, left, right = pack_edges(stator, rotor)
    ring = [(i, (i + 1) % count) for i in range(count)]
    line = [(i, i + 1) for i in range(spans - 1)]
    from_left = lax.ppermute(right, "pitch", ring)
    from_right = lax.ppermute(left, "pitch", [(b, a) for a, b in ring])
    from_below = lax.ppermute(high, "span", line)
    from_above = lax.ppermute(low, "span", [(b, a) for a, b in line])

    mirrored = jacobians * jnp.array([-1.0, 1.0, 1.0], jnp.float32)[:, None, None]
    courses = jnp.stack([jacobians, mirrored])
    weights = (-0.5 * time_step) * courses
    mixed = exact_dot(courses[:, 0], field_mix)
    far = (-time_step * damping) * field_mix
    near = (-0.5 * time_step) * mixed + (4.0 * time_step * damping) * field_mix
    signs = jnp.array([1.0, -1.0], jnp.float32)[:, None, None]
    rim_weights = jnp.stack([signs * near, signs * far], axis=1)

    stator_mid, rotor_mid = stencil(
        stator, rotor, from_below, from_above, from_left, from_right,
        weights.reshape(-1), field_mix.reshape(-1),
    )

    blend = mode_blend.reshape(fields, LANES, OUTER) * (1.0 / NP)
    blend = jnp.moveaxis(blend, 2, 0)[outer_order().reshape(-1)]
    blend = blend.reshape(PAIRS, 2, fields, LANES).transpose(0, 2, 1, 3).reshape(PAIRS, fields, 2 * LANES)
    sent = transform(received, rotor_offset, blend, fields)
    modes = lax.all_to_all(sent, "pitch", 0, 0, tiled=True)
    modes = modes.reshape(count, 2, fields, 2, step, cols)
    return close(modes, stator_mid, rotor_mid, rim_weights.reshape(-1))


def solution(mesh):
    block = P(None, None, "span", "pitch")
    in_specs = (block, block, P(), P(), P(), P())
    return jax.shard_map(
        shards, mesh=mesh, in_specs=in_specs, out_specs=(block, block), check_vma=False
    )
```

```python
import functools
import math

import jax
import jax.numpy as jnp
import ml_dtypes
import numpy as np
from jax import lax
from jax.experimental import pallas as pl
from jax.experimental.pallas import tpu as pltpu
from jax.sharding import PartitionSpec as P

NP = 2048
LANES = 128
OUTER = NP // LANES
PAIRS = OUTER // 2
UNITS = 12

time_step = 0.5
damping = 1.0 / 32.0
VMEM_LIMIT = 56 * 1024 * 1024


def mode_tables():
    inner = np.arange(LANES)
    out = np.zeros((PAIRS, 2 * LANES, 2 * LANES))

    def angles(outer):
        return 2.0 * math.pi * (np.outer(inner, outer + OUTER * inner) % NP) / NP

    for m in range(PAIRS):
        first, second = (0, PAIRS) if m == 0 else (m, OUTER - m)
        a, b = angles(first), angles(second)
        if m == 0:
            out[m, :LANES, :LANES] = np.cos(a) + np.sin(a)
            out[m, LANES:, LANES:] = np.cos(b) + np.sin(b)
        else:
            out[m, :LANES, :LANES] = np.cos(a)
            out[m, LANES:, :LANES] = np.sin(a)
            out[m, :LANES, LANES:] = np.sin(b)
            out[m, LANES:, LANES:] = np.cos(b)
    high = out.astype(ml_dtypes.bfloat16)
    low = (out - high.astype(np.float64)).astype(ml_dtypes.bfloat16)
    return high, low


def outer_order():
    order = [(0, PAIRS)] + [(m, OUTER - m) for m in range(1, PAIRS)]
    return np.array(order)


def fast_hartley(parts):
    count = len(parts)
    if count == 1:
        return parts
    half = count // 2
    even = fast_hartley(parts[0::2])
    odd = fast_hartley(parts[1::2])
    turned = []
    for k in range(half):
        if k == 0:
            turned.append(odd[0])
        elif 4 * k == count:
            turned.append(odd[half - k])
        else:
            angle = 2.0 * math.pi * k / count
            turned.append(odd[k] * math.cos(angle) + odd[half - k] * math.sin(angle))
    return [even[k] + turned[k] for k in range(half)] + [even[k] - turned[k] for k in range(half)]


def split_dot(x, high, low, dims):
    x_high = x.astype(jnp.bfloat16)
    x_low = (x - x_high.astype(jnp.float32)).astype(jnp.bfloat16)
    dot = functools.partial(
        lax.dot_general, dimension_numbers=(dims, ((), ())), preferred_element_type=jnp.float32
    )
    return dot(x_high, high) + (dot(x_low, high) + dot(x_high, low))


def transform_kernel(fields, offset_ref, got_ref, blend_ref, high_ref, low_ref, out_ref, turn, work):
    rows, cols = got_ref.shape[2:]
    per = cols // LANES
    offset = offset_ref[0]
    whole, part = offset // LANES, offset % LANES
    chunk = 8 if rows % 8 == 0 else rows
    lane = lax.broadcasted_iota(jnp.int32, (chunk, LANES), 1)
    pairs = outer_order()

    def block(i):
        return i // per, slice((i % per) * LANES, (i % per + 1) * LANES)

    for i in range(OUTER):
        device, lanes = block(i)
        turn[i] = pltpu.roll(got_ref[device, 1, :, lanes], part, 1)
    for at in range(0, rows, chunk):
        span = slice(at, at + chunk)
        parts = []
        for i in range(OUTER):
            device, lanes = block(i)
            now = turn[(i - whole + OUTER) % OUTER, span, :]
            before = turn[(i - whole - 1 + OUTER) % OUTER, span, :]
            parts.append(jnp.where(lane >= part, now, before) - got_ref[device, 0, span, lanes])
        modes = fast_hartley(parts)
        for m in range(PAIRS):
            work[m, span, :LANES] = modes[pairs[m, 0]]
            work[m, span, LANES:] = modes[pairs[m, 1]]
    for m in range(PAIRS):
        got = split_dot(work[m], high_ref[m], low_ref[m], ((1,), (0,)))
        per_field = rows // fields
        got = jnp.concatenate(
            [
                got[f * per_field : (f + 1) * per_field] * blend_ref[m, f : f + 1, :]
                for f in range(fields)
            ],
            axis=0,
        )
        work[m] = split_dot(got, high_ref[m], low_ref[m], ((1,), (1,)))
    back = (LANES - part) % LANES
    for at in range(0, rows, chunk):
        span = slice(at, at + chunk)
        modes = [None] * OUTER
        for m in range(PAIRS):
            modes[pairs[m, 0]] = work[m, span, :LANES]
            modes[pairs[m, 1]] = work[m, span, LANES:]
        parts = fast_hartley(modes)
        for i in range(OUTER):
            device, lanes = block(i)
            out_ref[device, 0, span, lanes] = parts[i]
            turn[i, span, :] = pltpu.roll(parts[i], back, 1)
        for i in range(OUTER):
            device, lanes = block(i)
            now = turn[(i + whole) % OUTER, span, :]
            after = turn[(i + whole + 1) % OUTER, span, :]
            out_ref[device, 1, span, lanes] = jnp.where(lane < LANES - part, now, after)


def transform(received, offset, blend, fields):
    high, low = mode_tables()
    count, _, rows, cols = received.shape
    vmem = pl.BlockSpec(memory_space=pltpu.VMEM)
    return pl.pallas_call(
        functools.partial(transform_kernel, fields),
        out_shape=jax.ShapeDtypeStruct(received.shape, jnp.float32),
        in_specs=[pl.BlockSpec(memory_space=pltpu.SMEM)] + [vmem] * 4,
        out_specs=vmem,
        scratch_shapes=[
            pltpu.VMEM((OUTER, rows, LANES), jnp.float32),
            pltpu.VMEM((PAIRS, rows, 2 * LANES), jnp.float32),
        ],
        compiler_params=pltpu.CompilerParams(vmem_limit_bytes=VMEM_LIMIT),
        cost_estimate=pl.CostEstimate(
            flops=12 * rows * PAIRS * 4 * LANES * LANES, bytes_accessed=5_000_000, transcendentals=0
        ),
        name="modes",
    )(offset, received, blend, jnp.asarray(high), jnp.asarray(low))


def pack_kernel(stator_ref, rotor_ref, low_ref, high_ref, left_ref, right_ref):
    step = pl.program_id(0)
    fields, _, rows, cols = stator_ref.shape
    lane = lax.broadcasted_iota(jnp.int32, (rows, LANES), 1)
    for side, ref in enumerate((stator_ref, rotor_ref)):
        unit = 2 * step + side
        place, first = unit // UNITS, unit % UNITS * (2 * fields)
        left = jnp.zeros((rows, LANES), jnp.float32)
        right = jnp.zeros((rows, LANES), jnp.float32)
        for f in range(fields):
            low_ref[side, 0, f] = ref[f, 0, :2, :]
            high_ref[side, 0, f] = ref[f, 0, rows - 2 :, :]
            here = lane // 2 == f
            a, b = ref[f, 0, :, :LANES], ref[f, 0, :, cols - LANES :]
            left = jnp.where(here, pltpu.roll(a, 2 * f, 1) if f else a, left)
            right = jnp.where(here, pltpu.roll(b, 2 * f + 2, 1), right)
        left = pltpu.roll(left, first, 1)
        right = pltpu.roll(right, first, 1)

        fresh = (lane >= first) & (lane < first + 2 * fields)
        left_ref[place] = jnp.where(fresh, left, left_ref[place])
        right_ref[place] = jnp.where(fresh, right, right_ref[place])


def pack_edges(stator, rotor):
    fields, layers, rows, cols = stator.shape
    blocks = -(-2 * layers // UNITS)
    one = (fields, 1, rows, cols)
    edge = jax.ShapeDtypeStruct((2, layers, fields, 2, cols), jnp.float32)
    side = jax.ShapeDtypeStruct((blocks, rows, LANES), jnp.float32)
    edge_spec = pl.BlockSpec((2, 1, fields, 2, cols), lambda t: (0, t, 0, 0, 0))
    side_spec = pl.BlockSpec((blocks, rows, LANES), lambda t: (0, 0, 0))
    return pl.pallas_call(
        pack_kernel,
        grid=(layers,),
        out_shape=(edge, edge, side, side),
        in_specs=[
            pl.BlockSpec(one, lambda t: (0, t, 0, 0)),
            pl.BlockSpec(one, lambda t: (0, layers - 1 - t, 0, 0)),
        ],
        out_specs=(edge_spec, edge_spec, side_spec, side_spec),
        compiler_params=pltpu.CompilerParams(vmem_limit_bytes=VMEM_LIMIT),
        cost_estimate=pl.CostEstimate(
            flops=0, bytes_accessed=2 * 4 * stator.size, transcendentals=0
        ),
        name="edges",
    )(stator, rotor)


def difference_tables(rows, cols):
    scale = time_step * damping
    slope = {1: 1.0, -1: -1.0}
    smooth = {0: -6.0 * scale, 1: 4.0 * scale, -1: 4.0 * scale, 2: -scale, -2: -scale}

    def banded(extent, halo_places, halo_width):
        whole = np.zeros((2, extent, extent))
        halo = np.zeros((2, extent, halo_width))
        for which, taps in enumerate((slope, smooth)):
            for i in range(extent):
                for shift, value in taps.items():
                    j = i + shift
                    if 0 <= j < extent:
                        whole[which, i, j] += value
                    else:
                        halo[which, i, halo_places[j if j < 0 else j - extent]] += value
        return whole.reshape(2 * extent, extent), halo.reshape(2 * extent, halo_width)

    main, rim = banded(rows, {-2: 0, -1: 1, 0: 2, 1: 3}, 8)
    along_rows = np.concatenate([main, main, rim, rim], axis=1)
    main, rim = banded(cols, {0: 0, 1: 1, -2: LANES - 2, -1: LANES - 1}, LANES)
    along_cols = np.concatenate([main, main, rim, rim], axis=1).T
    return along_rows.astype(ml_dtypes.bfloat16), along_cols.astype(ml_dtypes.bfloat16)


def halves(x):
    high = x.astype(jnp.bfloat16)
    return high, (x - high.astype(jnp.float32)).astype(jnp.bfloat16)


def stencil_kernel(
    side, layers, jac_ref, mix_ref, source, low_ref, high_ref, left_ref, right_ref, rows_ref, cols_ref,
    out, state, radial, pitch, parts, sems,
):
    t = pl.program_id(0)
    fields, _, rows, cols = out.shape
    chunk = 16

    def load(layer):
        taken = layer if side == 0 else layers - 1 - layer
        return pltpu.make_async_copy(source.at[:, taken], state.at[:, layer + 2], sems.at[layer])

    @pl.when(t == 0)
    def _():
        for layer in range(layers):
            load(layer).start()
        state[:, 0:2] = jnp.zeros((fields, 2, rows, cols), jnp.float32)
        for layer in range(2):
            load(layer).wait()

    @pl.when(t + 2 < layers)
    def _():
        load(t + 2).wait()

    @pl.when(t == layers - 2)
    def _():
        for ghost in range(2):
            for at in range(0, rows, chunk):
                span = slice(at, at + chunk)
                planes = [state[g, layers + 1 - ghost, span, :] for g in range(fields)]
                for f in range(fields):
                    total = mix_ref[f * fields] * planes[0]
                    for g in range(1, fields):
                        total = total + mix_ref[f * fields + g] * planes[g]
                    state[f, layers + 2 + ghost, span, :] = total

    here = t + 2
    unit = 2 * t + side
    place, first = unit // UNITS, unit % UNITS * (2 * fields)
    turn = (LANES - first) % LANES
    lane = lax.broadcasted_iota(jnp.int32, (rows, LANES), 1)
    from_left = pltpu.roll(left_ref[place], turn, 1)
    from_right = pltpu.roll(right_ref[place], turn, 1)
    for f in range(fields):
        shift = (LANES - 2 * f) % LANES
        rim = jnp.where(lane < 2, pltpu.roll(from_right, shift, 1) if shift else from_right, 0.0)
        rim = jnp.where(lane < LANES - 2, rim, pltpu.roll(from_left, LANES - 2 * f - 2, 1))
        span = slice(f * rows, (f + 1) * rows)
        x_high, x_low = halves(state[f, here])
        rim_high, rim_low = halves(rim)
        parts[span, :cols] = x_high
        parts[span, cols : 2 * cols] = x_low
        parts[span, 2 * cols : 2 * cols + LANES] = rim_high
        parts[span, 2 * cols + LANES :] = rim_low
        halo = jnp.concatenate(
            [low_ref[0, 0, f], high_ref[0, 0, f], jnp.zeros((4, cols), jnp.float32)], axis=0
        )
        halo_high = halo.astype(jnp.bfloat16).astype(jnp.float32)
        halo = jnp.concatenate([halo_high, halo - halo_high], axis=0).astype(jnp.bfloat16)
        radial[f] = jnp.dot(
            rows_ref[...],
            jnp.concatenate([x_high, x_low, halo], axis=0),
            preferred_element_type=jnp.float32,
        )
    pitch[...] = jnp.dot(parts[...], cols_ref[...], preferred_element_type=jnp.float32)

    scale = time_step * damping
    for at in range(0, rows, chunk):
        span = slice(at, at + chunk)
        totals = []
        for f in range(fields):
            near = state[f, here + 1, span, :] + state[f, here - 1, span, :]
            far = state[f, here + 2, span, :] + state[f, here - 2, span, :]
            totals.append(
                (state[f, here, span, :] * (1.0 - 6.0 * scale) + (near * 4.0 - far) * scale)
                + (radial[f, rows + at : rows + at + chunk, :] + pitch[f * rows + at : f * rows + at + chunk, cols:])
            )
        for g in range(fields):
            slopes = (
                state[g, here + 1, span, :] - state[g, here - 1, span, :],
                radial[g, span, :],
                pitch[g * rows + at : g * rows + at + chunk, :cols],
            )
            for d in range(3):
                for f in range(fields):
                    totals[f] = totals[f] + jac_ref[(d * fields + f) * fields + g] * slopes[d]
        for f in range(fields):
            out[f, 0, span, :] = totals[f]


def stencil(side, state, low, high, left, right, weights, mix):
    fields, layers, rows, cols = state.shape
    along_rows, along_cols = difference_tables(rows, cols)
    smem = pl.BlockSpec(memory_space=pltpu.SMEM)
    vmem = pl.BlockSpec(memory_space=pltpu.VMEM)
    edge_spec = pl.BlockSpec((1, 1, fields, 2, cols), lambda t: (side, t, 0, 0, 0))
    side_spec = pl.BlockSpec(left.shape, lambda t: (0, 0, 0))
    return pl.pallas_call(
        functools.partial(stencil_kernel, side, layers),
        grid=(layers,),
        out_shape=jax.ShapeDtypeStruct(state.shape, jnp.float32),
        in_specs=[smem, smem, pl.BlockSpec(memory_space=pl.ANY), edge_spec, edge_spec, side_spec, side_spec, vmem, vmem],
        out_specs=pl.BlockSpec(
            (fields, 1, rows, cols), lambda t: (0, t if side == 0 else layers - 1 - t, 0, 0)
        ),
        scratch_shapes=[
            pltpu.VMEM((fields, layers + 4, rows, cols), jnp.float32),
            pltpu.VMEM((fields, 2 * rows, cols), jnp.float32),
            pltpu.VMEM((fields * rows, 2 * cols), jnp.float32),
            pltpu.VMEM((fields * rows, 2 * cols + 2 * LANES), jnp.bfloat16),
            pltpu.SemaphoreType.DMA((layers,)),
        ],
        compiler_params=pltpu.CompilerParams(vmem_limit_bytes=VMEM_LIMIT),
        cost_estimate=pl.CostEstimate(
            flops=60 * state.size, bytes_accessed=16 * state.size, transcendentals=0
        ),
        name=("stator_stencil", "rotor_stencil")[side],
    )(weights, mix, state, low, high, left, right, jnp.asarray(along_rows), jnp.asarray(along_cols))


def close_kernel(weight_ref, modes_ref, stator_ref, rotor_ref, stator_out, rotor_out):
    fields, _, rows, cols = stator_ref.shape
    count = modes_ref.shape[0]
    step = modes_ref.shape[4]
    for side, (ref, out) in enumerate(((stator_ref, stator_out), (rotor_ref, rotor_out))):
        near, far = (1, 0) if side == 0 else (0, 1)
        for q in range(count):
            span = slice(q * step, (q + 1) * step)
            first = [modes_ref[q, side, g, 0] for g in range(fields)]
            second = [modes_ref[q, side, g, 1] for g in range(fields)]
            for f in range(fields):
                rim, inner = ref[f, near, span, :], ref[f, far, span, :]
                for g in range(fields):
                    at = (side * 2 * fields + f) * fields + g
                    weight_near = weight_ref[at]
                    weight_far = weight_ref[at + fields * fields]
                    rim = rim + (weight_near * first[g] + weight_far * second[g])
                    inner = inner + weight_far * first[g]
                out[f, near, span, :] = rim
                out[f, far, span, :] = inner


def close(modes, stator, rotor, weights):
    fields, layers, rows, cols = stator.shape
    count, _, _, _, step, _ = modes.shape
    group = max(1, count // 4)
    block = (fields, 2, rows // count * group, cols)
    specs = (
        pl.BlockSpec(block, lambda q: (0, layers // 2 - 1, q, 0)),
        pl.BlockSpec(block, lambda q: (0, 0, q, 0)),
    )
    shape = jax.ShapeDtypeStruct(stator.shape, jnp.float32)
    return pl.pallas_call(
        close_kernel,
        grid=(count // group,),
        out_shape=(shape, shape),
        in_specs=[
            pl.BlockSpec(memory_space=pltpu.SMEM),
            pl.BlockSpec((group,) + modes.shape[1:], lambda q: (q, 0, 0, 0, 0, 0)),
            *specs,
        ],
        out_specs=specs,
        input_output_aliases={2: 0, 3: 1},
        compiler_params=pltpu.CompilerParams(vmem_limit_bytes=VMEM_LIMIT),
        cost_estimate=pl.CostEstimate(
            flops=30 * modes.size, bytes_accessed=12 * modes.size, transcendentals=0
        ),
        name="interface",
    )(weights, modes, stator, rotor)


def exact_dot(a, b):
    return jnp.matmul(a, b, precision=lax.Precision.HIGHEST)


def shards(stator, rotor, jacobians, field_mix, mode_blend, rotor_offset):
    fields, layers, rows, cols = stator.shape
    count = lax.axis_size("pitch")
    spans = lax.axis_size("span")
    step = rows // count

    def by_owner(planes):
        return jnp.moveaxis(planes.reshape(fields, 2, count, step, cols), 2, 0)

    planes = jnp.stack([by_owner(stator[:, layers - 2 :][:, ::-1]), by_owner(rotor[:, :2])], axis=1)
    planes = planes.reshape(count, 2, fields * 2 * step, cols)
    received = lax.all_to_all(planes, "pitch", 0, 0, tiled=True)

    low, high, left, right = pack_edges(stator, rotor)
    ring = [(i, (i + 1) % count) for i in range(count)]
    line = [(i, i + 1) for i in range(spans - 1)]
    from_left = lax.ppermute(right, "pitch", ring)
    from_right = lax.ppermute(left, "pitch", [(b, a) for a, b in ring])
    from_below = lax.ppermute(high, "span", line)
    from_above = lax.ppermute(low, "span", [(b, a) for a, b in line])

    mirrored = jacobians * jnp.array([-1.0, 1.0, 1.0], jnp.float32)[:, None, None]
    courses = jnp.stack([jacobians, mirrored])
    weights = (-0.5 * time_step) * courses
    mixed = exact_dot(courses[:, 0], field_mix)
    far = (-time_step * damping) * field_mix
    near = (-0.5 * time_step) * mixed + (4.0 * time_step * damping) * field_mix
    signs = jnp.array([1.0, -1.0], jnp.float32)[:, None, None]
    rim_weights = jnp.stack([signs * near, signs * far], axis=1)

    edges = (from_below, from_above, from_left, from_right)
    mix = field_mix.reshape(-1)
    stator_mid = stencil(0, stator, *edges, weights[0].reshape(-1), mix)
    received, stator_mid = lax.optimization_barrier((received, stator_mid))

    blend = mode_blend.reshape(fields, LANES, OUTER) * (1.0 / NP)
    blend = jnp.moveaxis(blend, 2, 0)[outer_order().reshape(-1)]
    blend = blend.reshape(PAIRS, 2, fields, LANES).transpose(0, 2, 1, 3).reshape(PAIRS, fields, 2 * LANES)
    sent = transform(received, rotor_offset, blend, fields)
    modes = lax.all_to_all(sent, "pitch", 0, 0, tiled=True)
    modes = modes.reshape(count, 2, fields, 2, step, cols)
    rotor_mid = stencil(1, rotor, *edges, weights[1].reshape(-1), mix)
    return close(modes, stator_mid, rotor_mid, rim_weights.reshape(-1))


def solution(mesh):
    block = P(None, None, "span", "pitch")
    in_specs = (block, block, P(), P(), P(), P())
    return jax.shard_map(
        shards, mesh=mesh, in_specs=in_specs, out_specs=(block, block), check_vma=False
    )
```

```python
import functools
import math

import jax
import jax.numpy as jnp
import ml_dtypes
import numpy as np
from jax import lax
from jax.experimental import pallas as pl
from jax.experimental.pallas import tpu as pltpu
from jax.sharding import PartitionSpec as P

NP = 2048
LANES = 128
OUTER = NP // LANES
PAIRS = OUTER // 2
UNITS = 12

time_step = 0.5
damping = 1.0 / 32.0
WIDE = 56 * 1024 * 1024
NARROW = 16 * 1024 * 1024


def mode_tables():
    inner = np.arange(LANES)
    out = np.zeros((PAIRS, 2 * LANES, 2 * LANES))

    def angles(outer):
        return 2.0 * math.pi * (np.outer(inner, outer + OUTER * inner) % NP) / NP

    for m in range(PAIRS):
        first, second = (0, PAIRS) if m == 0 else (m, OUTER - m)
        a, b = angles(first), angles(second)
        if m == 0:
            out[m, :LANES, :LANES] = np.cos(a) + np.sin(a)
            out[m, LANES:, LANES:] = np.cos(b) + np.sin(b)
        else:
            out[m, :LANES, :LANES] = np.cos(a)
            out[m, LANES:, :LANES] = np.sin(a)
            out[m, :LANES, LANES:] = np.sin(b)
            out[m, LANES:, LANES:] = np.cos(b)
    high = out.astype(ml_dtypes.bfloat16)
    low = (out - high.astype(np.float64)).astype(ml_dtypes.bfloat16)
    return high, low


def outer_order():
    order = [(0, PAIRS)] + [(m, OUTER - m) for m in range(1, PAIRS)]
    return np.array(order)


def fast_hartley(parts):
    count = len(parts)
    if count == 1:
        return parts
    half = count // 2
    even = fast_hartley(parts[0::2])
    odd = fast_hartley(parts[1::2])
    turned = []
    for k in range(half):
        if k == 0:
            turned.append(odd[0])
        elif 4 * k == count:
            turned.append(odd[half - k])
        else:
            angle = 2.0 * math.pi * k / count
            turned.append(odd[k] * math.cos(angle) + odd[half - k] * math.sin(angle))
    return [even[k] + turned[k] for k in range(half)] + [even[k] - turned[k] for k in range(half)]


def split_dot(x, high, low, dims):
    x_high = x.astype(jnp.bfloat16)
    x_low = (x - x_high.astype(jnp.float32)).astype(jnp.bfloat16)
    dot = functools.partial(
        lax.dot_general, dimension_numbers=(dims, ((), ())), preferred_element_type=jnp.float32
    )
    return dot(x_high, high) + (dot(x_low, high) + dot(x_high, low))


def transform_kernel(fields, offset_ref, got_ref, blend_ref, high_ref, low_ref, out_ref, turn, work):
    rows, cols = got_ref.shape[2:]
    per = cols // LANES
    offset = offset_ref[0]
    whole, part = offset // LANES, offset % LANES
    chunk = 8 if rows % 8 == 0 else rows
    lane = lax.broadcasted_iota(jnp.int32, (chunk, LANES), 1)
    pairs = outer_order()

    def block(i):
        return i // per, slice((i % per) * LANES, (i % per + 1) * LANES)

    for i in range(OUTER):
        device, lanes = block(i)
        turn[i] = pltpu.roll(got_ref[device, 1, :, lanes], part, 1)
    for at in range(0, rows, chunk):
        span = slice(at, at + chunk)
        parts = []
        for i in range(OUTER):
            device, lanes = block(i)
            now = turn[(i - whole + OUTER) % OUTER, span, :]
            before = turn[(i - whole - 1 + OUTER) % OUTER, span, :]
            parts.append(jnp.where(lane >= part, now, before) - got_ref[device, 0, span, lanes])
        modes = fast_hartley(parts)
        for m in range(PAIRS):
            work[m, span, :LANES] = modes[pairs[m, 0]]
            work[m, span, LANES:] = modes[pairs[m, 1]]
    for m in range(PAIRS):
        got = split_dot(work[m], high_ref[m], low_ref[m], ((1,), (0,)))
        per_field = rows // fields
        got = jnp.concatenate(
            [
                got[f * per_field : (f + 1) * per_field] * blend_ref[m, f : f + 1, :]
                for f in range(fields)
            ],
            axis=0,
        )
        work[m] = split_dot(got, high_ref[m], low_ref[m], ((1,), (1,)))
    back = (LANES - part) % LANES
    for at in range(0, rows, chunk):
        span = slice(at, at + chunk)
        modes = [None] * OUTER
        for m in range(PAIRS):
            modes[pairs[m, 0]] = work[m, span, :LANES]
            modes[pairs[m, 1]] = work[m, span, LANES:]
        parts = fast_hartley(modes)
        for i in range(OUTER):
            device, lanes = block(i)
            out_ref[device, 0, span, lanes] = parts[i]
            turn[i, span, :] = pltpu.roll(parts[i], back, 1)
        for i in range(OUTER):
            device, lanes = block(i)
            now = turn[(i + whole) % OUTER, span, :]
            after = turn[(i + whole + 1) % OUTER, span, :]
            out_ref[device, 1, span, lanes] = jnp.where(lane < LANES - part, now, after)


def transform(received, offset, blend, fields):
    high, low = mode_tables()
    count, _, rows, cols = received.shape
    vmem = pl.BlockSpec(memory_space=pltpu.VMEM)
    return pl.pallas_call(
        functools.partial(transform_kernel, fields),
        out_shape=jax.ShapeDtypeStruct(received.shape, jnp.float32),
        in_specs=[pl.BlockSpec(memory_space=pltpu.SMEM)] + [vmem] * 4,
        out_specs=vmem,
        scratch_shapes=[
            pltpu.VMEM((OUTER, rows, LANES), jnp.float32),
            pltpu.VMEM((PAIRS, rows, 2 * LANES), jnp.float32),
        ],
        compiler_params=pltpu.CompilerParams(vmem_limit_bytes=NARROW),
        cost_estimate=pl.CostEstimate(
            flops=12 * rows * PAIRS * 4 * LANES * LANES, bytes_accessed=5_000_000, transcendentals=0
        ),
        name="modes",
    )(offset, received, blend, jnp.asarray(high), jnp.asarray(low))


def planes_kernel(stator, rotor, out, sems):
    count, _, _, _, step, _ = out.shape
    layers = stator.shape[1]
    copies = []
    for q in range(count):
        span = pl.ds(q * step, step)
        for ghost in range(2):
            copies.append((stator.at[:, layers - 1 - ghost, span], out.at[q, 0, :, ghost]))
            copies.append((rotor.at[:, ghost, span], out.at[q, 1, :, ghost]))
    copies = [pltpu.make_async_copy(a, b, sems.at[i]) for i, (a, b) in enumerate(copies)]
    for copy in copies:
        copy.start()
    for copy in copies:
        copy.wait()


def interface_planes(stator, rotor, count):
    fields, layers, rows, cols = stator.shape
    step = rows // count
    if step % 8:

        def by_owner(planes):
            return jnp.moveaxis(planes.reshape(fields, 2, count, step, cols), 2, 0)

        return jnp.stack([by_owner(stator[:, layers - 2 :][:, ::-1]), by_owner(rotor[:, :2])], axis=1)
    hbm = pl.BlockSpec(memory_space=pl.ANY)
    return pl.pallas_call(
        planes_kernel,
        out_shape=jax.ShapeDtypeStruct((count, 2, fields, 2, step, cols), jnp.float32),
        in_specs=[hbm, hbm],
        out_specs=hbm,
        scratch_shapes=[pltpu.SemaphoreType.DMA((4 * count,))],
        compiler_params=pltpu.CompilerParams(vmem_limit_bytes=WIDE),
        name="planes",
    )(stator, rotor)


def pack_kernel(stator_ref, rotor_ref, low_ref, high_ref, left_ref, right_ref):
    step = pl.program_id(0)
    fields, _, rows, cols = stator_ref.shape
    lane = lax.broadcasted_iota(jnp.int32, (rows, LANES), 1)
    for side, ref in enumerate((stator_ref, rotor_ref)):
        unit = 2 * step + side
        place, first = unit // UNITS, unit % UNITS * (2 * fields)
        left = jnp.zeros((rows, LANES), jnp.float32)
        right = jnp.zeros((rows, LANES), jnp.float32)
        for f in range(fields):
            low_ref[side, 0, f] = ref[f, 0, :2, :]
            high_ref[side, 0, f] = ref[f, 0, rows - 2 :, :]
            here = lane // 2 == f
            a, b = ref[f, 0, :, :LANES], ref[f, 0, :, cols - LANES :]
            left = jnp.where(here, pltpu.roll(a, 2 * f, 1) if f else a, left)
            right = jnp.where(here, pltpu.roll(b, 2 * f + 2, 1), right)
        left = pltpu.roll(left, first, 1)
        right = pltpu.roll(right, first, 1)

        fresh = (lane >= first) & (lane < first + 2 * fields)
        left_ref[place] = jnp.where(fresh, left, left_ref[place])
        right_ref[place] = jnp.where(fresh, right, right_ref[place])


def pack_edges(stator, rotor):
    fields, layers, rows, cols = stator.shape
    blocks = -(-2 * layers // UNITS)
    one = (fields, 1, rows, cols)
    edge = jax.ShapeDtypeStruct((2, layers, fields, 2, cols), jnp.float32)
    side = jax.ShapeDtypeStruct((blocks, rows, LANES), jnp.float32)
    edge_spec = pl.BlockSpec((2, 1, fields, 2, cols), lambda t: (0, t, 0, 0, 0))
    side_spec = pl.BlockSpec((blocks, rows, LANES), lambda t: (0, 0, 0))
    return pl.pallas_call(
        pack_kernel,
        grid=(layers,),
        out_shape=(edge, edge, side, side),
        in_specs=[
            pl.BlockSpec(one, lambda t: (0, t, 0, 0)),
            pl.BlockSpec(one, lambda t: (0, layers - 1 - t, 0, 0)),
        ],
        out_specs=(edge_spec, edge_spec, side_spec, side_spec),
        compiler_params=pltpu.CompilerParams(vmem_limit_bytes=WIDE),
        cost_estimate=pl.CostEstimate(
            flops=0, bytes_accessed=2 * 4 * stator.size, transcendentals=0
        ),
        name="edges",
    )(stator, rotor)


def difference_tables(rows, cols):
    scale = time_step * damping
    slope = {1: 1.0, -1: -1.0}
    smooth = {0: -6.0 * scale, 1: 4.0 * scale, -1: 4.0 * scale, 2: -scale, -2: -scale}

    def banded(extent, halo_places, halo_width):
        whole = np.zeros((2, extent, extent))
        halo = np.zeros((2, extent, halo_width))
        for which, taps in enumerate((slope, smooth)):
            for i in range(extent):
                for shift, value in taps.items():
                    j = i + shift
                    if 0 <= j < extent:
                        whole[which, i, j] += value
                    else:
                        halo[which, i, halo_places[j if j < 0 else j - extent]] += value
        return whole.reshape(2 * extent, extent), halo.reshape(2 * extent, halo_width)

    main, rim = banded(rows, {-2: 0, -1: 1, 0: 2, 1: 3}, 8)
    along_rows = np.concatenate([main, main, rim, rim], axis=1)
    main, rim = banded(cols, {0: 0, 1: 1, -2: LANES - 2, -1: LANES - 1}, LANES)
    along_cols = np.concatenate([main, main, rim, rim], axis=1).T
    return along_rows.astype(ml_dtypes.bfloat16), along_cols.astype(ml_dtypes.bfloat16)


def halves(x):
    high = x.astype(jnp.bfloat16)
    return high, (x - high.astype(jnp.float32)).astype(jnp.bfloat16)


def stencil_kernel(
    side, layers, jac_ref, mix_ref, source, low_ref, high_ref, left_ref, right_ref, rows_ref, cols_ref,
    out, state, radial, pitch, parts, sems,
):
    step = pl.program_id(0)
    fields, _, rows, cols = out.shape
    chunk = 16
    scale = time_step * damping
    lane = lax.broadcasted_iota(jnp.int32, (rows, LANES), 1)

    def load(layer):
        taken = layer if side == 0 else layers - 1 - layer
        return pltpu.make_async_copy(source.at[:, taken], state.at[:, layer + 2], sems.at[layer])

    def products(t, slot):
        unit = 2 * t + side
        place, first = unit // UNITS, unit % UNITS * (2 * fields)
        turn = (LANES - first) % LANES
        from_left = pltpu.roll(left_ref[place], turn, 1)
        from_right = pltpu.roll(right_ref[place], turn, 1)
        for f in range(fields):
            shift = (LANES - 2 * f) % LANES
            rim = jnp.where(lane < 2, pltpu.roll(from_right, shift, 1) if shift else from_right, 0.0)
            rim = jnp.where(lane < LANES - 2, rim, pltpu.roll(from_left, LANES - 2 * f - 2, 1))
            span = slice(f * rows, (f + 1) * rows)
            x_high, x_low = halves(state[f, t + 2])
            rim_high, rim_low = halves(rim)
            parts[span, :cols] = x_high
            parts[span, cols : 2 * cols] = x_low
            parts[span, 2 * cols : 2 * cols + LANES] = rim_high
            parts[span, 2 * cols + LANES :] = rim_low
            halo = jnp.concatenate(
                [low_ref[0, t, f], high_ref[0, t, f], jnp.zeros((4, cols), jnp.float32)], axis=0
            )
            halo_high = halo.astype(jnp.bfloat16).astype(jnp.float32)
            halo = jnp.concatenate([halo_high, halo - halo_high], axis=0).astype(jnp.bfloat16)
            radial[slot, f] = jnp.dot(
                rows_ref[...],
                jnp.concatenate([x_high, x_low, halo], axis=0),
                preferred_element_type=jnp.float32,
            )
        pitch[slot] = jnp.dot(parts[...], cols_ref[...], preferred_element_type=jnp.float32)

    def advance(t, slot):
        here = t + 2
        for at in range(0, rows, chunk):
            span = slice(at, at + chunk)
            totals = []
            for f in range(fields):
                near = state[f, here + 1, span, :] + state[f, here - 1, span, :]
                far = state[f, here + 2, span, :] + state[f, here - 2, span, :]
                totals.append(
                    (state[f, here, span, :] * (1.0 - 6.0 * scale) + (near * 4.0 - far) * scale)
                    + (
                        radial[slot, f, rows + at : rows + at + chunk, :]
                        + pitch[slot, f * rows + at : f * rows + at + chunk, cols:]
                    )
                )
            for g in range(fields):
                slopes = (
                    state[g, here + 1, span, :] - state[g, here - 1, span, :],
                    radial[slot, g, span, :],
                    pitch[slot, g * rows + at : g * rows + at + chunk, :cols],
                )
                for d in range(3):
                    for f in range(fields):
                        totals[f] = totals[f] + jac_ref[(d * fields + f) * fields + g] * slopes[d]
            for f in range(fields):
                out[f, slot if side == 0 else 1 - slot, span, :] = totals[f]

    @pl.when(step == 0)
    def _():
        for layer in range(layers):
            load(layer).start()
        state[:, 0:2] = jnp.zeros((fields, 2, rows, cols), jnp.float32)
        load(0).wait()
        load(1).wait()
        products(0, 0)

    @pl.when(2 * step + 2 < layers)
    def _():
        load(2 * step + 2).wait()
        load(2 * step + 3).wait()

    @pl.when(2 * step == layers - 2)
    def _():
        for ghost in range(2):
            for at in range(0, rows, chunk):
                span = slice(at, at + chunk)
                planes = [state[g, layers + 1 - ghost, span, :] for g in range(fields)]
                for f in range(fields):
                    total = mix_ref[f * fields] * planes[0]
                    for g in range(1, fields):
                        total = total + mix_ref[f * fields + g] * planes[g]
                    state[f, layers + 2 + ghost, span, :] = total

    products(2 * step + 1, 1)
    advance(2 * step, 0)
    products(jnp.minimum(2 * step + 2, layers - 1), 0)
    advance(2 * step + 1, 1)


def stencil(side, state, low, high, left, right, weights, mix):
    fields, layers, rows, cols = state.shape
    along_rows, along_cols = difference_tables(rows, cols)
    smem = pl.BlockSpec(memory_space=pltpu.SMEM)
    vmem = pl.BlockSpec(memory_space=pltpu.VMEM)
    edge_spec = pl.BlockSpec((1, layers, fields, 2, cols), lambda t: (side, 0, 0, 0, 0))
    side_spec = pl.BlockSpec(left.shape, lambda t: (0, 0, 0))
    steps = layers // 2
    return pl.pallas_call(
        functools.partial(stencil_kernel, side, layers),
        grid=(steps,),
        out_shape=jax.ShapeDtypeStruct(state.shape, jnp.float32),
        in_specs=[smem, smem, pl.BlockSpec(memory_space=pl.ANY), edge_spec, edge_spec, side_spec, side_spec, vmem, vmem],
        out_specs=pl.BlockSpec(
            (fields, 2, rows, cols), lambda t: (0, t if side == 0 else steps - 1 - t, 0, 0)
        ),
        scratch_shapes=[
            pltpu.VMEM((fields, layers + 4, rows, cols), jnp.float32),
            pltpu.VMEM((2, fields, 2 * rows, cols), jnp.float32),
            pltpu.VMEM((2, fields * rows, 2 * cols), jnp.float32),
            pltpu.VMEM((fields * rows, 2 * cols + 2 * LANES), jnp.bfloat16),
            pltpu.SemaphoreType.DMA((layers,)),
        ],
        compiler_params=pltpu.CompilerParams(vmem_limit_bytes=WIDE),
        cost_estimate=pl.CostEstimate(
            flops=60 * state.size, bytes_accessed=16 * state.size, transcendentals=0
        ),
        name=("stator_stencil", "rotor_stencil")[side],
    )(weights, mix, state, low, high, left, right, jnp.asarray(along_rows), jnp.asarray(along_cols))


def close_kernel(weight_ref, modes_ref, stator_ref, rotor_ref, stator_out, rotor_out):
    fields, _, rows, cols = stator_ref.shape
    count = modes_ref.shape[0]
    step = modes_ref.shape[4]
    for side, (ref, out) in enumerate(((stator_ref, stator_out), (rotor_ref, rotor_out))):
        near, far = (1, 0) if side == 0 else (0, 1)
        for q in range(count):
            span = slice(q * step, (q + 1) * step)
            first = [modes_ref[q, side, g, 0] for g in range(fields)]
            second = [modes_ref[q, side, g, 1] for g in range(fields)]
            for f in range(fields):
                rim, inner = ref[f, near, span, :], ref[f, far, span, :]
                for g in range(fields):
                    at = (side * 2 * fields + f) * fields + g
                    weight_near = weight_ref[at]
                    weight_far = weight_ref[at + fields * fields]
                    rim = rim + (weight_near * first[g] + weight_far * second[g])
                    inner = inner + weight_far * first[g]
                out[f, near, span, :] = rim
                out[f, far, span, :] = inner


def close(modes, stator, rotor, weights):
    fields, layers, rows, cols = stator.shape
    count, _, _, _, step, _ = modes.shape
    group = max(1, count // 4)
    block = (fields, 2, rows // count * group, cols)
    specs = (
        pl.BlockSpec(block, lambda q: (0, layers // 2 - 1, q, 0)),
        pl.BlockSpec(block, lambda q: (0, 0, q, 0)),
    )
    shape = jax.ShapeDtypeStruct(stator.shape, jnp.float32)
    return pl.pallas_call(
        close_kernel,
        grid=(count // group,),
        out_shape=(shape, shape),
        in_specs=[
            pl.BlockSpec(memory_space=pltpu.SMEM),
            pl.BlockSpec((group,) + modes.shape[1:], lambda q: (q, 0, 0, 0, 0, 0)),
            *specs,
        ],
        out_specs=specs,
        input_output_aliases={2: 0, 3: 1},
        compiler_params=pltpu.CompilerParams(vmem_limit_bytes=NARROW),
        cost_estimate=pl.CostEstimate(
            flops=30 * modes.size, bytes_accessed=12 * modes.size, transcendentals=0
        ),
        name="interface",
    )(weights, modes, stator, rotor)


def exact_dot(a, b):
    return jnp.matmul(a, b, precision=lax.Precision.HIGHEST)


def shards(stator, rotor, jacobians, field_mix, mode_blend, rotor_offset):
    fields, layers, rows, cols = stator.shape
    count = lax.axis_size("pitch")
    spans = lax.axis_size("span")
    step = rows // count

    planes = interface_planes(stator, rotor, count).reshape(count, 2, fields * 2 * step, cols)

    planes, *states = lax.optimization_barrier((planes, stator, rotor))
    received = lax.all_to_all(planes, "pitch", 0, 0, tiled=True)
    low, high, left, right = pack_edges(*states)
    ring = [(i, (i + 1) % count) for i in range(count)]
    line = [(i, i + 1) for i in range(spans - 1)]
    from_left = lax.ppermute(right, "pitch", ring)
    from_right = lax.ppermute(left, "pitch", [(b, a) for a, b in ring])
    from_below = lax.ppermute(high, "span", line)
    from_above = lax.ppermute(low, "span", [(b, a) for a, b in line])

    mirrored = jacobians * jnp.array([-1.0, 1.0, 1.0], jnp.float32)[:, None, None]
    courses = jnp.stack([jacobians, mirrored])
    weights = (-0.5 * time_step) * courses
    mixed = exact_dot(courses[:, 0], field_mix)
    far = (-time_step * damping) * field_mix
    near = (-0.5 * time_step) * mixed + (4.0 * time_step * damping) * field_mix
    signs = jnp.array([1.0, -1.0], jnp.float32)[:, None, None]
    rim_weights = jnp.stack([signs * near, signs * far], axis=1)

    edges = (from_below, from_above, from_left, from_right)
    mix = field_mix.reshape(-1)
    blend = mode_blend.reshape(fields, LANES, OUTER) * (1.0 / NP)
    blend = jnp.moveaxis(blend, 2, 0)[outer_order().reshape(-1)]
    blend = blend.reshape(PAIRS, 2, fields, LANES).transpose(0, 2, 1, 3).reshape(PAIRS, fields, 2 * LANES)
    received, edges = lax.optimization_barrier((received, edges))
    sent = transform(received, rotor_offset, blend, fields)
    modes = lax.all_to_all(sent, "pitch", 0, 0, tiled=True)
    modes = modes.reshape(count, 2, fields, 2, step, cols)
    stator_mid = stencil(0, stator, *edges, weights[0].reshape(-1), mix)
    rotor_mid = stencil(1, rotor, *edges, weights[1].reshape(-1), mix)
    return close(modes, stator_mid, rotor_mid, rim_weights.reshape(-1))


def solution(mesh):
    block = P(None, None, "span", "pitch")
    in_specs = (block, block, P(), P(), P(), P())
    return jax.shard_map(
        shards, mesh=mesh, in_specs=in_specs, out_specs=(block, block), check_vma=False
    )
```

```python
import functools
import math

import jax
import jax.numpy as jnp
import ml_dtypes
import numpy as np
from jax import lax
from jax.experimental import pallas as pl
from jax.experimental.pallas import tpu as pltpu
from jax.sharding import PartitionSpec as P

NP = 2048
LANES = 128
OUTER = NP // LANES
PAIRS = OUTER // 2
UNITS = 12

time_step = 0.5
damping = 1.0 / 32.0
WIDE = 56 * 1024 * 1024
NARROW = 16 * 1024 * 1024


def mode_tables():
    inner = np.arange(LANES)
    out = np.zeros((PAIRS, 2 * LANES, 2 * LANES))

    def angles(outer):
        return 2.0 * math.pi * (np.outer(inner, outer + OUTER * inner) % NP) / NP

    for m in range(PAIRS):
        first, second = (0, PAIRS) if m == 0 else (m, OUTER - m)
        a, b = angles(first), angles(second)
        if m == 0:
            out[m, :LANES, :LANES] = np.cos(a) + np.sin(a)
            out[m, LANES:, LANES:] = np.cos(b) + np.sin(b)
        else:
            out[m, :LANES, :LANES] = np.cos(a)
            out[m, LANES:, :LANES] = np.sin(a)
            out[m, :LANES, LANES:] = np.sin(b)
            out[m, LANES:, LANES:] = np.cos(b)
    high = out.astype(ml_dtypes.bfloat16)
    low = (out - high.astype(np.float64)).astype(ml_dtypes.bfloat16)
    return high, low


def outer_order():
    order = [(0, PAIRS)] + [(m, OUTER - m) for m in range(1, PAIRS)]
    return np.array(order)


def fast_hartley(parts):
    count = len(parts)
    if count == 1:
        return parts
    half = count // 2
    even = fast_hartley(parts[0::2])
    odd = fast_hartley(parts[1::2])
    turned = []
    for k in range(half):
        if k == 0:
            turned.append(odd[0])
        elif 4 * k == count:
            turned.append(odd[half - k])
        else:
            angle = 2.0 * math.pi * k / count
            turned.append(odd[k] * math.cos(angle) + odd[half - k] * math.sin(angle))
    return [even[k] + turned[k] for k in range(half)] + [even[k] - turned[k] for k in range(half)]


def split_dot(x, high, low, dims):
    x_high = x.astype(jnp.bfloat16)
    x_low = (x - x_high.astype(jnp.float32)).astype(jnp.bfloat16)
    dot = functools.partial(
        lax.dot_general, dimension_numbers=(dims, ((), ())), preferred_element_type=jnp.float32
    )
    return dot(x_high, high) + (dot(x_low, high) + dot(x_high, low))


def transform_kernel(fields, offset_ref, got_ref, blend_ref, high_ref, low_ref, out_ref, turn, work):
    rows, cols = got_ref.shape[2:]
    per = cols // LANES
    offset = offset_ref[0]
    whole, part = offset // LANES, offset % LANES
    chunk = 8 if rows % 8 == 0 else rows
    lane = lax.broadcasted_iota(jnp.int32, (chunk, LANES), 1)
    pairs = outer_order()

    def block(i):
        return i // per, slice((i % per) * LANES, (i % per + 1) * LANES)

    for i in range(OUTER):
        device, lanes = block(i)
        turn[i] = pltpu.roll(got_ref[device, 1, :, lanes], part, 1)
    for at in range(0, rows, chunk):
        span = slice(at, at + chunk)
        parts = []
        for i in range(OUTER):
            device, lanes = block(i)
            now = turn[(i - whole + OUTER) % OUTER, span, :]
            before = turn[(i - whole - 1 + OUTER) % OUTER, span, :]
            parts.append(jnp.where(lane >= part, now, before) - got_ref[device, 0, span, lanes])
        modes = fast_hartley(parts)
        for m in range(PAIRS):
            work[m, span, :LANES] = modes[pairs[m, 0]]
            work[m, span, LANES:] = modes[pairs[m, 1]]
    for m in range(PAIRS):
        got = split_dot(work[m], high_ref[m], low_ref[m], ((1,), (0,)))
        per_field = rows // fields
        got = jnp.concatenate(
            [
                got[f * per_field : (f + 1) * per_field] * blend_ref[m, f : f + 1, :]
                for f in range(fields)
            ],
            axis=0,
        )
        work[m] = split_dot(got, high_ref[m], low_ref[m], ((1,), (1,)))
    back = (LANES - part) % LANES
    for at in range(0, rows, chunk):
        span = slice(at, at + chunk)
        modes = [None] * OUTER
        for m in range(PAIRS):
            modes[pairs[m, 0]] = work[m, span, :LANES]
            modes[pairs[m, 1]] = work[m, span, LANES:]
        parts = fast_hartley(modes)
        for i in range(OUTER):
            device, lanes = block(i)
            out_ref[device, 0, span, lanes] = parts[i]
            turn[i, span, :] = pltpu.roll(parts[i], back, 1)
        for i in range(OUTER):
            device, lanes = block(i)
            now = turn[(i + whole) % OUTER, span, :]
            after = turn[(i + whole + 1) % OUTER, span, :]
            out_ref[device, 1, span, lanes] = jnp.where(lane < LANES - part, now, after)


def transform(received, offset, blend, fields):
    high, low = mode_tables()
    count, _, rows, cols = received.shape
    vmem = pl.BlockSpec(memory_space=pltpu.VMEM)
    return pl.pallas_call(
        functools.partial(transform_kernel, fields),
        out_shape=jax.ShapeDtypeStruct(received.shape, jnp.float32),
        in_specs=[pl.BlockSpec(memory_space=pltpu.SMEM)] + [vmem] * 4,
        out_specs=vmem,
        scratch_shapes=[
            pltpu.VMEM((OUTER, rows, LANES), jnp.float32),
            pltpu.VMEM((PAIRS, rows, 2 * LANES), jnp.float32),
        ],
        compiler_params=pltpu.CompilerParams(vmem_limit_bytes=NARROW),
        cost_estimate=pl.CostEstimate(
            flops=12 * rows * PAIRS * 4 * LANES * LANES, bytes_accessed=5_000_000, transcendentals=0
        ),
        name="modes",
    )(offset, received, blend, jnp.asarray(high), jnp.asarray(low))


def planes_kernel(stator, rotor, out):
    count, _, _, _, step, _ = out.shape
    for q in range(count):
        span = slice(q * step, (q + 1) * step)
        for ghost in range(2):
            out[q, 0, :, ghost] = stator[:, 1 - ghost, span, :]
            out[q, 1, :, ghost] = rotor[:, ghost, span, :]


def interface_planes(stator, rotor, count):
    fields, layers, rows, cols = stator.shape
    step = rows // count
    group = max(1, count // 2)
    block = (fields, 2, group * step, cols)
    return pl.pallas_call(
        planes_kernel,
        grid=(count // group,),
        out_shape=jax.ShapeDtypeStruct((count, 2, fields, 2, step, cols), jnp.float32),
        in_specs=[
            pl.BlockSpec(block, lambda q: (0, layers // 2 - 1, q, 0)),
            pl.BlockSpec(block, lambda q: (0, 0, q, 0)),
        ],
        out_specs=pl.BlockSpec((group, 2, fields, 2, step, cols), lambda q: (q, 0, 0, 0, 0, 0)),
        compiler_params=pltpu.CompilerParams(vmem_limit_bytes=WIDE),
        name="planes",
    )(stator, rotor)


def pack_kernel(stator_ref, rotor_ref, low_ref, high_ref, left_ref, right_ref):
    fields, layers, rows, cols = stator_ref.shape
    lane = lax.broadcasted_iota(jnp.int32, (rows, LANES), 1)
    for layer in range(layers):
        for side, ref in enumerate((stator_ref, rotor_ref)):
            taken = layer if side == 0 else layers - 1 - layer
            unit = 2 * (pl.program_id(0) * layers + layer) + side
            place, first = unit // UNITS, unit % UNITS * (2 * fields)
            left = jnp.zeros((rows, LANES), jnp.float32)
            right = jnp.zeros((rows, LANES), jnp.float32)
            for f in range(fields):
                low_ref[side, layer, f] = ref[f, taken, :2, :]
                high_ref[side, layer, f] = ref[f, taken, rows - 2 :, :]
                ends = jnp.where(
                    lane < LANES // 2, ref[f, taken, :, :LANES], ref[f, taken, :, cols - LANES :]
                )
                ends = pltpu.roll(ends, 2 * f, 1) if f else ends
                left = jnp.where(lane // 2 == f, ends, left)
                right = jnp.where(lane // 2 == (f - 1) % (LANES // 2), ends, right)
            fresh = (lane >= first) & (lane < first + 2 * fields)
            left_ref[place] = jnp.where(fresh, pltpu.roll(left, first, 1), left_ref[place])
            after = jnp.where(lane < LANES - 2, lane + 2, lane + 2 - LANES)
            fresh = (after >= first) & (after < first + 2 * fields)
            right_ref[place] = jnp.where(fresh, pltpu.roll(right, first, 1), right_ref[place])


def pack_edges(stator, rotor):
    fields, layers, rows, cols = stator.shape
    blocks = -(-2 * layers // UNITS)
    each = max(n for n in (4, 2, 1) if layers % n == 0)
    steps = layers // each
    block = (fields, each, rows, cols)
    edge = jax.ShapeDtypeStruct((2, layers, fields, 2, cols), jnp.float32)
    side = jax.ShapeDtypeStruct((blocks, rows, LANES), jnp.float32)
    edge_spec = pl.BlockSpec((2, each, fields, 2, cols), lambda t: (0, t, 0, 0, 0))
    side_spec = pl.BlockSpec((blocks, rows, LANES), lambda t: (0, 0, 0))
    return pl.pallas_call(
        pack_kernel,
        grid=(steps,),
        out_shape=(edge, edge, side, side),
        in_specs=[
            pl.BlockSpec(block, lambda t: (0, t, 0, 0)),
            pl.BlockSpec(block, lambda t: (0, steps - 1 - t, 0, 0)),
        ],
        out_specs=(edge_spec, edge_spec, side_spec, side_spec),
        compiler_params=pltpu.CompilerParams(vmem_limit_bytes=WIDE),
        cost_estimate=pl.CostEstimate(
            flops=0, bytes_accessed=2 * 4 * stator.size, transcendentals=0
        ),
        name="edges",
    )(stator, rotor)


def difference_tables(rows, cols):
    scale = time_step * damping
    slope = {1: -0.5 * time_step, -1: 0.5 * time_step}
    smooth = {0: -6.0 * scale, 1: 4.0 * scale, -1: 4.0 * scale, 2: -scale, -2: -scale}

    def banded(extent, halo_places, halo_width):
        whole = np.zeros((2, extent, extent))
        halo = np.zeros((2, extent, halo_width))
        for which, taps in enumerate((slope, smooth)):
            for i in range(extent):
                for shift, value in taps.items():
                    j = i + shift
                    if 0 <= j < extent:
                        whole[which, i, j] += value
                    else:
                        halo[which, i, halo_places[j if j < 0 else j - extent]] += value
        return whole.reshape(2 * extent, extent), halo.reshape(2 * extent, halo_width)

    main, rim = banded(rows, {-2: 0, -1: 1, 0: 2, 1: 3}, 8)
    along_rows = np.concatenate([main, main, rim, rim], axis=1)
    main, rim = banded(cols, {0: 0, 1: 1, -2: LANES - 2, -1: LANES - 1}, LANES)
    along_cols = np.concatenate([main, main, rim, rim], axis=1).T
    return along_rows.astype(ml_dtypes.bfloat16), along_cols.astype(ml_dtypes.bfloat16)


def halves(x):
    high = x.astype(jnp.bfloat16)
    return high, (x - high.astype(jnp.float32)).astype(jnp.bfloat16)


def stencil_kernel(
    side, layers, jac_ref, mix_ref, source, low_ref, high_ref, left_ref, right_ref, rows_ref, cols_ref,
    out, state, radial, pitch, parts, sems,
):
    step = pl.program_id(0)
    fields, _, rows, cols = out.shape
    chunk = 16
    scale = time_step * damping
    axial = (0.5 if side else -0.5) * time_step
    lane = lax.broadcasted_iota(jnp.int32, (rows, LANES), 1)

    def load(layer):
        taken = layer if side == 0 else layers - 1 - layer
        return pltpu.make_async_copy(source.at[:, taken], state.at[:, layer + 2], sems.at[layer])

    def products(t, slot):
        unit = 2 * t + side
        place, first = unit // UNITS, unit % UNITS * (2 * fields)
        from_left, from_right = left_ref[place], right_ref[place]
        for f in range(fields):
            at = first + 2 * f
            before = jnp.where(lane < LANES - 2, lane + 2, lane + 2 - LANES)
            rim = jnp.where((before >= at) & (before < at + 2), from_left, from_right)
            rim = pltpu.roll(rim, (LANES - at) % LANES, 1)
            rim = jnp.where((lane < 2) | (lane >= LANES - 2), rim, 0.0)
            span = slice(f * rows, (f + 1) * rows)
            x_high, x_low = halves(state[f, t + 2])
            rim_high, rim_low = halves(rim)
            parts[span, :cols] = x_high
            parts[span, cols : 2 * cols] = x_low
            parts[span, 2 * cols : 2 * cols + LANES] = rim_high
            parts[span, 2 * cols + LANES :] = rim_low
            halo = jnp.concatenate(
                [low_ref[0, t, f], high_ref[0, t, f], jnp.zeros((4, cols), jnp.float32)], axis=0
            )
            halo_high = halo.astype(jnp.bfloat16).astype(jnp.float32)
            halo = jnp.concatenate([halo_high, halo - halo_high], axis=0).astype(jnp.bfloat16)
            radial[slot, f] = jnp.dot(
                rows_ref[...],
                jnp.concatenate([x_high, x_low, halo], axis=0),
                preferred_element_type=jnp.float32,
            )
        pitch[slot] = jnp.dot(parts[...], cols_ref[...], preferred_element_type=jnp.float32)

    def advance(t, slot):
        here = t + 2
        for at in range(0, rows, chunk):
            span = slice(at, at + chunk)
            totals = []
            for f in range(fields):
                near = state[f, here + 1, span, :] + state[f, here - 1, span, :]
                far = state[f, here + 2, span, :] + state[f, here - 2, span, :]
                totals.append(
                    (state[f, here, span, :] * (1.0 - 6.0 * scale) + (near * 4.0 - far) * scale)
                    + (
                        radial[slot, f, rows + at : rows + at + chunk, :]
                        + pitch[slot, f * rows + at : f * rows + at + chunk, cols:]
                    )
                )
            for g in range(fields):
                slopes = (
                    (state[g, here + 1, span, :] - state[g, here - 1, span, :]) * axial,
                    radial[slot, g, span, :],
                    pitch[slot, g * rows + at : g * rows + at + chunk, :cols],
                )
                for d in range(3):
                    for f in range(fields):
                        totals[f] = totals[f] + jac_ref[d, f, g] * slopes[d]
            for f in range(fields):
                out[f, slot if side == 0 else 1 - slot, span, :] = totals[f]

    @pl.when(step == 0)
    def _():
        for layer in range(layers):
            load(layer).start()
        state[:, 0:2] = jnp.zeros((fields, 2, rows, cols), jnp.float32)
        load(0).wait()
        load(1).wait()

    @pl.when(2 * step + 2 < layers)
    def _():
        load(2 * step + 2).wait()
        load(2 * step + 3).wait()

    @pl.when(2 * step == layers - 2)
    def _():
        for ghost in range(2):
            for at in range(0, rows, chunk):
                span = slice(at, at + chunk)
                planes = [state[g, layers + 1 - ghost, span, :] for g in range(fields)]
                for f in range(fields):
                    total = mix_ref[f, 0] * planes[0]
                    for g in range(1, fields):
                        total = total + mix_ref[f, g] * planes[g]
                    state[f, layers + 2 + ghost, span, :] = total

    for slot in range(2):
        products(2 * step + slot, slot)
    for slot in range(2):
        advance(2 * step + slot, slot)


def stencil(side, state, low, high, left, right, weights, mix):
    fields, layers, rows, cols = state.shape
    along_rows, along_cols = difference_tables(rows, cols)
    smem = pl.BlockSpec(memory_space=pltpu.SMEM)
    vmem = pl.BlockSpec(memory_space=pltpu.VMEM)
    edge_spec = pl.BlockSpec((1, layers, fields, 2, cols), lambda t: (side, 0, 0, 0, 0))
    side_spec = pl.BlockSpec(left.shape, lambda t: (0, 0, 0))
    steps = layers // 2
    return pl.pallas_call(
        functools.partial(stencil_kernel, side, layers),
        grid=(steps,),
        out_shape=jax.ShapeDtypeStruct(state.shape, jnp.float32),
        in_specs=[smem, smem, pl.BlockSpec(memory_space=pl.ANY), edge_spec, edge_spec, side_spec, side_spec, vmem, vmem],
        out_specs=pl.BlockSpec(
            (fields, 2, rows, cols), lambda t: (0, t if side == 0 else steps - 1 - t, 0, 0)
        ),
        scratch_shapes=[
            pltpu.VMEM((fields, layers + 4, rows, cols), jnp.float32),
            pltpu.VMEM((2, fields, 2 * rows, cols), jnp.float32),
            pltpu.VMEM((2, fields * rows, 2 * cols), jnp.float32),
            pltpu.VMEM((fields * rows, 2 * cols + 2 * LANES), jnp.bfloat16),
            pltpu.SemaphoreType.DMA((layers,)),
        ],
        compiler_params=pltpu.CompilerParams(vmem_limit_bytes=WIDE),
        cost_estimate=pl.CostEstimate(
            flops=60 * state.size, bytes_accessed=16 * state.size, transcendentals=0
        ),
        name=("stator_stencil", "rotor_stencil")[side],
    )(weights, mix, state, low, high, left, right, jnp.asarray(along_rows), jnp.asarray(along_cols))


def close_kernel(jac_ref, mix_ref, modes_ref, stator_ref, rotor_ref, stator_out, rotor_out):
    fields = stator_ref.shape[0]
    count = modes_ref.shape[0]
    step = modes_ref.shape[4]
    scale = time_step * damping

    def combine(row, sources):
        total = row(0) * sources[0]
        for g in range(1, fields):
            total = total + row(g) * sources[g]
        return total

    for side, (ref, out) in enumerate(((stator_ref, stator_out), (rotor_ref, rotor_out))):
        near, far = (1, 0) if side == 0 else (0, 1)
        sign = -1.0 if side else 1.0
        for q in range(count):
            span = slice(q * step, (q + 1) * step)
            ghosts = []
            for ghost in range(2):
                planes = [modes_ref[q, side, g, ghost] for g in range(fields)]
                ghosts.append([combine(lambda g: mix_ref[f, g], planes) for f in range(fields)])
            first, second = ghosts
            for f in range(fields):
                slope = combine(lambda g: jac_ref[0, f, g], first) * (-0.5 * time_step)
                bend = first[f] * 4.0 - second[f]
                out[f, near, span, :] = ref[f, near, span, :] + (slope + bend * (sign * scale))
                out[f, far, span, :] = ref[f, far, span, :] - first[f] * (sign * scale)


def close(modes, stator, rotor, jacobians, field_mix):
    fields, layers, rows, cols = stator.shape
    count, _, _, _, step, _ = modes.shape
    group = max(1, count // 4)
    block = (fields, 2, rows // count * group, cols)
    specs = (
        pl.BlockSpec(block, lambda q: (0, layers // 2 - 1, q, 0)),
        pl.BlockSpec(block, lambda q: (0, 0, q, 0)),
    )
    shape = jax.ShapeDtypeStruct(stator.shape, jnp.float32)
    return pl.pallas_call(
        close_kernel,
        grid=(count // group,),
        out_shape=(shape, shape),
        in_specs=[
            pl.BlockSpec(memory_space=pltpu.SMEM),
            pl.BlockSpec(memory_space=pltpu.SMEM),
            pl.BlockSpec((group,) + modes.shape[1:], lambda q: (q, 0, 0, 0, 0, 0)),
            *specs,
        ],
        out_specs=specs,
        input_output_aliases={3: 0, 4: 1},
        compiler_params=pltpu.CompilerParams(vmem_limit_bytes=NARROW),
        cost_estimate=pl.CostEstimate(
            flops=30 * modes.size, bytes_accessed=12 * modes.size, transcendentals=0
        ),
        name="interface",
    )(jacobians, field_mix, modes, stator, rotor)


def shards(stator, rotor, jacobians, field_mix, mode_blend, rotor_offset):
    fields, layers, rows, cols = stator.shape
    count = lax.axis_size("pitch")
    spans = lax.axis_size("span")
    step = rows // count

    planes = interface_planes(stator, rotor, count).reshape(count, 2, fields * 2 * step, cols)

    planes, *states = lax.optimization_barrier((planes, stator, rotor))
    received = lax.all_to_all(planes, "pitch", 0, 0, tiled=True)
    low, high, left, right = pack_edges(*states)
    ring = [(i, (i + 1) % count) for i in range(count)]
    line = [(i, i + 1) for i in range(spans - 1)]
    from_left = lax.ppermute(right, "pitch", ring)
    from_right = lax.ppermute(left, "pitch", [(b, a) for a, b in ring])
    from_below = lax.ppermute(high, "span", line)
    from_above = lax.ppermute(low, "span", [(b, a) for a, b in line])

    edges = (from_below, from_above, from_left, from_right)
    blend = mode_blend.reshape(fields, LANES, OUTER) * (1.0 / NP)
    blend = jnp.moveaxis(blend, 2, 0)[outer_order().reshape(-1)]
    blend = blend.reshape(PAIRS, 2, fields, LANES).transpose(0, 2, 1, 3).reshape(PAIRS, fields, 2 * LANES)
    received, edges = lax.optimization_barrier((received, edges))
    sent = transform(received, rotor_offset, blend, fields)
    modes = lax.all_to_all(sent, "pitch", 0, 0, tiled=True)
    modes = modes.reshape(count, 2, fields, 2, step, cols)
    stator_mid = stencil(0, stator, *edges, jacobians, field_mix)
    rotor_mid = stencil(1, rotor, *edges, jacobians, field_mix)
    return close(modes, stator_mid, rotor_mid, jacobians, field_mix)


def solution(mesh):
    block = P(None, None, "span", "pitch")
    in_specs = (block, block, P(), P(), P(), P())
    return jax.shard_map(
        shards, mesh=mesh, in_specs=in_specs, out_specs=(block, block), check_vma=False
    )
```

```python
import functools
import math

import jax
import jax.numpy as jnp
import ml_dtypes
import numpy as np
from jax import lax
from jax.experimental import pallas as pl
from jax.experimental.pallas import tpu as pltpu
from jax.sharding import PartitionSpec as P

NP = 2048
LANES = 128
OUTER = NP // LANES
PAIRS = OUTER // 2
UNITS = 12

time_step = 0.5
damping = 1.0 / 32.0
WIDE = 56 * 1024 * 1024
NARROW = 16 * 1024 * 1024


def mode_tables():
    inner = np.arange(LANES)
    out = np.zeros((PAIRS, 2 * LANES, 2 * LANES))

    def angles(outer):
        return 2.0 * math.pi * (np.outer(inner, outer + OUTER * inner) % NP) / NP

    for m in range(PAIRS):
        first, second = (0, PAIRS) if m == 0 else (m, OUTER - m)
        a, b = angles(first), angles(second)
        if m == 0:
            out[m, :LANES, :LANES] = np.cos(a) + np.sin(a)
            out[m, LANES:, LANES:] = np.cos(b) + np.sin(b)
        else:
            out[m, :LANES, :LANES] = np.cos(a)
            out[m, LANES:, :LANES] = np.sin(a)
            out[m, :LANES, LANES:] = np.sin(b)
            out[m, LANES:, LANES:] = np.cos(b)
    high = out.astype(ml_dtypes.bfloat16)
    low = (out - high.astype(np.float64)).astype(ml_dtypes.bfloat16)
    return high, low


def outer_order():
    order = [(0, PAIRS)] + [(m, OUTER - m) for m in range(1, PAIRS)]
    return np.array(order)


def fast_hartley(parts):
    count = len(parts)
    if count == 1:
        return parts
    half = count // 2
    even = fast_hartley(parts[0::2])
    odd = fast_hartley(parts[1::2])
    turned = []
    for k in range(half):
        if k == 0:
            turned.append(odd[0])
        elif 4 * k == count:
            turned.append(odd[half - k])
        else:
            angle = 2.0 * math.pi * k / count
            turned.append(odd[k] * math.cos(angle) + odd[half - k] * math.sin(angle))
    return [even[k] + turned[k] for k in range(half)] + [even[k] - turned[k] for k in range(half)]


def split_dot(x, high, low, dims):
    x_high = x.astype(jnp.bfloat16)
    x_low = (x - x_high.astype(jnp.float32)).astype(jnp.bfloat16)
    dot = functools.partial(
        lax.dot_general, dimension_numbers=(dims, ((), ())), preferred_element_type=jnp.float32
    )
    return dot(x_high, high) + (dot(x_low, high) + dot(x_high, low))


def transform_kernel(fields, offset_ref, got_ref, blend_ref, high_ref, low_ref, out_ref, turn, work):
    rows, cols = got_ref.shape[2:]
    per = cols // LANES
    offset = offset_ref[0]
    whole, part = offset // LANES, offset % LANES
    chunk = 8 if rows % 8 == 0 else rows
    lane = lax.broadcasted_iota(jnp.int32, (chunk, LANES), 1)
    pairs = outer_order()

    def block(i):
        return i // per, slice((i % per) * LANES, (i % per + 1) * LANES)

    for i in range(OUTER):
        device, lanes = block(i)
        turn[i] = pltpu.roll(got_ref[device, 1, :, lanes], part, 1)
    for at in range(0, rows, chunk):
        span = slice(at, at + chunk)
        parts = []
        for i in range(OUTER):
            device, lanes = block(i)
            now = turn[(i - whole + OUTER) % OUTER, span, :]
            before = turn[(i - whole - 1 + OUTER) % OUTER, span, :]
            parts.append(jnp.where(lane >= part, now, before) - got_ref[device, 0, span, lanes])
        modes = fast_hartley(parts)
        for m in range(PAIRS):
            work[m, span, :LANES] = modes[pairs[m, 0]]
            work[m, span, LANES:] = modes[pairs[m, 1]]
    for m in range(PAIRS):
        got = split_dot(work[m], high_ref[m], low_ref[m], ((1,), (0,)))
        per_field = rows // fields
        got = jnp.concatenate(
            [
                got[f * per_field : (f + 1) * per_field] * blend_ref[m, f : f + 1, :]
                for f in range(fields)
            ],
            axis=0,
        )
        work[m] = split_dot(got, high_ref[m], low_ref[m], ((1,), (1,)))
    back = (LANES - part) % LANES
    for at in range(0, rows, chunk):
        span = slice(at, at + chunk)
        modes = [None] * OUTER
        for m in range(PAIRS):
            modes[pairs[m, 0]] = work[m, span, :LANES]
            modes[pairs[m, 1]] = work[m, span, LANES:]
        parts = fast_hartley(modes)
        for i in range(OUTER):
            device, lanes = block(i)
            out_ref[device, 0, span, lanes] = parts[i]
            turn[i, span, :] = pltpu.roll(parts[i], back, 1)
        for i in range(OUTER):
            device, lanes = block(i)
            now = turn[(i + whole) % OUTER, span, :]
            after = turn[(i + whole + 1) % OUTER, span, :]
            out_ref[device, 1, span, lanes] = jnp.where(lane < LANES - part, now, after)


def transform(received, offset, blend, fields):
    high, low = mode_tables()
    count, _, rows, cols = received.shape
    vmem = pl.BlockSpec(memory_space=pltpu.VMEM)
    return pl.pallas_call(
        functools.partial(transform_kernel, fields),
        out_shape=jax.ShapeDtypeStruct(received.shape, jnp.float32),
        in_specs=[pl.BlockSpec(memory_space=pltpu.SMEM)] + [vmem] * 4,
        out_specs=vmem,
        scratch_shapes=[
            pltpu.VMEM((OUTER, rows, LANES), jnp.float32),
            pltpu.VMEM((PAIRS, rows, 2 * LANES), jnp.float32),
        ],
        compiler_params=pltpu.CompilerParams(vmem_limit_bytes=NARROW),
        cost_estimate=pl.CostEstimate(
            flops=12 * rows * PAIRS * 4 * LANES * LANES, bytes_accessed=5_000_000, transcendentals=0
        ),
        name="modes",
    )(offset, received, blend, jnp.asarray(high), jnp.asarray(low))


def planes_kernel(stator, rotor, out):
    count, _, _, _, step, _ = out.shape
    for q in range(count):
        span = slice(q * step, (q + 1) * step)
        for ghost in range(2):
            out[q, 0, :, ghost] = stator[:, 1 - ghost, span, :]
            out[q, 1, :, ghost] = rotor[:, ghost, span, :]


def interface_planes(stator, rotor, count):
    fields, layers, rows, cols = stator.shape
    step = rows // count
    group = max(1, count // 2)
    block = (fields, 2, group * step, cols)
    return pl.pallas_call(
        planes_kernel,
        grid=(count // group,),
        out_shape=jax.ShapeDtypeStruct((count, 2, fields, 2, step, cols), jnp.float32),
        in_specs=[
            pl.BlockSpec(block, lambda q: (0, layers // 2 - 1, q, 0)),
            pl.BlockSpec(block, lambda q: (0, 0, q, 0)),
        ],
        out_specs=pl.BlockSpec((group, 2, fields, 2, step, cols), lambda q: (q, 0, 0, 0, 0, 0)),
        compiler_params=pltpu.CompilerParams(vmem_limit_bytes=WIDE),
        name="planes",
    )(stator, rotor)


def pack_kernel(stator_ref, rotor_ref, low_ref, high_ref, left_ref, right_ref):
    fields, layers, rows, cols = stator_ref.shape
    lane = lax.broadcasted_iota(jnp.int32, (rows, LANES), 1)
    for layer in range(layers):
        for side, ref in enumerate((stator_ref, rotor_ref)):
            taken = layer if side == 0 else layers - 1 - layer
            unit = 2 * (pl.program_id(0) * layers + layer) + side
            place, first = unit // UNITS, unit % UNITS * (2 * fields)
            left = jnp.zeros((rows, LANES), jnp.float32)
            right = jnp.zeros((rows, LANES), jnp.float32)
            for f in range(fields):
                low_ref[side, layer, f] = ref[f, taken, :2, :]
                high_ref[side, layer, f] = ref[f, taken, rows - 2 :, :]
                ends = jnp.where(
                    lane < LANES // 2, ref[f, taken, :, :LANES], ref[f, taken, :, cols - LANES :]
                )
                ends = pltpu.roll(ends, 2 * f, 1) if f else ends
                left = jnp.where(lane // 2 == f, ends, left)
                right = jnp.where(lane // 2 == (f - 1) % (LANES // 2), ends, right)
            fresh = (lane >= first) & (lane < first + 2 * fields)
            left_ref[place] = jnp.where(fresh, pltpu.roll(left, first, 1), left_ref[place])
            after = jnp.where(lane < LANES - 2, lane + 2, lane + 2 - LANES)
            fresh = (after >= first) & (after < first + 2 * fields)
            right_ref[place] = jnp.where(fresh, pltpu.roll(right, first, 1), right_ref[place])


def pack_edges(stator, rotor):
    fields, layers, rows, cols = stator.shape
    blocks = -(-2 * layers // UNITS)
    each = max(n for n in (4, 2, 1) if layers % n == 0)
    steps = layers // each
    block = (fields, each, rows, cols)
    edge = jax.ShapeDtypeStruct((2, layers, fields, 2, cols), jnp.float32)
    side = jax.ShapeDtypeStruct((blocks, rows, LANES), jnp.float32)
    edge_spec = pl.BlockSpec((2, each, fields, 2, cols), lambda t: (0, t, 0, 0, 0))
    side_spec = pl.BlockSpec((blocks, rows, LANES), lambda t: (0, 0, 0))
    return pl.pallas_call(
        pack_kernel,
        grid=(steps,),
        out_shape=(edge, edge, side, side),
        in_specs=[
            pl.BlockSpec(block, lambda t: (0, t, 0, 0)),
            pl.BlockSpec(block, lambda t: (0, steps - 1 - t, 0, 0)),
        ],
        out_specs=(edge_spec, edge_spec, side_spec, side_spec),
        compiler_params=pltpu.CompilerParams(vmem_limit_bytes=WIDE),
        cost_estimate=pl.CostEstimate(
            flops=0, bytes_accessed=2 * 4 * stator.size, transcendentals=0
        ),
        name="edges",
    )(stator, rotor)


def difference_tables(rows, cols):
    scale = time_step * damping
    slope = {1: -0.5 * time_step, -1: 0.5 * time_step}
    smooth = {0: -6.0 * scale, 1: 4.0 * scale, -1: 4.0 * scale, 2: -scale, -2: -scale}

    def banded(extent, halo_places, halo_width):
        whole = np.zeros((2, extent, extent))
        halo = np.zeros((2, extent, halo_width))
        for which, taps in enumerate((slope, smooth)):
            for i in range(extent):
                for shift, value in taps.items():
                    j = i + shift
                    if 0 <= j < extent:
                        whole[which, i, j] += value
                    else:
                        halo[which, i, halo_places[j if j < 0 else j - extent]] += value
        return whole.reshape(2 * extent, extent), halo.reshape(2 * extent, halo_width)

    main, rim = banded(rows, {-2: 0, -1: 1, 0: 2, 1: 3}, 8)
    along_rows = np.concatenate([main, main, rim, rim], axis=1)
    main, rim = banded(cols, {0: 0, 1: 1, -2: LANES - 2, -1: LANES - 1}, LANES)
    along_cols = np.concatenate([main, main, rim, rim], axis=1).T
    return along_rows.astype(ml_dtypes.bfloat16), along_cols.astype(ml_dtypes.bfloat16)


def halves(x):
    high = x.astype(jnp.bfloat16)
    return high, (x - high.astype(jnp.float32)).astype(jnp.bfloat16)


def stencil_kernel(
    side, layers, jac_ref, mix_ref, source, low_ref, high_ref, left_ref, right_ref, rows_ref, cols_ref,
    out, state, radial, pitch, parts, mixer, slopes, sems,
):
    step = pl.program_id(0)
    fields, _, rows, cols = out.shape
    chunk, wide = 16, 2 * LANES
    scale = time_step * damping
    axial = (0.5 if side else -0.5) * time_step
    lane = lax.broadcasted_iota(jnp.int32, (rows, LANES), 1)

    def load(layer):
        taken = layer if side == 0 else layers - 1 - layer
        return pltpu.make_async_copy(source.at[:, taken], state.at[:, layer + 2], sems.at[layer])

    def products(t, slot):
        unit = 2 * t + side
        place, first = unit // UNITS, unit % UNITS * (2 * fields)
        from_left, from_right = left_ref[place], right_ref[place]
        for f in range(fields):
            at = first + 2 * f
            before = jnp.where(lane < LANES - 2, lane + 2, lane + 2 - LANES)
            rim = jnp.where((before >= at) & (before < at + 2), from_left, from_right)
            rim = pltpu.roll(rim, (LANES - at) % LANES, 1)
            rim = jnp.where((lane < 2) | (lane >= LANES - 2), rim, 0.0)
            span = slice(f * rows, (f + 1) * rows)
            x_high, x_low = halves(state[f, t + 2])
            rim_high, rim_low = halves(rim)
            parts[span, :cols] = x_high
            parts[span, cols : 2 * cols] = x_low
            parts[span, 2 * cols : 2 * cols + LANES] = rim_high
            parts[span, 2 * cols + LANES :] = rim_low
            halo = jnp.concatenate(
                [low_ref[0, t, f], high_ref[0, t, f], jnp.zeros((4, cols), jnp.float32)], axis=0
            )
            halo_high = halo.astype(jnp.bfloat16).astype(jnp.float32)
            halo = jnp.concatenate([halo_high, halo - halo_high], axis=0).astype(jnp.bfloat16)
            radial[slot, f] = jnp.dot(
                rows_ref[...],
                jnp.concatenate([x_high, x_low, halo], axis=0),
                preferred_element_type=jnp.float32,
            )
        pitch[slot] = jnp.dot(parts[...], cols_ref[...], preferred_element_type=jnp.float32)

    def advance(t, slot):
        here = t + 2
        for at in range(0, rows, chunk):
            span = slice(at, at + chunk)
            totals = []
            for f in range(fields):
                near = state[f, here + 1, span, :] + state[f, here - 1, span, :]
                far = state[f, here + 2, span, :] + state[f, here - 2, span, :]
                totals.append(
                    (state[f, here, span, :] * (1.0 - 6.0 * scale) + (near * 4.0 - far) * scale)
                    + (
                        radial[slot, f, rows + at : rows + at + chunk, :]
                        + pitch[slot, f * rows + at : f * rows + at + chunk, cols:]
                    )
                )
            place = at // chunk
            for g in range(fields):
                for d, slope in enumerate(
                    (
                        state[g, here + 1, span, :] - state[g, here - 1, span, :],
                        radial[slot, g, span, :],
                        pitch[slot, g * rows + at : g * rows + at + chunk, :cols],
                    )
                ):
                    first = (d * fields + g) * chunk
                    high, low = halves(slope)
                    slopes[slot, place, first : first + chunk, :] = high
                    slopes[slot, place, wide + first : wide + first + chunk, :] = low
            mixed = jnp.dot(
                mixer[:, : 2 * wide], slopes[slot, place], preferred_element_type=jnp.float32
            ) + jnp.dot(
                mixer[:, 2 * wide :], slopes[slot, place, :wide, :], preferred_element_type=jnp.float32
            )
            for f in range(fields):
                out[f, slot if side == 0 else 1 - slot, span, :] = (
                    totals[f] + mixed[f * chunk : (f + 1) * chunk]
                )

    @pl.when(step == 0)
    def _():
        for layer in range(layers):
            load(layer).start()
        state[:, 0:2] = jnp.zeros((fields, 2, rows, cols), jnp.float32)
        spot = lax.broadcasted_iota(jnp.int32, (chunk, wide), 1)
        own = spot % chunk == lax.broadcasted_iota(jnp.int32, (chunk, wide), 0)
        for f in range(fields):
            entries = jnp.zeros((chunk, wide), jnp.float32)
            for d in range(3):
                for g in range(fields):
                    entry = jnp.where(own & (spot // chunk == d * fields + g), jac_ref[d, f, g], 0.0)
                    entries = entries + (entry * axial if d == 0 else entry)
            high, low = halves(entries)
            band = slice(f * chunk, (f + 1) * chunk)
            mixer[band, :wide] = high
            mixer[band, wide : 2 * wide] = high
            mixer[band, 2 * wide :] = low
        used = 3 * fields * chunk
        blank = jnp.zeros((2, rows // chunk, wide - used, cols), jnp.bfloat16)
        slopes[:, :, used:wide, :] = blank
        slopes[:, :, wide + used :, :] = blank
        load(0).wait()
        load(1).wait()

    @pl.when(2 * step + 2 < layers)
    def _():
        load(2 * step + 2).wait()
        load(2 * step + 3).wait()

    @pl.when(2 * step == layers - 2)
    def _():
        for ghost in range(2):
            for at in range(0, rows, chunk):
                span = slice(at, at + chunk)
                planes = [state[g, layers + 1 - ghost, span, :] for g in range(fields)]
                for f in range(fields):
                    total = mix_ref[f, 0] * planes[0]
                    for g in range(1, fields):
                        total = total + mix_ref[f, g] * planes[g]
                    state[f, layers + 2 + ghost, span, :] = total

    for slot in range(2):
        products(2 * step + slot, slot)
    for slot in range(2):
        advance(2 * step + slot, slot)


def stencil(side, state, low, high, left, right, weights, mix):
    fields, layers, rows, cols = state.shape
    along_rows, along_cols = difference_tables(rows, cols)
    smem = pl.BlockSpec(memory_space=pltpu.SMEM)
    vmem = pl.BlockSpec(memory_space=pltpu.VMEM)
    edge_spec = pl.BlockSpec((1, layers, fields, 2, cols), lambda t: (side, 0, 0, 0, 0))
    side_spec = pl.BlockSpec(left.shape, lambda t: (0, 0, 0))
    steps = layers // 2
    return pl.pallas_call(
        functools.partial(stencil_kernel, side, layers),
        grid=(steps,),
        out_shape=jax.ShapeDtypeStruct(state.shape, jnp.float32),
        in_specs=[smem, smem, pl.BlockSpec(memory_space=pl.ANY), edge_spec, edge_spec, side_spec, side_spec, vmem, vmem],
        out_specs=pl.BlockSpec(
            (fields, 2, rows, cols), lambda t: (0, t if side == 0 else steps - 1 - t, 0, 0)
        ),
        scratch_shapes=[
            pltpu.VMEM((fields, layers + 4, rows, cols), jnp.float32),
            pltpu.VMEM((2, fields, 2 * rows, cols), jnp.float32),
            pltpu.VMEM((2, fields * rows, 2 * cols), jnp.float32),
            pltpu.VMEM((fields * rows, 2 * cols + 2 * LANES), jnp.bfloat16),
            pltpu.VMEM((fields * 16, 6 * LANES), jnp.bfloat16),
            pltpu.VMEM((2, rows // 16, 4 * LANES, cols), jnp.bfloat16),
            pltpu.SemaphoreType.DMA((layers,)),
        ],
        compiler_params=pltpu.CompilerParams(vmem_limit_bytes=WIDE),
        cost_estimate=pl.CostEstimate(
            flops=60 * state.size, bytes_accessed=16 * state.size, transcendentals=0
        ),
        name=("stator_stencil", "rotor_stencil")[side],
    )(weights, mix, state, low, high, left, right, jnp.asarray(along_rows), jnp.asarray(along_cols))


def close_kernel(jac_ref, mix_ref, modes_ref, stator_ref, rotor_ref, stator_out, rotor_out):
    fields = stator_ref.shape[0]
    count = modes_ref.shape[0]
    step = modes_ref.shape[4]
    scale = time_step * damping

    def combine(row, sources):
        total = row(0) * sources[0]
        for g in range(1, fields):
            total = total + row(g) * sources[g]
        return total

    for side, (ref, out) in enumerate(((stator_ref, stator_out), (rotor_ref, rotor_out))):
        near, far = (1, 0) if side == 0 else (0, 1)
        sign = -1.0 if side else 1.0
        for q in range(count):
            span = slice(q * step, (q + 1) * step)
            ghosts = []
            for ghost in range(2):
                planes = [modes_ref[q, side, g, ghost] for g in range(fields)]
                ghosts.append([combine(lambda g: mix_ref[f, g], planes) for f in range(fields)])
            first, second = ghosts
            for f in range(fields):
                slope = combine(lambda g: jac_ref[0, f, g], first) * (-0.5 * time_step)
                bend = first[f] * 4.0 - second[f]
                out[f, near, span, :] = ref[f, near, span, :] + (slope + bend * (sign * scale))
                out[f, far, span, :] = ref[f, far, span, :] - first[f] * (sign * scale)


def close(modes, stator, rotor, jacobians, field_mix):
    fields, layers, rows, cols = stator.shape
    count, _, _, _, step, _ = modes.shape
    group = max(1, count // 4)
    block = (fields, 2, rows // count * group, cols)
    specs = (
        pl.BlockSpec(block, lambda q: (0, layers // 2 - 1, q, 0)),
        pl.BlockSpec(block, lambda q: (0, 0, q, 0)),
    )
    shape = jax.ShapeDtypeStruct(stator.shape, jnp.float32)
    return pl.pallas_call(
        close_kernel,
        grid=(count // group,),
        out_shape=(shape, shape),
        in_specs=[
            pl.BlockSpec(memory_space=pltpu.SMEM),
            pl.BlockSpec(memory_space=pltpu.SMEM),
            pl.BlockSpec((group,) + modes.shape[1:], lambda q: (q, 0, 0, 0, 0, 0)),
            *specs,
        ],
        out_specs=specs,
        input_output_aliases={3: 0, 4: 1},
        compiler_params=pltpu.CompilerParams(vmem_limit_bytes=NARROW),
        cost_estimate=pl.CostEstimate(
            flops=30 * modes.size, bytes_accessed=12 * modes.size, transcendentals=0
        ),
        name="interface",
    )(jacobians, field_mix, modes, stator, rotor)


def shards(stator, rotor, jacobians, field_mix, mode_blend, rotor_offset):
    fields, layers, rows, cols = stator.shape
    count = lax.axis_size("pitch")
    spans = lax.axis_size("span")
    step = rows // count

    planes = interface_planes(stator, rotor, count).reshape(count, 2, fields * 2 * step, cols)

    planes, *states = lax.optimization_barrier((planes, stator, rotor))
    received = lax.all_to_all(planes, "pitch", 0, 0, tiled=True)
    low, high, left, right = pack_edges(*states)
    ring = [(i, (i + 1) % count) for i in range(count)]
    line = [(i, i + 1) for i in range(spans - 1)]
    from_left = lax.ppermute(right, "pitch", ring)
    from_right = lax.ppermute(left, "pitch", [(b, a) for a, b in ring])
    from_below = lax.ppermute(high, "span", line)
    from_above = lax.ppermute(low, "span", [(b, a) for a, b in line])

    edges = (from_below, from_above, from_left, from_right)
    blend = mode_blend.reshape(fields, LANES, OUTER) * (1.0 / NP)
    blend = jnp.moveaxis(blend, 2, 0)[outer_order().reshape(-1)]
    blend = blend.reshape(PAIRS, 2, fields, LANES).transpose(0, 2, 1, 3).reshape(PAIRS, fields, 2 * LANES)
    received, edges = lax.optimization_barrier((received, edges))
    sent = transform(received, rotor_offset, blend, fields)
    modes = lax.all_to_all(sent, "pitch", 0, 0, tiled=True)
    modes = modes.reshape(count, 2, fields, 2, step, cols)
    stator_mid = stencil(0, stator, *edges, jacobians, field_mix)
    rotor_mid = stencil(1, rotor, *edges, jacobians, field_mix)
    return close(modes, stator_mid, rotor_mid, jacobians, field_mix)


def solution(mesh):
    block = P(None, None, "span", "pitch")
    in_specs = (block, block, P(), P(), P(), P())
    return jax.shard_map(
        shards, mesh=mesh, in_specs=in_specs, out_specs=(block, block), check_vma=False
    )
```

```python
import functools
import math

import jax
import jax.numpy as jnp
import ml_dtypes
import numpy as np
from jax import lax
from jax.experimental import pallas as pl
from jax.experimental.pallas import tpu as pltpu
from jax.sharding import PartitionSpec as P

NP = 2048
LANES = 128
OUTER = NP // LANES
PAIRS = OUTER // 2
UNITS = 12

time_step = 0.5
damping = 1.0 / 32.0
WIDE = 56 * 1024 * 1024
NARROW = 16 * 1024 * 1024


def mode_tables():
    inner = np.arange(LANES)
    out = np.zeros((PAIRS, 2 * LANES, 2 * LANES))

    def angles(outer):
        return 2.0 * math.pi * (np.outer(inner, outer + OUTER * inner) % NP) / NP

    for m in range(PAIRS):
        first, second = (0, PAIRS) if m == 0 else (m, OUTER - m)
        a, b = angles(first), angles(second)
        if m == 0:
            out[m, :LANES, :LANES] = np.cos(a) + np.sin(a)
            out[m, LANES:, LANES:] = np.cos(b) + np.sin(b)
        else:
            out[m, :LANES, :LANES] = np.cos(a)
            out[m, LANES:, :LANES] = np.sin(a)
            out[m, :LANES, LANES:] = np.sin(b)
            out[m, LANES:, LANES:] = np.cos(b)
    high = out.astype(ml_dtypes.bfloat16)
    low = (out - high.astype(np.float64)).astype(ml_dtypes.bfloat16)
    return high, low


def outer_order():
    order = [(0, PAIRS)] + [(m, OUTER - m) for m in range(1, PAIRS)]
    return np.array(order)


def fast_hartley(parts):
    count = len(parts)
    if count == 1:
        return parts
    half = count // 2
    even = fast_hartley(parts[0::2])
    odd = fast_hartley(parts[1::2])
    turned = []
    for k in range(half):
        if k == 0:
            turned.append(odd[0])
        elif 4 * k == count:
            turned.append(odd[half - k])
        else:
            angle = 2.0 * math.pi * k / count
            turned.append(odd[k] * math.cos(angle) + odd[half - k] * math.sin(angle))
    return [even[k] + turned[k] for k in range(half)] + [even[k] - turned[k] for k in range(half)]


def split_dot(x, high, low, dims):
    x_high = x.astype(jnp.bfloat16)
    x_low = (x - x_high.astype(jnp.float32)).astype(jnp.bfloat16)
    dot = functools.partial(
        lax.dot_general, dimension_numbers=(dims, ((), ())), preferred_element_type=jnp.float32
    )
    return dot(x_high, high) + (dot(x_low, high) + dot(x_high, low))


def transform_kernel(fields, offset_ref, got_ref, blend_ref, high_ref, low_ref, out_ref, turn, work):
    rows, cols = got_ref.shape[2:]
    per = cols // LANES
    offset = offset_ref[0]
    whole, part = offset // LANES, offset % LANES
    chunk = 8 if rows % 8 == 0 else rows
    lane = lax.broadcasted_iota(jnp.int32, (chunk, LANES), 1)
    pairs = outer_order()

    def block(i):
        return i // per, slice((i % per) * LANES, (i % per + 1) * LANES)

    for i in range(OUTER):
        device, lanes = block(i)
        turn[i] = pltpu.roll(got_ref[device, 1, :, lanes], part, 1)
    for at in range(0, rows, chunk):
        span = slice(at, at + chunk)
        parts = []
        for i in range(OUTER):
            device, lanes = block(i)
            now = turn[(i - whole + OUTER) % OUTER, span, :]
            before = turn[(i - whole - 1 + OUTER) % OUTER, span, :]
            parts.append(jnp.where(lane >= part, now, before) - got_ref[device, 0, span, lanes])
        modes = fast_hartley(parts)
        for m in range(PAIRS):
            work[m, span, :LANES] = modes[pairs[m, 0]]
            work[m, span, LANES:] = modes[pairs[m, 1]]
    for m in range(PAIRS):
        got = split_dot(work[m], high_ref[m], low_ref[m], ((1,), (0,))) * (1.0 / NP)
        per_field = rows // fields
        got = jnp.concatenate(
            [
                got[f * per_field : (f + 1) * per_field]
                * jnp.concatenate([blend_ref[k, f : f + 1, :] for k in pairs[m]], axis=1)
                for f in range(fields)
            ],
            axis=0,
        )
        work[m] = split_dot(got, high_ref[m], low_ref[m], ((1,), (1,)))
    back = (LANES - part) % LANES
    for at in range(0, rows, chunk):
        span = slice(at, at + chunk)
        modes = [None] * OUTER
        for m in range(PAIRS):
            modes[pairs[m, 0]] = work[m, span, :LANES]
            modes[pairs[m, 1]] = work[m, span, LANES:]
        parts = fast_hartley(modes)
        for i in range(OUTER):
            device, lanes = block(i)
            out_ref[device, 0, span, lanes] = parts[i]
            turn[i, span, :] = pltpu.roll(parts[i], back, 1)
        for i in range(OUTER):
            device, lanes = block(i)
            now = turn[(i + whole) % OUTER, span, :]
            after = turn[(i + whole + 1) % OUTER, span, :]
            out_ref[device, 1, span, lanes] = jnp.where(lane < LANES - part, now, after)


def transform(received, offset, blend, fields):
    high, low = mode_tables()
    count, _, rows, cols = received.shape
    vmem = pl.BlockSpec(memory_space=pltpu.VMEM)
    return pl.pallas_call(
        functools.partial(transform_kernel, fields),
        out_shape=jax.ShapeDtypeStruct(received.shape, jnp.float32),
        in_specs=[pl.BlockSpec(memory_space=pltpu.SMEM)] + [vmem] * 4,
        out_specs=vmem,
        scratch_shapes=[
            pltpu.VMEM((OUTER, rows, LANES), jnp.float32),
            pltpu.VMEM((PAIRS, rows, 2 * LANES), jnp.float32),
        ],
        compiler_params=pltpu.CompilerParams(vmem_limit_bytes=NARROW),
        cost_estimate=pl.CostEstimate(
            flops=12 * rows * PAIRS * 4 * LANES * LANES, bytes_accessed=5_000_000, transcendentals=0
        ),
        name="modes",
    )(offset, received, blend, jnp.asarray(high), jnp.asarray(low))


def planes_kernel(stator, rotor, *outs):
    count, _, _, step, _ = outs[0].shape
    for q in range(count):
        span = slice(q * step, (q + 1) * step)
        for ghost, out in enumerate(outs):
            out[q, 0] = stator[:, 1 - ghost, span, :]
            out[q, 1] = rotor[:, ghost, span, :]


def interface_planes(stator, rotor, count):
    fields, layers, rows, cols = stator.shape
    step = rows // count
    group = max(1, count // 2)
    block = (fields, 2, group * step, cols)
    return pl.pallas_call(
        planes_kernel,
        grid=(count // group,),
        out_shape=(jax.ShapeDtypeStruct((count, 2, fields, step, cols), jnp.float32),) * 2,
        in_specs=[
            pl.BlockSpec(block, lambda q: (0, layers // 2 - 1, q, 0)),
            pl.BlockSpec(block, lambda q: (0, 0, q, 0)),
        ],
        out_specs=(pl.BlockSpec((group, 2, fields, step, cols), lambda q: (q, 0, 0, 0, 0)),) * 2,
        compiler_params=pltpu.CompilerParams(vmem_limit_bytes=WIDE),
        name="planes",
    )(stator, rotor)


def pack_kernel(stator_ref, rotor_ref, low_ref, high_ref, left_ref, right_ref):
    fields, layers, rows, cols = stator_ref.shape
    lane = lax.broadcasted_iota(jnp.int32, (rows, LANES), 1)
    for layer in range(layers):
        for side, ref in enumerate((stator_ref, rotor_ref)):
            taken = layer if side == 0 else layers - 1 - layer
            unit = 2 * (pl.program_id(0) * layers + layer) + side
            place, first = unit // UNITS, unit % UNITS * (2 * fields)
            left = jnp.zeros((rows, LANES), jnp.float32)
            right = jnp.zeros((rows, LANES), jnp.float32)
            for f in range(fields):
                low_ref[side, layer, f] = ref[f, taken, :2, :]
                high_ref[side, layer, f] = ref[f, taken, rows - 2 :, :]
                ends = jnp.where(
                    lane < LANES // 2, ref[f, taken, :, :LANES], ref[f, taken, :, cols - LANES :]
                )
                ends = pltpu.roll(ends, 2 * f, 1) if f else ends
                left = jnp.where(lane // 2 == f, ends, left)
                right = jnp.where(lane // 2 == (f - 1) % (LANES // 2), ends, right)
            fresh = (lane >= first) & (lane < first + 2 * fields)
            left_ref[place] = jnp.where(fresh, pltpu.roll(left, first, 1), left_ref[place])
            after = jnp.where(lane < LANES - 2, lane + 2, lane + 2 - LANES)
            fresh = (after >= first) & (after < first + 2 * fields)
            right_ref[place] = jnp.where(fresh, pltpu.roll(right, first, 1), right_ref[place])


def pack_edges(stator, rotor):
    fields, layers, rows, cols = stator.shape
    blocks = -(-2 * layers // UNITS)
    each = max(n for n in (4, 2, 1) if layers % n == 0)
    steps = layers // each
    block = (fields, each, rows, cols)
    edge = jax.ShapeDtypeStruct((2, layers, fields, 2, cols), jnp.float32)
    side = jax.ShapeDtypeStruct((blocks, rows, LANES), jnp.float32)
    edge_spec = pl.BlockSpec((2, each, fields, 2, cols), lambda t: (0, t, 0, 0, 0))
    side_spec = pl.BlockSpec((blocks, rows, LANES), lambda t: (0, 0, 0))
    return pl.pallas_call(
        pack_kernel,
        grid=(steps,),
        out_shape=(edge, edge, side, side),
        in_specs=[
            pl.BlockSpec(block, lambda t: (0, t, 0, 0)),
            pl.BlockSpec(block, lambda t: (0, steps - 1 - t, 0, 0)),
        ],
        out_specs=(edge_spec, edge_spec, side_spec, side_spec),
        compiler_params=pltpu.CompilerParams(vmem_limit_bytes=WIDE),
        cost_estimate=pl.CostEstimate(
            flops=0, bytes_accessed=2 * 4 * stator.size, transcendentals=0
        ),
        name="edges",
    )(stator, rotor)


def difference_tables(rows, cols):
    scale = time_step * damping
    slope = {1: -0.5 * time_step, -1: 0.5 * time_step}
    smooth = {0: -6.0 * scale, 1: 4.0 * scale, -1: 4.0 * scale, 2: -scale, -2: -scale}

    def banded(extent, halo_places, halo_width):
        whole = np.zeros((2, extent, extent))
        halo = np.zeros((2, extent, halo_width))
        for which, taps in enumerate((slope, smooth)):
            for i in range(extent):
                for shift, value in taps.items():
                    j = i + shift
                    if 0 <= j < extent:
                        whole[which, i, j] += value
                    else:
                        halo[which, i, halo_places[j if j < 0 else j - extent]] += value
        return whole.reshape(2 * extent, extent), halo.reshape(2 * extent, halo_width)

    main, rim = banded(rows, {-2: 0, -1: 1, 0: 2, 1: 3}, 8)
    along_rows = np.concatenate([main, main, rim, rim], axis=1)
    main, rim = banded(cols, {0: 0, 1: 1, -2: LANES - 2, -1: LANES - 1}, LANES)
    along_cols = np.concatenate([main, main, rim, rim], axis=1).T
    return along_rows.astype(ml_dtypes.bfloat16), along_cols.astype(ml_dtypes.bfloat16)


def halves(x):
    high = x.astype(jnp.bfloat16)
    return high, (x - high.astype(jnp.float32)).astype(jnp.bfloat16)


def stencil_kernel(
    side, layers, jac_ref, mix_ref, source, low_ref, high_ref, left_ref, right_ref, rows_ref, cols_ref,
    out, state, radial, pitch, parts, mixer, slopes, sems,
):
    step = pl.program_id(0)
    fields, _, rows, cols = out.shape
    chunk, wide = 16, 2 * LANES
    scale = time_step * damping
    axial = (0.5 if side else -0.5) * time_step
    lane = lax.broadcasted_iota(jnp.int32, (rows, LANES), 1)

    def load(layer):
        taken = layer if side == 0 else layers - 1 - layer
        return pltpu.make_async_copy(source.at[:, taken], state.at[:, layer + 2], sems.at[layer])

    def products(t, slot):
        unit = 2 * t + side
        place, first = unit // UNITS, unit % UNITS * (2 * fields)
        from_left, from_right = left_ref[place], right_ref[place]
        for f in range(fields):
            at = first + 2 * f
            before = jnp.where(lane < LANES - 2, lane + 2, lane + 2 - LANES)
            rim = jnp.where((before >= at) & (before < at + 2), from_left, from_right)
            rim = pltpu.roll(rim, (LANES - at) % LANES, 1)
            rim = jnp.where((lane < 2) | (lane >= LANES - 2), rim, 0.0)
            span = slice(f * rows, (f + 1) * rows)
            x_high, x_low = halves(state[f, t + 2])
            rim_high, rim_low = halves(rim)
            parts[span, :cols] = x_high
            parts[span, cols : 2 * cols] = x_low
            parts[span, 2 * cols : 2 * cols + LANES] = rim_high
            parts[span, 2 * cols + LANES :] = rim_low
            halo = jnp.concatenate(
                [low_ref[0, t, f], high_ref[0, t, f], jnp.zeros((4, cols), jnp.float32)], axis=0
            )
            halo_high = halo.astype(jnp.bfloat16).astype(jnp.float32)
            halo = jnp.concatenate([halo_high, halo - halo_high], axis=0).astype(jnp.bfloat16)
            radial[slot, f] = jnp.dot(
                rows_ref[...],
                jnp.concatenate([x_high, x_low, halo], axis=0),
                preferred_element_type=jnp.float32,
            )
        pitch[slot] = jnp.dot(parts[...], cols_ref[...], preferred_element_type=jnp.float32)

    def advance(t, slot):
        here = t + 2
        for at in range(0, rows, chunk):
            span = slice(at, at + chunk)
            totals = []
            for f in range(fields):
                near = state[f, here + 1, span, :] + state[f, here - 1, span, :]
                far = state[f, here + 2, span, :] + state[f, here - 2, span, :]
                totals.append(
                    (state[f, here, span, :] * (1.0 - 6.0 * scale) + (near * 4.0 - far) * scale)
                    + (
                        radial[slot, f, rows + at : rows + at + chunk, :]
                        + pitch[slot, f * rows + at : f * rows + at + chunk, cols:]
                    )
                )
            place = at // chunk
            for g in range(fields):
                for d, slope in enumerate(
                    (
                        state[g, here + 1, span, :] - state[g, here - 1, span, :],
                        radial[slot, g, span, :],
                        pitch[slot, g * rows + at : g * rows + at + chunk, :cols],
                    )
                ):
                    first = (d * fields + g) * chunk
                    high, low = halves(slope)
                    slopes[slot, place, first : first + chunk, :] = high
                    slopes[slot, place, wide + first : wide + first + chunk, :] = low
            mixed = jnp.dot(
                mixer[:, : 2 * wide], slopes[slot, place], preferred_element_type=jnp.float32
            ) + jnp.dot(
                mixer[:, 2 * wide :], slopes[slot, place, :wide, :], preferred_element_type=jnp.float32
            )
            for f in range(fields):
                out[f, slot if side == 0 else 1 - slot, span, :] = (
                    totals[f] + mixed[f * chunk : (f + 1) * chunk]
                )

    @pl.when(step == 0)
    def _():
        for layer in range(layers):
            load(layer).start()
        state[:, 0:2] = jnp.zeros((fields, 2, rows, cols), jnp.float32)
        spot = lax.broadcasted_iota(jnp.int32, (chunk, wide), 1)
        own = spot % chunk == lax.broadcasted_iota(jnp.int32, (chunk, wide), 0)
        for f in range(fields):
            entries = jnp.zeros((chunk, wide), jnp.float32)
            for d in range(3):
                for g in range(fields):
                    entry = jnp.where(own & (spot // chunk == d * fields + g), jac_ref[d, f, g], 0.0)
                    entries = entries + (entry * axial if d == 0 else entry)
            high, low = halves(entries)
            band = slice(f * chunk, (f + 1) * chunk)
            mixer[band, :wide] = high
            mixer[band, wide : 2 * wide] = high
            mixer[band, 2 * wide :] = low
        used = 3 * fields * chunk
        blank = jnp.zeros((2, rows // chunk, wide - used, cols), jnp.bfloat16)
        slopes[:, :, used:wide, :] = blank
        slopes[:, :, wide + used :, :] = blank
        load(0).wait()
        load(1).wait()

    @pl.when(2 * step + 2 < layers)
    def _():
        load(2 * step + 2).wait()
        load(2 * step + 3).wait()

    @pl.when(2 * step == layers - 2)
    def _():
        for ghost in range(2):
            for at in range(0, rows, chunk):
                span = slice(at, at + chunk)
                planes = [state[g, layers + 1 - ghost, span, :] for g in range(fields)]
                for f in range(fields):
                    total = mix_ref[f, 0] * planes[0]
                    for g in range(1, fields):
                        total = total + mix_ref[f, g] * planes[g]
                    state[f, layers + 2 + ghost, span, :] = total

    for slot in range(2):
        products(2 * step + slot, slot)
    for slot in range(2):
        advance(2 * step + slot, slot)


def stencil(side, state, low, high, left, right, weights, mix):
    fields, layers, rows, cols = state.shape
    along_rows, along_cols = difference_tables(rows, cols)
    smem = pl.BlockSpec(memory_space=pltpu.SMEM)
    vmem = pl.BlockSpec(memory_space=pltpu.VMEM)
    edge_spec = pl.BlockSpec((1, layers, fields, 2, cols), lambda t: (side, 0, 0, 0, 0))
    side_spec = pl.BlockSpec(left.shape, lambda t: (0, 0, 0))
    steps = layers // 2
    return pl.pallas_call(
        functools.partial(stencil_kernel, side, layers),
        grid=(steps,),
        out_shape=jax.ShapeDtypeStruct(state.shape, jnp.float32),
        in_specs=[smem, smem, pl.BlockSpec(memory_space=pl.ANY), edge_spec, edge_spec, side_spec, side_spec, vmem, vmem],
        out_specs=pl.BlockSpec(
            (fields, 2, rows, cols), lambda t: (0, t if side == 0 else steps - 1 - t, 0, 0)
        ),
        scratch_shapes=[
            pltpu.VMEM((fields, layers + 4, rows, cols), jnp.float32),
            pltpu.VMEM((2, fields, 2 * rows, cols), jnp.float32),
            pltpu.VMEM((2, fields * rows, 2 * cols), jnp.float32),
            pltpu.VMEM((fields * rows, 2 * cols + 2 * LANES), jnp.bfloat16),
            pltpu.VMEM((fields * 16, 6 * LANES), jnp.bfloat16),
            pltpu.VMEM((2, rows // 16, 4 * LANES, cols), jnp.bfloat16),
            pltpu.SemaphoreType.DMA((layers,)),
        ],
        compiler_params=pltpu.CompilerParams(vmem_limit_bytes=WIDE),
        cost_estimate=pl.CostEstimate(
            flops=60 * state.size, bytes_accessed=16 * state.size, transcendentals=0
        ),
        name=("stator_stencil", "rotor_stencil")[side],
    )(weights, mix, state, low, high, left, right, jnp.asarray(along_rows), jnp.asarray(along_cols))


def close_kernel(jac_ref, mix_ref, first_ref, second_ref, stator_ref, rotor_ref, stator_out, rotor_out):
    fields = stator_ref.shape[0]
    count, _, _, step, _ = first_ref.shape
    scale = time_step * damping

    def combine(row, sources):
        total = row(0) * sources[0]
        for g in range(1, fields):
            total = total + row(g) * sources[g]
        return total

    for side, (ref, out) in enumerate(((stator_ref, stator_out), (rotor_ref, rotor_out))):
        near, far = (1, 0) if side == 0 else (0, 1)
        sign = -1.0 if side else 1.0
        for q in range(count):
            span = slice(q * step, (q + 1) * step)
            ghosts = []
            for modes_ref in (first_ref, second_ref):
                planes = [modes_ref[q, side, g] for g in range(fields)]
                ghosts.append([combine(lambda g: mix_ref[f, g], planes) for f in range(fields)])
            first, second = ghosts
            for f in range(fields):
                slope = combine(lambda g: jac_ref[0, f, g], first) * (-0.5 * time_step)
                bend = first[f] * 4.0 - second[f]
                out[f, near, span, :] = ref[f, near, span, :] + (slope + bend * (sign * scale))
                out[f, far, span, :] = ref[f, far, span, :] - first[f] * (sign * scale)


def close(first, second, stator, rotor, jacobians, field_mix):
    fields, layers, rows, cols = stator.shape
    count = first.shape[0]
    group = max(1, count // 4)
    block = (fields, 2, rows // count * group, cols)
    specs = (
        pl.BlockSpec(block, lambda q: (0, layers // 2 - 1, q, 0)),
        pl.BlockSpec(block, lambda q: (0, 0, q, 0)),
    )
    shape = jax.ShapeDtypeStruct(stator.shape, jnp.float32)
    return pl.pallas_call(
        close_kernel,
        grid=(count // group,),
        out_shape=(shape, shape),
        in_specs=[
            pl.BlockSpec(memory_space=pltpu.SMEM),
            pl.BlockSpec(memory_space=pltpu.SMEM),
            pl.BlockSpec((group,) + first.shape[1:], lambda q: (q, 0, 0, 0, 0)),
            pl.BlockSpec((group,) + first.shape[1:], lambda q: (q, 0, 0, 0, 0)),
            *specs,
        ],
        out_specs=specs,
        input_output_aliases={4: 0, 5: 1},
        compiler_params=pltpu.CompilerParams(vmem_limit_bytes=NARROW),
        cost_estimate=pl.CostEstimate(
            flops=60 * first.size, bytes_accessed=24 * first.size, transcendentals=0
        ),
        name="interface",
    )(jacobians, field_mix, first, second, stator, rotor)


def shards(stator, rotor, jacobians, field_mix, mode_blend, rotor_offset):
    fields, layers, rows, cols = stator.shape
    count = lax.axis_size("pitch")
    spans = lax.axis_size("span")
    step = rows // count

    def exchange(block):
        return lax.all_to_all(block.reshape(count, 2, fields * step, cols), "pitch", 0, 0, tiled=True)

    blend = jnp.moveaxis(mode_blend.reshape(fields, LANES, OUTER), 2, 0)

    nearest, second = interface_planes(stator, rotor, count)
    nearest, *states = lax.optimization_barrier((nearest, stator, rotor))
    got = exchange(nearest)
    low, high, left, right = pack_edges(*states)
    ring = [(i, (i + 1) % count) for i in range(count)]
    line = [(i, i + 1) for i in range(spans - 1)]
    from_left = lax.ppermute(right, "pitch", ring)
    from_right = lax.ppermute(left, "pitch", [(b, a) for a, b in ring])
    from_below = lax.ppermute(high, "span", line)
    from_above = lax.ppermute(low, "span", [(b, a) for a, b in line])
    got, second, from_left, from_right = lax.optimization_barrier((got, second, from_left, from_right))
    got_second = exchange(second)
    sent = transform(got, rotor_offset, blend, fields)
    sent, from_left, from_right = lax.optimization_barrier((sent, from_left, from_right))
    edges = (from_below, from_above, from_left, from_right)
    modes = exchange(sent)
    stator_mid = stencil(0, stator, *edges, jacobians, field_mix)
    got_second, stator_mid = lax.optimization_barrier((got_second, stator_mid))
    sent_second = transform(got_second, rotor_offset, blend, fields)
    sent_second, rotor = lax.optimization_barrier((sent_second, rotor))
    modes_second = exchange(sent_second)
    rotor_mid = stencil(1, rotor, *edges, jacobians, field_mix)
    layout = (count, 2, fields, step, cols)
    return close(
        modes.reshape(layout), modes_second.reshape(layout), stator_mid, rotor_mid, jacobians, field_mix
    )


def solution(mesh):
    block = P(None, None, "span", "pitch")
    in_specs = (block, block, P(), P(), P(), P())
    return jax.shard_map(
        shards, mesh=mesh, in_specs=in_specs, out_specs=(block, block), check_vma=False
    )
```

```python
import functools
import math

import jax
import jax.numpy as jnp
import ml_dtypes
import numpy as np
from jax import lax
from jax.experimental import pallas as pl
from jax.experimental.pallas import tpu as pltpu
from jax.sharding import PartitionSpec as P

NP = 2048
LANES = 128
OUTER = NP // LANES
PAIRS = OUTER // 2
UNITS = 12

time_step = 0.5
damping = 1.0 / 32.0
WIDE = 56 * 1024 * 1024
NARROW = 16 * 1024 * 1024


def mode_tables():
    inner = np.arange(LANES)
    out = np.zeros((PAIRS, 2 * LANES, 2 * LANES))

    def angles(outer):
        return 2.0 * math.pi * (np.outer(inner, outer + OUTER * inner) % NP) / NP

    for m in range(PAIRS):
        first, second = (0, PAIRS) if m == 0 else (m, OUTER - m)
        a, b = angles(first), angles(second)
        if m == 0:
            out[m, :LANES, :LANES] = np.cos(a) + np.sin(a)
            out[m, LANES:, LANES:] = np.cos(b) + np.sin(b)
        else:
            out[m, :LANES, :LANES] = np.cos(a)
            out[m, LANES:, :LANES] = np.sin(a)
            out[m, :LANES, LANES:] = np.sin(b)
            out[m, LANES:, LANES:] = np.cos(b)
    high = out.astype(ml_dtypes.bfloat16)
    low = (out - high.astype(np.float64)).astype(ml_dtypes.bfloat16)
    return high, low


def outer_order():
    order = [(0, PAIRS)] + [(m, OUTER - m) for m in range(1, PAIRS)]
    return np.array(order)


def fast_hartley(parts):
    count = len(parts)
    if count == 1:
        return parts
    half = count // 2
    even = fast_hartley(parts[0::2])
    odd = fast_hartley(parts[1::2])
    turned = []
    for k in range(half):
        if k == 0:
            turned.append(odd[0])
        elif 4 * k == count:
            turned.append(odd[half - k])
        else:
            angle = 2.0 * math.pi * k / count
            turned.append(odd[k] * math.cos(angle) + odd[half - k] * math.sin(angle))
    return [even[k] + turned[k] for k in range(half)] + [even[k] - turned[k] for k in range(half)]


def split_dot(x, high, low, dims):
    x_high = x.astype(jnp.bfloat16)
    x_low = (x - x_high.astype(jnp.float32)).astype(jnp.bfloat16)
    dot = functools.partial(
        lax.dot_general, dimension_numbers=(dims, ((), ())), preferred_element_type=jnp.float32
    )
    return dot(x_high, high) + (dot(x_low, high) + dot(x_high, low))


def transform_kernel(fields, offset_ref, got_ref, blend_ref, high_ref, low_ref, out_ref, turn, work):
    rows, cols = got_ref.shape[2:]
    per = cols // LANES
    offset = offset_ref[0]
    whole, part = offset // LANES, offset % LANES
    chunk = 8 if rows % 8 == 0 else rows
    lane = lax.broadcasted_iota(jnp.int32, (chunk, LANES), 1)
    pairs = outer_order()

    def block(i):
        return i // per, slice((i % per) * LANES, (i % per + 1) * LANES)

    for i in range(OUTER):
        device, lanes = block(i)
        turn[i] = pltpu.roll(got_ref[device, 1, :, lanes], part, 1)
    for at in range(0, rows, chunk):
        span = slice(at, at + chunk)
        parts = []
        for i in range(OUTER):
            device, lanes = block(i)
            now = turn[(i - whole + OUTER) % OUTER, span, :]
            before = turn[(i - whole - 1 + OUTER) % OUTER, span, :]
            parts.append(jnp.where(lane >= part, now, before) - got_ref[device, 0, span, lanes])
        modes = fast_hartley(parts)
        for m in range(PAIRS):
            work[m, span, :LANES] = modes[pairs[m, 0]]
            work[m, span, LANES:] = modes[pairs[m, 1]]
    for m in range(PAIRS):
        got = split_dot(work[m], high_ref[m], low_ref[m], ((1,), (0,)))
        per_field = rows // fields
        got = jnp.concatenate(
            [
                got[f * per_field : (f + 1) * per_field] * blend_ref[m, f : f + 1, :]
                for f in range(fields)
            ],
            axis=0,
        )
        work[m] = split_dot(got, high_ref[m], low_ref[m], ((1,), (1,)))
    back = (LANES - part) % LANES
    for at in range(0, rows, chunk):
        span = slice(at, at + chunk)
        modes = [None] * OUTER
        for m in range(PAIRS):
            modes[pairs[m, 0]] = work[m, span, :LANES]
            modes[pairs[m, 1]] = work[m, span, LANES:]
        parts = fast_hartley(modes)
        for i in range(OUTER):
            device, lanes = block(i)
            out_ref[device, 0, span, lanes] = parts[i]
            turn[i, span, :] = pltpu.roll(parts[i], back, 1)
        for i in range(OUTER):
            device, lanes = block(i)
            now = turn[(i + whole) % OUTER, span, :]
            after = turn[(i + whole + 1) % OUTER, span, :]
            out_ref[device, 1, span, lanes] = jnp.where(lane < LANES - part, now, after)


def transform(received, offset, blend, fields):
    high, low = mode_tables()
    count, _, rows, cols = received.shape
    vmem = pl.BlockSpec(memory_space=pltpu.VMEM)
    return pl.pallas_call(
        functools.partial(transform_kernel, fields),
        out_shape=jax.ShapeDtypeStruct(received.shape, jnp.float32),
        in_specs=[pl.BlockSpec(memory_space=pltpu.SMEM)] + [vmem] * 4,
        out_specs=vmem,
        scratch_shapes=[
            pltpu.VMEM((OUTER, rows, LANES), jnp.float32),
            pltpu.VMEM((PAIRS, rows, 2 * LANES), jnp.float32),
        ],
        compiler_params=pltpu.CompilerParams(vmem_limit_bytes=NARROW),
        cost_estimate=pl.CostEstimate(
            flops=12 * rows * PAIRS * 4 * LANES * LANES, bytes_accessed=5_000_000, transcendentals=0
        ),
        name="modes",
    )(offset, received, blend, jnp.asarray(high), jnp.asarray(low))


def planes_kernel(stator, rotor, out):
    count, _, _, _, step, _ = out.shape
    for q in range(count):
        span = slice(q * step, (q + 1) * step)
        for ghost in range(2):
            out[q, 0, :, ghost] = stator[:, 1 - ghost, span, :]
            out[q, 1, :, ghost] = rotor[:, ghost, span, :]


def interface_planes(stator, rotor, count):
    fields, layers, rows, cols = stator.shape
    step = rows // count
    group = max(1, count // 2)
    block = (fields, 2, group * step, cols)
    return pl.pallas_call(
        planes_kernel,
        grid=(count // group,),
        out_shape=jax.ShapeDtypeStruct((count, 2, fields, 2, step, cols), jnp.float32),
        in_specs=[
            pl.BlockSpec(block, lambda q: (0, layers // 2 - 1, q, 0)),
            pl.BlockSpec(block, lambda q: (0, 0, q, 0)),
        ],
        out_specs=pl.BlockSpec((group, 2, fields, 2, step, cols), lambda q: (q, 0, 0, 0, 0, 0)),
        compiler_params=pltpu.CompilerParams(vmem_limit_bytes=WIDE),
        name="planes",
    )(stator, rotor)


def pack_kernel(stator_ref, rotor_ref, low_ref, high_ref, left_ref, right_ref):
    fields, layers, rows, cols = stator_ref.shape
    lane = lax.broadcasted_iota(jnp.int32, (rows, LANES), 1)
    for layer in range(layers):
        for side, ref in enumerate((stator_ref, rotor_ref)):
            taken = layer if side == 0 else layers - 1 - layer
            unit = 2 * (pl.program_id(0) * layers + layer) + side
            place, first = unit // UNITS, unit % UNITS * (2 * fields)
            left = jnp.zeros((rows, LANES), jnp.float32)
            right = jnp.zeros((rows, LANES), jnp.float32)
            for f in range(fields):
                low_ref[side, layer, f] = ref[f, taken, :2, :]
                high_ref[side, layer, f] = ref[f, taken, rows - 2 :, :]
                ends = jnp.where(
                    lane < LANES // 2, ref[f, taken, :, :LANES], ref[f, taken, :, cols - LANES :]
                )
                ends = pltpu.roll(ends, 2 * f, 1) if f else ends
                left = jnp.where(lane // 2 == f, ends, left)
                right = jnp.where(lane // 2 == (f - 1) % (LANES // 2), ends, right)
            fresh = (lane >= first) & (lane < first + 2 * fields)
            left_ref[place] = jnp.where(fresh, pltpu.roll(left, first, 1), left_ref[place])
            after = jnp.where(lane < LANES - 2, lane + 2, lane + 2 - LANES)
            fresh = (after >= first) & (after < first + 2 * fields)
            right_ref[place] = jnp.where(fresh, pltpu.roll(right, first, 1), right_ref[place])


def pack_edges(stator, rotor):
    fields, layers, rows, cols = stator.shape
    blocks = -(-2 * layers // UNITS)
    each = max(n for n in (4, 2, 1) if layers % n == 0)
    steps = layers // each
    block = (fields, each, rows, cols)
    edge = jax.ShapeDtypeStruct((2, layers, fields, 2, cols), jnp.float32)
    side = jax.ShapeDtypeStruct((blocks, rows, LANES), jnp.float32)
    edge_spec = pl.BlockSpec((2, each, fields, 2, cols), lambda t: (0, t, 0, 0, 0))
    side_spec = pl.BlockSpec((blocks, rows, LANES), lambda t: (0, 0, 0))
    return pl.pallas_call(
        pack_kernel,
        grid=(steps,),
        out_shape=(edge, edge, side, side),
        in_specs=[
            pl.BlockSpec(block, lambda t: (0, t, 0, 0)),
            pl.BlockSpec(block, lambda t: (0, steps - 1 - t, 0, 0)),
        ],
        out_specs=(edge_spec, edge_spec, side_spec, side_spec),
        compiler_params=pltpu.CompilerParams(vmem_limit_bytes=WIDE),
        cost_estimate=pl.CostEstimate(
            flops=0, bytes_accessed=2 * 4 * stator.size, transcendentals=0
        ),
        name="edges",
    )(stator, rotor)


def difference_tables(rows, cols):
    scale = time_step * damping
    slope = {1: -0.5 * time_step, -1: 0.5 * time_step}
    smooth = {0: -6.0 * scale, 1: 4.0 * scale, -1: 4.0 * scale, 2: -scale, -2: -scale}

    def banded(extent, halo_places, halo_width):
        whole = np.zeros((2, extent, extent))
        halo = np.zeros((2, extent, halo_width))
        for which, taps in enumerate((slope, smooth)):
            for i in range(extent):
                for shift, value in taps.items():
                    j = i + shift
                    if 0 <= j < extent:
                        whole[which, i, j] += value
                    else:
                        halo[which, i, halo_places[j if j < 0 else j - extent]] += value
        return whole.reshape(2 * extent, extent), halo.reshape(2 * extent, halo_width)

    main, rim = banded(rows, {-2: 0, -1: 1, 0: 2, 1: 3}, 8)
    along_rows = np.concatenate([main, main, rim, rim], axis=1)
    main, rim = banded(cols, {0: 0, 1: 1, -2: LANES - 2, -1: LANES - 1}, LANES)
    along_cols = np.concatenate([main, main, rim, rim], axis=1).T
    return along_rows.astype(ml_dtypes.bfloat16), along_cols.astype(ml_dtypes.bfloat16)


def halves(x):
    high = x.astype(jnp.bfloat16)
    return high, (x - high.astype(jnp.float32)).astype(jnp.bfloat16)


def stencil_kernel(
    side, layers, jac_ref, mix_ref, source, low_ref, high_ref, left_ref, right_ref, rows_ref, cols_ref,
    out, state, radial, pitch, parts, mixer, slopes, sems,
):
    step = pl.program_id(0)
    fields, _, rows, cols = out.shape
    chunk, wide = 16, 2 * LANES
    scale = time_step * damping
    axial = (0.5 if side else -0.5) * time_step
    lane = lax.broadcasted_iota(jnp.int32, (rows, LANES), 1)

    def load(layer):
        taken = layer if side == 0 else layers - 1 - layer
        return pltpu.make_async_copy(source.at[:, taken], state.at[:, layer + 2], sems.at[layer])

    def products(t, slot):
        unit = 2 * t + side
        place, first = unit // UNITS, unit % UNITS * (2 * fields)
        from_left, from_right = left_ref[place], right_ref[place]
        for f in range(fields):
            at = first + 2 * f
            before = jnp.where(lane < LANES - 2, lane + 2, lane + 2 - LANES)
            rim = jnp.where((before >= at) & (before < at + 2), from_left, from_right)
            rim = pltpu.roll(rim, (LANES - at) % LANES, 1)
            rim = jnp.where((lane < 2) | (lane >= LANES - 2), rim, 0.0)
            span = slice((slot * fields + f) * rows, (slot * fields + f + 1) * rows)
            x_high, x_low = halves(state[f, t + 2])
            rim_high, rim_low = halves(rim)
            parts[span, :cols] = x_high
            parts[span, cols : 2 * cols] = x_low
            parts[span, 2 * cols : 2 * cols + LANES] = rim_high
            parts[span, 2 * cols + LANES :] = rim_low
            halo = jnp.concatenate(
                [low_ref[0, t, f], high_ref[0, t, f], jnp.zeros((4, cols), jnp.float32)], axis=0
            )
            halo_high = halo.astype(jnp.bfloat16).astype(jnp.float32)
            halo = jnp.concatenate([halo_high, halo - halo_high], axis=0).astype(jnp.bfloat16)
            radial[slot, f] = jnp.dot(
                rows_ref[...],
                jnp.concatenate([x_high, x_low, halo], axis=0),
                preferred_element_type=jnp.float32,
            )

    def advance(t, slot):
        here = t + 2
        for at in range(0, rows, chunk):
            span = slice(at, at + chunk)
            totals = []
            for f in range(fields):
                near = state[f, here + 1, span, :] + state[f, here - 1, span, :]
                far = state[f, here + 2, span, :] + state[f, here - 2, span, :]
                totals.append(
                    (state[f, here, span, :] * (1.0 - 6.0 * scale) + (near * 4.0 - far) * scale)
                    + (
                        radial[slot, f, rows + at : rows + at + chunk, :]
                        + pitch[pl.ds((slot * fields + f) * rows + at, chunk), cols:]
                    )
                )
            place = at // chunk
            for g in range(fields):
                for d, slope in enumerate(
                    (
                        state[g, here + 1, span, :] - state[g, here - 1, span, :],
                        radial[slot, g, span, :],
                        pitch[pl.ds((slot * fields + g) * rows + at, chunk), :cols],
                    )
                ):
                    first = (d * fields + g) * chunk
                    high, low = halves(slope)
                    slopes[slot, place, 0, first : first + chunk, :] = high
                    slopes[slot, place, 1, first : first + chunk, :] = low
            both = jnp.dot(mixer[...], slopes[slot, place, 0], preferred_element_type=jnp.float32)
            fine = jnp.dot(
                mixer[: fields * chunk, :], slopes[slot, place, 1], preferred_element_type=jnp.float32
            )
            mixed = both[: fields * chunk] + (both[fields * chunk :] + fine)
            for f in range(fields):
                out[f, slot if side == 0 else 1 - slot, span, :] = (
                    totals[f] + mixed[f * chunk : (f + 1) * chunk]
                )

    @pl.when(step == 0)
    def _():
        for layer in range(layers):
            load(layer).start()
        state[:, 0:2] = jnp.zeros((fields, 2, rows, cols), jnp.float32)
        spot = lax.broadcasted_iota(jnp.int32, (chunk, wide), 1)
        own = spot % chunk == lax.broadcasted_iota(jnp.int32, (chunk, wide), 0)
        for f in range(fields):
            entries = jnp.zeros((chunk, wide), jnp.float32)
            for d in range(3):
                for g in range(fields):
                    entry = jnp.where(own & (spot // chunk == d * fields + g), jac_ref[(d * fields + f) * fields + g], 0.0)
                    entries = entries + (entry * axial if d == 0 else entry)
            high, low = halves(entries)
            mixer[f * chunk : (f + 1) * chunk, :] = high
            mixer[(fields + f) * chunk : (fields + f + 1) * chunk, :] = low
        used = 3 * fields * chunk
        slopes[:, :, :, used:, :] = jnp.zeros((2, rows // chunk, 2, wide - used, cols), jnp.bfloat16)
        load(0).wait()
        load(1).wait()

    @pl.when(2 * step + 2 < layers)
    def _():
        load(2 * step + 2).wait()
        load(2 * step + 3).wait()

    @pl.when(2 * step == layers - 2)
    def _():
        for ghost in range(2):
            for at in range(0, rows, chunk):
                span = slice(at, at + chunk)
                planes = [state[g, layers + 1 - ghost, span, :] for g in range(fields)]
                for f in range(fields):
                    total = mix_ref[f, 0] * planes[0]
                    for g in range(1, fields):
                        total = total + mix_ref[f, g] * planes[g]
                    state[f, layers + 2 + ghost, span, :] = total

    for slot in range(2):
        products(2 * step + slot, slot)
    pitch[...] = jnp.dot(parts[...], cols_ref[...], preferred_element_type=jnp.float32)
    for slot in range(2):
        advance(2 * step + slot, slot)


def stencil(side, state, low, high, left, right, weights, mix):
    fields, layers, rows, cols = state.shape
    along_rows, along_cols = difference_tables(rows, cols)
    smem = pl.BlockSpec(memory_space=pltpu.SMEM)
    vmem = pl.BlockSpec(memory_space=pltpu.VMEM)
    edge_spec = pl.BlockSpec((1, layers, fields, 2, cols), lambda t: (side, 0, 0, 0, 0))
    side_spec = pl.BlockSpec(left.shape, lambda t: (0, 0, 0))
    steps = layers // 2
    return pl.pallas_call(
        functools.partial(stencil_kernel, side, layers),
        grid=(steps,),
        out_shape=jax.ShapeDtypeStruct(state.shape, jnp.float32),
        in_specs=[smem, smem, pl.BlockSpec(memory_space=pl.ANY), edge_spec, edge_spec, side_spec, side_spec, vmem, vmem],
        out_specs=pl.BlockSpec(
            (fields, 2, rows, cols), lambda t: (0, t if side == 0 else steps - 1 - t, 0, 0)
        ),
        scratch_shapes=[
            pltpu.VMEM((fields, layers + 4, rows, cols), jnp.float32),
            pltpu.VMEM((2, fields, 2 * rows, cols), jnp.float32),
            pltpu.VMEM((2 * fields * rows, 2 * cols), jnp.float32),
            pltpu.VMEM((2 * fields * rows, 2 * cols + 2 * LANES), jnp.bfloat16),
            pltpu.VMEM((2 * fields * 16, 2 * LANES), jnp.bfloat16),
            pltpu.VMEM((2, rows // 16, 2, 2 * LANES, cols), jnp.bfloat16),
            pltpu.SemaphoreType.DMA((layers,)),
        ],
        compiler_params=pltpu.CompilerParams(vmem_limit_bytes=WIDE),
        cost_estimate=pl.CostEstimate(
            flops=60 * state.size, bytes_accessed=16 * state.size, transcendentals=0
        ),
        name=("stator_stencil", "rotor_stencil")[side],
    )(weights, mix, state, low, high, left, right, jnp.asarray(along_rows), jnp.asarray(along_cols))


def close_kernel(jac_ref, mix_ref, modes_ref, stator_ref, rotor_ref, stator_out, rotor_out):
    fields = stator_ref.shape[0]
    count = modes_ref.shape[0]
    step = modes_ref.shape[4]
    scale = time_step * damping

    def combine(row, sources):
        total = row(0) * sources[0]
        for g in range(1, fields):
            total = total + row(g) * sources[g]
        return total

    for side, (ref, out) in enumerate(((stator_ref, stator_out), (rotor_ref, rotor_out))):
        near, far = (1, 0) if side == 0 else (0, 1)
        sign = -1.0 if side else 1.0
        for q in range(count):
            span = slice(q * step, (q + 1) * step)
            ghosts = []
            for ghost in range(2):
                planes = [modes_ref[q, side, g, ghost] for g in range(fields)]
                ghosts.append([combine(lambda g: mix_ref[f, g], planes) for f in range(fields)])
            first, second = ghosts
            for f in range(fields):
                slope = combine(lambda g: jac_ref[f * fields + g], first) * (-0.5 * time_step)
                bend = first[f] * 4.0 - second[f]
                out[f, near, span, :] = ref[f, near, span, :] + (slope + bend * (sign * scale))
                out[f, far, span, :] = ref[f, far, span, :] - first[f] * (sign * scale)


def close(modes, stator, rotor, jacobians, field_mix):
    fields, layers, rows, cols = stator.shape
    count, _, _, _, step, _ = modes.shape
    group = max(1, count // 4)
    block = (fields, 2, rows // count * group, cols)
    specs = (
        pl.BlockSpec(block, lambda q: (0, layers // 2 - 1, q, 0)),
        pl.BlockSpec(block, lambda q: (0, 0, q, 0)),
    )
    shape = jax.ShapeDtypeStruct(stator.shape, jnp.float32)
    return pl.pallas_call(
        close_kernel,
        grid=(count // group,),
        out_shape=(shape, shape),
        in_specs=[
            pl.BlockSpec(memory_space=pltpu.SMEM),
            pl.BlockSpec(memory_space=pltpu.SMEM),
            pl.BlockSpec((group,) + modes.shape[1:], lambda q: (q, 0, 0, 0, 0, 0)),
            *specs,
        ],
        out_specs=specs,
        input_output_aliases={3: 0, 4: 1},
        compiler_params=pltpu.CompilerParams(vmem_limit_bytes=NARROW),
        cost_estimate=pl.CostEstimate(
            flops=30 * modes.size, bytes_accessed=12 * modes.size, transcendentals=0
        ),
        name="interface",
    )(jacobians, field_mix, modes, stator, rotor)


def shards(stator, rotor, jacobians, field_mix, mode_blend, rotor_offset):
    fields, layers, rows, cols = stator.shape
    count = lax.axis_size("pitch")
    spans = lax.axis_size("span")
    step = rows // count

    planes = interface_planes(stator, rotor, count).reshape(count, 2, fields * 2 * step, cols)

    planes, *states = lax.optimization_barrier((planes, stator, rotor))
    received = lax.all_to_all(planes, "pitch", 0, 0, tiled=True)
    low, high, left, right = pack_edges(*states)
    ring = [(i, (i + 1) % count) for i in range(count)]
    line = [(i, i + 1) for i in range(spans - 1)]
    from_left = lax.ppermute(right, "pitch", ring)
    from_right = lax.ppermute(left, "pitch", [(b, a) for a, b in ring])
    from_below = lax.ppermute(high, "span", line)
    from_above = lax.ppermute(low, "span", [(b, a) for a, b in line])

    edges = (from_below, from_above, from_left, from_right)
    blend = mode_blend.reshape(fields, LANES, OUTER) * (1.0 / NP)
    blend = jnp.moveaxis(blend, 2, 0)[outer_order().reshape(-1)]
    blend = blend.reshape(PAIRS, 2, fields, LANES).transpose(0, 2, 1, 3).reshape(PAIRS, fields, 2 * LANES)
    received, edges, flat = lax.optimization_barrier((received, edges, jacobians.reshape(-1)))
    sent = transform(received, rotor_offset, blend, fields)
    sent, edges, flat = lax.optimization_barrier((sent, edges, flat))
    modes = lax.all_to_all(sent, "pitch", 0, 0, tiled=True)
    modes = modes.reshape(count, 2, fields, 2, step, cols)
    stator_mid = stencil(0, stator, *edges, flat, field_mix)
    rotor_mid = stencil(1, rotor, *edges, flat, field_mix)
    return close(modes, stator_mid, rotor_mid, flat, field_mix)


def solution(mesh):
    block = P(None, None, "span", "pitch")
    in_specs = (block, block, P(), P(), P(), P())
    return jax.shard_map(
        shards, mesh=mesh, in_specs=in_specs, out_specs=(block, block), check_vma=False
    )
```

```python
import functools
import math

import jax
import jax.numpy as jnp
import ml_dtypes
import numpy as np
from jax import lax
from jax.experimental import pallas as pl
from jax.experimental.pallas import tpu as pltpu
from jax.sharding import PartitionSpec as P

NP = 2048
LANES = 128
OUTER = NP // LANES
PAIRS = OUTER // 2
UNITS = 12

time_step = 0.5
damping = 1.0 / 32.0
WIDE = 56 * 1024 * 1024
NARROW = 16 * 1024 * 1024


def mode_tables():
    inner = np.arange(LANES)
    out = np.zeros((PAIRS, 2 * LANES, 2 * LANES))

    def angles(outer):
        return 2.0 * math.pi * (np.outer(inner, outer + OUTER * inner) % NP) / NP

    for m in range(PAIRS):
        first, second = (0, PAIRS) if m == 0 else (m, OUTER - m)
        a, b = angles(first), angles(second)
        if m == 0:
            out[m, :LANES, :LANES] = np.cos(a) + np.sin(a)
            out[m, LANES:, LANES:] = np.cos(b) + np.sin(b)
        else:
            out[m, :LANES, :LANES] = np.cos(a)
            out[m, LANES:, :LANES] = np.sin(a)
            out[m, :LANES, LANES:] = np.sin(b)
            out[m, LANES:, LANES:] = np.cos(b)
    high = out.astype(ml_dtypes.bfloat16)
    low = (out - high.astype(np.float64)).astype(ml_dtypes.bfloat16)
    return high, low


def outer_order():
    order = [(0, PAIRS)] + [(m, OUTER - m) for m in range(1, PAIRS)]
    return np.array(order)


def fast_hartley(parts):
    count = len(parts)
    if count == 1:
        return parts
    half = count // 2
    even = fast_hartley(parts[0::2])
    odd = fast_hartley(parts[1::2])
    turned = []
    for k in range(half):
        if k == 0:
            turned.append(odd[0])
        elif 4 * k == count:
            turned.append(odd[half - k])
        else:
            angle = 2.0 * math.pi * k / count
            turned.append(odd[k] * math.cos(angle) + odd[half - k] * math.sin(angle))
    return [even[k] + turned[k] for k in range(half)] + [even[k] - turned[k] for k in range(half)]


def split_dot(x, high, low, dims):
    x_high = x.astype(jnp.bfloat16)
    x_low = (x - x_high.astype(jnp.float32)).astype(jnp.bfloat16)
    dot = functools.partial(
        lax.dot_general, dimension_numbers=(dims, ((), ())), preferred_element_type=jnp.float32
    )
    return dot(x_high, high) + (dot(x_low, high) + dot(x_high, low))


def transform_kernel(fields, offset_ref, got_ref, blend_ref, high_ref, low_ref, out_ref, turn, work):
    rows, cols = got_ref.shape[2:]
    per = cols // LANES
    offset = offset_ref[0]
    whole, part = offset // LANES, offset % LANES
    chunk = 8 if rows % 8 == 0 else rows
    lane = lax.broadcasted_iota(jnp.int32, (chunk, LANES), 1)
    pairs = outer_order()

    def block(i):
        return i // per, slice((i % per) * LANES, (i % per + 1) * LANES)

    for i in range(OUTER):
        device, lanes = block(i)
        turn[i] = pltpu.roll(got_ref[device, 1, :, lanes], part, 1)
    for at in range(0, rows, chunk):
        span = slice(at, at + chunk)
        parts = []
        for i in range(OUTER):
            device, lanes = block(i)
            now = turn[(i - whole + OUTER) % OUTER, span, :]
            before = turn[(i - whole - 1 + OUTER) % OUTER, span, :]
            parts.append(jnp.where(lane >= part, now, before) - got_ref[device, 0, span, lanes])
        modes = fast_hartley(parts)
        for m in range(PAIRS):
            work[m, span, :LANES] = modes[pairs[m, 0]]
            work[m, span, LANES:] = modes[pairs[m, 1]]
    for m in range(PAIRS):
        got = split_dot(work[m], high_ref[m], low_ref[m], ((1,), (0,)))
        per_field = rows // fields
        got = jnp.concatenate(
            [
                got[f * per_field : (f + 1) * per_field] * blend_ref[m, f : f + 1, :]
                for f in range(fields)
            ],
            axis=0,
        )
        work[m] = split_dot(got, high_ref[m], low_ref[m], ((1,), (1,)))
    back = (LANES - part) % LANES
    for at in range(0, rows, chunk):
        span = slice(at, at + chunk)
        modes = [None] * OUTER
        for m in range(PAIRS):
            modes[pairs[m, 0]] = work[m, span, :LANES]
            modes[pairs[m, 1]] = work[m, span, LANES:]
        parts = fast_hartley(modes)
        for i in range(OUTER):
            device, lanes = block(i)
            out_ref[device, 0, span, lanes] = parts[i]
            turn[i, span, :] = pltpu.roll(parts[i], back, 1)
        for i in range(OUTER):
            device, lanes = block(i)
            now = turn[(i + whole) % OUTER, span, :]
            after = turn[(i + whole + 1) % OUTER, span, :]
            out_ref[device, 1, span, lanes] = jnp.where(lane < LANES - part, now, after)


def transform(received, offset, blend, fields):
    high, low = mode_tables()
    count, _, rows, cols = received.shape
    vmem = pl.BlockSpec(memory_space=pltpu.VMEM)
    return pl.pallas_call(
        functools.partial(transform_kernel, fields),
        out_shape=jax.ShapeDtypeStruct(received.shape, jnp.float32),
        in_specs=[pl.BlockSpec(memory_space=pltpu.SMEM)] + [vmem] * 4,
        out_specs=vmem,
        scratch_shapes=[
            pltpu.VMEM((OUTER, rows, LANES), jnp.float32),
            pltpu.VMEM((PAIRS, rows, 2 * LANES), jnp.float32),
        ],
        compiler_params=pltpu.CompilerParams(vmem_limit_bytes=NARROW),
        cost_estimate=pl.CostEstimate(
            flops=12 * rows * PAIRS * 4 * LANES * LANES, bytes_accessed=5_000_000, transcendentals=0
        ),
        name="modes",
    )(offset, received, blend, jnp.asarray(high), jnp.asarray(low))


def planes_kernel(stator, rotor, out):
    count, _, _, _, step, _ = out.shape
    for q in range(count):
        span = slice(q * step, (q + 1) * step)
        for ghost in range(2):
            out[q, 0, :, ghost] = stator[:, 1 - ghost, span, :]
            out[q, 1, :, ghost] = rotor[:, ghost, span, :]


def interface_planes(stator, rotor, count):
    fields, layers, rows, cols = stator.shape
    step = rows // count
    group = max(1, count // 2)
    block = (fields, 2, group * step, cols)
    return pl.pallas_call(
        planes_kernel,
        grid=(count // group,),
        out_shape=jax.ShapeDtypeStruct((count, 2, fields, 2, step, cols), jnp.float32),
        in_specs=[
            pl.BlockSpec(block, lambda q: (0, layers // 2 - 1, q, 0)),
            pl.BlockSpec(block, lambda q: (0, 0, q, 0)),
        ],
        out_specs=pl.BlockSpec((group, 2, fields, 2, step, cols), lambda q: (q, 0, 0, 0, 0, 0)),
        compiler_params=pltpu.CompilerParams(vmem_limit_bytes=WIDE),
        name="planes",
    )(stator, rotor)


def pack_kernel(stator_ref, rotor_ref, low_ref, high_ref, left_ref, right_ref):
    fields, layers, rows, cols = stator_ref.shape
    lane = lax.broadcasted_iota(jnp.int32, (rows, LANES), 1)
    for layer in range(layers):
        for side, ref in enumerate((stator_ref, rotor_ref)):
            taken = layer if side == 0 else layers - 1 - layer
            unit = 2 * (pl.program_id(0) * layers + layer) + side
            place, first = unit // UNITS, unit % UNITS * (2 * fields)
            left = jnp.zeros((rows, LANES), jnp.float32)
            right = jnp.zeros((rows, LANES), jnp.float32)
            for f in range(fields):
                low_ref[side, layer, f] = ref[f, taken, :2, :]
                high_ref[side, layer, f] = ref[f, taken, rows - 2 :, :]
                ends = jnp.where(
                    lane < LANES // 2, ref[f, taken, :, :LANES], ref[f, taken, :, cols - LANES :]
                )
                ends = pltpu.roll(ends, 2 * f, 1) if f else ends
                left = jnp.where(lane // 2 == f, ends, left)
                right = jnp.where(lane // 2 == (f - 1) % (LANES // 2), ends, right)
            fresh = (lane >= first) & (lane < first + 2 * fields)
            left_ref[place] = jnp.where(fresh, pltpu.roll(left, first, 1), left_ref[place])
            after = jnp.where(lane < LANES - 2, lane + 2, lane + 2 - LANES)
            fresh = (after >= first) & (after < first + 2 * fields)
            right_ref[place] = jnp.where(fresh, pltpu.roll(right, first, 1), right_ref[place])


def pack_edges(stator, rotor):
    fields, layers, rows, cols = stator.shape
    blocks = -(-2 * layers // UNITS)
    each = max(n for n in (4, 2, 1) if layers % n == 0)
    steps = layers // each
    block = (fields, each, rows, cols)
    edge = jax.ShapeDtypeStruct((2, layers, fields, 2, cols), jnp.float32)
    side = jax.ShapeDtypeStruct((blocks, rows, LANES), jnp.float32)
    edge_spec = pl.BlockSpec((2, each, fields, 2, cols), lambda t: (0, t, 0, 0, 0))
    side_spec = pl.BlockSpec((blocks, rows, LANES), lambda t: (0, 0, 0))
    return pl.pallas_call(
        pack_kernel,
        grid=(steps,),
        out_shape=(edge, edge, side, side),
        in_specs=[
            pl.BlockSpec(block, lambda t: (0, t, 0, 0)),
            pl.BlockSpec(block, lambda t: (0, steps - 1 - t, 0, 0)),
        ],
        out_specs=(edge_spec, edge_spec, side_spec, side_spec),
        compiler_params=pltpu.CompilerParams(vmem_limit_bytes=WIDE),
        cost_estimate=pl.CostEstimate(
            flops=0, bytes_accessed=2 * 4 * stator.size, transcendentals=0
        ),
        name="edges",
    )(stator, rotor)


def difference_tables(rows, cols):
    scale = time_step * damping
    slope = {1: -0.5 * time_step, -1: 0.5 * time_step}
    smooth = {0: -6.0 * scale, 1: 4.0 * scale, -1: 4.0 * scale, 2: -scale, -2: -scale}

    def banded(extent, halo_places, halo_width):
        whole = np.zeros((2, extent, extent))
        halo = np.zeros((2, extent, halo_width))
        for which, taps in enumerate((slope, smooth)):
            for i in range(extent):
                for shift, value in taps.items():
                    j = i + shift
                    if 0 <= j < extent:
                        whole[which, i, j] += value
                    else:
                        halo[which, i, halo_places[j if j < 0 else j - extent]] += value
        return whole.reshape(2 * extent, extent), halo.reshape(2 * extent, halo_width)

    main, rim = banded(rows, {-2: 0, -1: 1, 0: 2, 1: 3}, 8)
    along_rows = np.concatenate([main, main, rim, rim], axis=1)
    main, rim = banded(cols, {0: 0, 1: 1, -2: LANES - 2, -1: LANES - 1}, LANES)
    along_cols = np.concatenate([main, main, rim, rim], axis=1).T
    return along_rows.astype(ml_dtypes.bfloat16), along_cols.astype(ml_dtypes.bfloat16)


def halves(x):
    high = x.astype(jnp.bfloat16)
    return high, (x - high.astype(jnp.float32)).astype(jnp.bfloat16)


def stencil_kernel(
    layers, jac_ref, mix_ref, stator_hbm, rotor_hbm, low_ref, high_ref, left_ref, right_ref, rows_ref,
    cols_ref, stator_out, rotor_out, state, radial, pitch, parts, mixer, slopes, sems,
):
    fields, _, rows, cols = stator_out.shape
    chunk, wide = 16, 2 * LANES
    steps = layers // 2
    step = pl.program_id(0)
    sources = (stator_hbm, rotor_hbm)

    def load(side, layer):
        taken = layer if side == 0 else layers - 1 - layer
        return pltpu.make_async_copy(
            sources[side].at[:, taken], state.at[side, :, layer + 2], sems.at[side, layer]
        )

    @pl.when(step == 0)
    def _():
        for side in range(2):
            for layer in range(layers):
                load(side, layer).start()
        state[:, :, 0:2] = jnp.zeros((2, fields, 2, rows, cols), jnp.float32)
        spot = lax.broadcasted_iota(jnp.int32, (chunk, wide), 1)
        own = spot % chunk == lax.broadcasted_iota(jnp.int32, (chunk, wide), 0)
        for f in range(fields):
            axial = jnp.zeros((chunk, wide), jnp.float32)
            others = jnp.zeros((chunk, wide), jnp.float32)
            for d in range(3):
                for g in range(fields):
                    here = own & (spot // chunk == d * fields + g)
                    entry = jnp.where(here, jac_ref[(d * fields + f) * fields + g], 0.0)
                    if d == 0:
                        axial = axial + entry
                    else:
                        others = others + entry
            band = slice(f * chunk, (f + 1) * chunk)
            for side in range(2):
                high, low = halves(others + axial * ((0.5 if side else -0.5) * time_step))
                mixer[side, band, :wide] = high
                mixer[side, band, wide : 2 * wide] = high
                mixer[side, band, 2 * wide :] = low
        used = 3 * fields * chunk
        blank = jnp.zeros((2, rows // chunk, wide - used, cols), jnp.bfloat16)
        slopes[:, :, used:wide, :] = blank
        slopes[:, :, wide + used :, :] = blank

    for side, out in enumerate((stator_out, rotor_out)):

        @pl.when(step // steps == side)
        def _():
            stencil_step(
                side, step - side * steps, layers, functools.partial(load, side), mix_ref, low_ref.at[side],
                high_ref.at[side], left_ref, right_ref, rows_ref, cols_ref, out, state.at[side], radial,
                pitch, parts, mixer.at[side], slopes,
            )


def stencil_step(
    side, step, layers, load, mix_ref, low_ref, high_ref, left_ref, right_ref, rows_ref, cols_ref,
    out, state, radial, pitch, parts, mixer, slopes,
):
    fields, _, rows, cols = out.shape
    chunk, wide = 16, 2 * LANES
    scale = time_step * damping
    lane = lax.broadcasted_iota(jnp.int32, (rows, LANES), 1)

    def products(t, slot):
        unit = 2 * t + side
        place, first = unit // UNITS, unit % UNITS * (2 * fields)
        from_left, from_right = left_ref[place], right_ref[place]
        for f in range(fields):
            at = first + 2 * f
            before = jnp.where(lane < LANES - 2, lane + 2, lane + 2 - LANES)
            rim = jnp.where((before >= at) & (before < at + 2), from_left, from_right)
            rim = pltpu.roll(rim, (LANES - at) % LANES, 1)
            rim = jnp.where((lane < 2) | (lane >= LANES - 2), rim, 0.0)
            span = slice(f * rows, (f + 1) * rows)
            x_high, x_low = halves(state[f, t + 2])
            rim_high, rim_low = halves(rim)
            parts[span, :cols] = x_high
            parts[span, cols : 2 * cols] = x_low
            parts[span, 2 * cols : 2 * cols + LANES] = rim_high
            parts[span, 2 * cols + LANES :] = rim_low
            halo = jnp.concatenate(
                [low_ref[t, f], high_ref[t, f], jnp.zeros((4, cols), jnp.float32)], axis=0
            )
            halo_high = halo.astype(jnp.bfloat16).astype(jnp.float32)
            halo = jnp.concatenate([halo_high, halo - halo_high], axis=0).astype(jnp.bfloat16)
            radial[slot, f] = jnp.dot(
                rows_ref[...],
                jnp.concatenate([x_high, x_low, halo], axis=0),
                preferred_element_type=jnp.float32,
            )
        pitch[slot] = jnp.dot(parts[...], cols_ref[...], preferred_element_type=jnp.float32)

    def advance(t, slot):
        here = t + 2
        for at in range(0, rows, chunk):
            span = slice(at, at + chunk)
            totals = []
            for f in range(fields):
                near = state[f, here + 1, span, :] + state[f, here - 1, span, :]
                far = state[f, here + 2, span, :] + state[f, here - 2, span, :]
                totals.append(
                    (state[f, here, span, :] * (1.0 - 6.0 * scale) + (near * 4.0 - far) * scale)
                    + (
                        radial[slot, f, rows + at : rows + at + chunk, :]
                        + pitch[slot, f * rows + at : f * rows + at + chunk, cols:]
                    )
                )
            place = at // chunk
            for g in range(fields):
                for d, slope in enumerate(
                    (
                        state[g, here + 1, span, :] - state[g, here - 1, span, :],
                        radial[slot, g, span, :],
                        pitch[slot, g * rows + at : g * rows + at + chunk, :cols],
                    )
                ):
                    first = (d * fields + g) * chunk
                    high, low = halves(slope)
                    slopes[slot, place, first : first + chunk, :] = high
                    slopes[slot, place, wide + first : wide + first + chunk, :] = low
            mixed = jnp.dot(
                mixer[:, : 2 * wide], slopes[slot, place], preferred_element_type=jnp.float32
            ) + jnp.dot(
                mixer[:, 2 * wide :], slopes[slot, place, :wide, :], preferred_element_type=jnp.float32
            )
            for f in range(fields):
                out[f, slot if side == 0 else 1 - slot, span, :] = (
                    totals[f] + mixed[f * chunk : (f + 1) * chunk]
                )

    @pl.when(step == 0)
    def _():
        load(0).wait()
        load(1).wait()

    @pl.when(2 * step + 2 < layers)
    def _():
        load(2 * step + 2).wait()
        load(2 * step + 3).wait()

    @pl.when(2 * step == layers - 2)
    def _():
        for ghost in range(2):
            for at in range(0, rows, chunk):
                span = slice(at, at + chunk)
                planes = [state[g, layers + 1 - ghost, span, :] for g in range(fields)]
                for f in range(fields):
                    total = mix_ref[f, 0] * planes[0]
                    for g in range(1, fields):
                        total = total + mix_ref[f, g] * planes[g]
                    state[f, layers + 2 + ghost, span, :] = total

    for slot in range(2):
        products(2 * step + slot, slot)
    for slot in range(2):
        advance(2 * step + slot, slot)


def stencil(stator, rotor, low, high, left, right, jacobians, mix):
    fields, layers, rows, cols = stator.shape
    along_rows, along_cols = difference_tables(rows, cols)
    steps = layers // 2
    block = (fields, 2, rows, cols)
    smem = pl.BlockSpec(memory_space=pltpu.SMEM)
    vmem = pl.BlockSpec(memory_space=pltpu.VMEM)
    hbm = pl.BlockSpec(memory_space=pl.ANY)
    shape = jax.ShapeDtypeStruct(stator.shape, jnp.float32)
    return pl.pallas_call(
        functools.partial(stencil_kernel, layers),
        grid=(2 * steps,),
        out_shape=(shape, shape),
        in_specs=[smem, smem, hbm, hbm] + [vmem] * 6,
        out_specs=(
            pl.BlockSpec(block, lambda t: (0, jnp.minimum(t, steps - 1), 0, 0)),
            pl.BlockSpec(block, lambda t: (0, steps - 1 - jnp.maximum(t - steps, 0), 0, 0)),
        ),
        scratch_shapes=[
            pltpu.VMEM((2, fields, layers + 4, rows, cols), jnp.float32),
            pltpu.VMEM((2, fields, 2 * rows, cols), jnp.float32),
            pltpu.VMEM((2, fields * rows, 2 * cols), jnp.float32),
            pltpu.VMEM((fields * rows, 2 * cols + 2 * LANES), jnp.bfloat16),
            pltpu.VMEM((2, fields * 16, 6 * LANES), jnp.bfloat16),
            pltpu.VMEM((2, rows // 16, 4 * LANES, cols), jnp.bfloat16),
            pltpu.SemaphoreType.DMA((2, layers)),
        ],
        compiler_params=pltpu.CompilerParams(vmem_limit_bytes=WIDE),
        cost_estimate=pl.CostEstimate(
            flops=120 * stator.size, bytes_accessed=32 * stator.size, transcendentals=0
        ),
        name="stencil",
    )(jacobians, mix, stator, rotor, low, high, left, right, jnp.asarray(along_rows), jnp.asarray(along_cols))


def close_kernel(
    jac_ref, mix_ref, modes_ref, stator_ref, rotor_ref, stator_out, rotor_out, before, after, sems
):
    count, _, fields, _, step, cols = modes_ref.shape
    layers = stator_ref.shape[1]
    pieces, _, _, _, height, _ = before.shape
    group = height // step
    scale = time_step * damping
    refs = ((stator_ref, stator_out, layers - 2), (rotor_ref, rotor_out, 0))

    def spot(side, piece):
        return slice(None), pl.ds(refs[side][2], 2), pl.ds(piece * height, height)

    def fetch(side, piece):
        given = refs[side][0].at[spot(side, piece)]
        return pltpu.make_async_copy(given, before.at[piece, side], sems.at[0, piece, side])

    def store(side, piece):
        out = refs[side][1].at[spot(side, piece)]
        return pltpu.make_async_copy(after.at[piece, side], out, sems.at[1, piece, side])

    def combine(row, sources):
        total = row(0) * sources[0]
        for g in range(1, fields):
            total = total + row(g) * sources[g]
        return total

    order = [(side, piece) for piece in range(pieces) for side in range(2)]
    for side, piece in order:
        fetch(side, piece).start()
    for side, piece in order:
        near, far = (1, 0) if side == 0 else (0, 1)
        sign = -1.0 if side else 1.0
        fetch(side, piece).wait()
        for q in range(group):
            span = slice(q * step, (q + 1) * step)
            ghosts = []
            for ghost in range(2):
                planes = [modes_ref[piece * group + q, side, g, ghost] for g in range(fields)]
                ghosts.append([combine(lambda g: mix_ref[f, g], planes) for f in range(fields)])
            first, second = ghosts
            for f in range(fields):
                slope = combine(lambda g: jac_ref[f * fields + g], first) * (-0.5 * time_step)
                bend = first[f] * 4.0 - second[f]
                after[piece, side, f, near, span, :] = before[piece, side, f, near, span, :] + (
                    slope + bend * (sign * scale)
                )
                after[piece, side, f, far, span, :] = before[piece, side, f, far, span, :] - first[f] * (
                    sign * scale
                )
        store(side, piece).start()
    for side, piece in order:
        store(side, piece).wait()


def close(modes, stator, rotor, jacobians, field_mix):
    fields, layers, rows, cols = stator.shape
    pieces = max(n for n in (4, 2, 1) if rows % (8 * n) == 0 and modes.shape[0] % n == 0)
    smem = pl.BlockSpec(memory_space=pltpu.SMEM)
    hbm = pl.BlockSpec(memory_space=pl.ANY)
    shape = jax.ShapeDtypeStruct(stator.shape, jnp.float32)
    buffer = pltpu.VMEM((pieces, 2, fields, 2, rows // pieces, cols), jnp.float32)
    return pl.pallas_call(
        close_kernel,
        out_shape=(shape, shape),
        in_specs=[smem, smem, pl.BlockSpec(memory_space=pltpu.VMEM), hbm, hbm],
        out_specs=(hbm, hbm),
        scratch_shapes=[buffer, buffer, pltpu.SemaphoreType.DMA((2, pieces, 2))],
        input_output_aliases={3: 0, 4: 1},
        compiler_params=pltpu.CompilerParams(vmem_limit_bytes=NARROW),
        cost_estimate=pl.CostEstimate(
            flops=30 * modes.size, bytes_accessed=12 * modes.size, transcendentals=0
        ),
        name="interface",
    )(jacobians, field_mix, modes, stator, rotor)


def shards(stator, rotor, jacobians, field_mix, mode_blend, rotor_offset):
    fields, layers, rows, cols = stator.shape
    count = lax.axis_size("pitch")
    spans = lax.axis_size("span")
    step = rows // count

    planes = interface_planes(stator, rotor, count).reshape(count, 2, fields * 2 * step, cols)

    planes, *states = lax.optimization_barrier((planes, stator, rotor))
    received = lax.all_to_all(planes, "pitch", 0, 0, tiled=True)
    low, high, left, right = pack_edges(*states)
    ring = [(i, (i + 1) % count) for i in range(count)]
    line = [(i, i + 1) for i in range(spans - 1)]
    from_left = lax.ppermute(right, "pitch", ring)
    from_right = lax.ppermute(left, "pitch", [(b, a) for a, b in ring])
    from_below = lax.ppermute(high, "span", line)
    from_above = lax.ppermute(low, "span", [(b, a) for a, b in line])

    edges = (from_below, from_above, from_left, from_right)
    blend = mode_blend.reshape(fields, LANES, OUTER) * (1.0 / NP)
    blend = jnp.moveaxis(blend, 2, 0)[outer_order().reshape(-1)]
    blend = blend.reshape(PAIRS, 2, fields, LANES).transpose(0, 2, 1, 3).reshape(PAIRS, fields, 2 * LANES)
    received, edges, flat = lax.optimization_barrier((received, edges, jacobians.reshape(-1)))
    sent = transform(received, rotor_offset, blend, fields)
    sent, edges, flat = lax.optimization_barrier((sent, edges, flat))
    modes = lax.all_to_all(sent, "pitch", 0, 0, tiled=True)
    modes = modes.reshape(count, 2, fields, 2, step, cols)
    stator_mid, rotor_mid = stencil(stator, rotor, *edges, flat, field_mix)
    return close(modes, stator_mid, rotor_mid, flat, field_mix)


def solution(mesh):
    block = P(None, None, "span", "pitch")
    in_specs = (block, block, P(), P(), P(), P())
    return jax.shard_map(
        shards, mesh=mesh, in_specs=in_specs, out_specs=(block, block), check_vma=False
    )
```

```python
import functools
import math

import jax
import jax.numpy as jnp
import ml_dtypes
import numpy as np
from jax import lax
from jax.experimental import pallas as pl
from jax.experimental.pallas import tpu as pltpu
from jax.sharding import PartitionSpec as P

NP = 2048
LANES = 128
OUTER = NP // LANES
PAIRS = OUTER // 2
UNITS = 12

time_step = 0.5
damping = 1.0 / 32.0
WIDE = 56 * 1024 * 1024
NARROW = 16 * 1024 * 1024


def mode_tables():
    inner = np.arange(LANES)
    out = np.zeros((PAIRS, 2 * LANES, 2 * LANES))

    def angles(outer):
        return 2.0 * math.pi * (np.outer(inner, outer + OUTER * inner) % NP) / NP

    for m in range(PAIRS):
        first, second = (0, PAIRS) if m == 0 else (m, OUTER - m)
        a, b = angles(first), angles(second)
        if m == 0:
            out[m, :LANES, :LANES] = np.cos(a) + np.sin(a)
            out[m, LANES:, LANES:] = np.cos(b) + np.sin(b)
        else:
            out[m, :LANES, :LANES] = np.cos(a)
            out[m, LANES:, :LANES] = np.sin(a)
            out[m, :LANES, LANES:] = np.sin(b)
            out[m, LANES:, LANES:] = np.cos(b)
    high = out.astype(ml_dtypes.bfloat16)
    low = (out - high.astype(np.float64)).astype(ml_dtypes.bfloat16)
    return high, low


def outer_order():
    order = [(0, PAIRS)] + [(m, OUTER - m) for m in range(1, PAIRS)]
    return np.array(order)


def fast_hartley(parts):
    count = len(parts)
    if count == 1:
        return parts
    half = count // 2
    even = fast_hartley(parts[0::2])
    odd = fast_hartley(parts[1::2])
    turned = []
    for k in range(half):
        if k == 0:
            turned.append(odd[0])
        elif 4 * k == count:
            turned.append(odd[half - k])
        else:
            angle = 2.0 * math.pi * k / count
            turned.append(odd[k] * math.cos(angle) + odd[half - k] * math.sin(angle))
    return [even[k] + turned[k] for k in range(half)] + [even[k] - turned[k] for k in range(half)]


def split_dot(x, high, low, dims):
    x_high = x.astype(jnp.bfloat16)
    x_low = (x - x_high.astype(jnp.float32)).astype(jnp.bfloat16)
    dot = functools.partial(
        lax.dot_general, dimension_numbers=(dims, ((), ())), preferred_element_type=jnp.float32
    )
    rows = x.shape[0]
    both = dot(jnp.concatenate([x_high, x_low], axis=0), high)
    return both[:rows] + (both[rows:] + dot(x_high, low))


def transform_kernel(fields, offset_ref, got_ref, blend_ref, high_ref, low_ref, out_ref, turn, work):
    rows, cols = got_ref.shape[2:]
    per = cols // LANES
    offset = offset_ref[0]
    whole, part = offset // LANES, offset % LANES
    chunk = 8 if rows % 8 == 0 else rows
    lane = lax.broadcasted_iota(jnp.int32, (chunk, LANES), 1)
    pairs = outer_order()

    def block(i):
        return i // per, slice((i % per) * LANES, (i % per + 1) * LANES)

    for i in range(OUTER):
        device, lanes = block(i)
        turn[i] = pltpu.roll(got_ref[device, 1, :, lanes], part, 1)
    for at in range(0, rows, chunk):
        span = slice(at, at + chunk)
        parts = []
        for i in range(OUTER):
            device, lanes = block(i)
            now = turn[(i - whole + OUTER) % OUTER, span, :]
            before = turn[(i - whole - 1 + OUTER) % OUTER, span, :]
            parts.append(jnp.where(lane >= part, now, before) - got_ref[device, 0, span, lanes])
        modes = fast_hartley(parts)
        for m in range(PAIRS):
            work[m, span, :LANES] = modes[pairs[m, 0]]
            work[m, span, LANES:] = modes[pairs[m, 1]]
    for m in range(PAIRS):
        got = split_dot(work[m], high_ref[m], low_ref[m], ((1,), (0,)))
        per_field = rows // fields
        got = jnp.concatenate(
            [
                got[f * per_field : (f + 1) * per_field] * blend_ref[m, f : f + 1, :]
                for f in range(fields)
            ],
            axis=0,
        )
        work[m] = split_dot(got, high_ref[m], low_ref[m], ((1,), (1,)))
    back = (LANES - part) % LANES
    for at in range(0, rows, chunk):
        span = slice(at, at + chunk)
        modes = [None] * OUTER
        for m in range(PAIRS):
            modes[pairs[m, 0]] = work[m, span, :LANES]
            modes[pairs[m, 1]] = work[m, span, LANES:]
        parts = fast_hartley(modes)
        for i in range(OUTER):
            device, lanes = block(i)
            out_ref[device, 0, span, lanes] = parts[i]
            turn[i, span, :] = pltpu.roll(parts[i], back, 1)
        for i in range(OUTER):
            device, lanes = block(i)
            now = turn[(i + whole) % OUTER, span, :]
            after = turn[(i + whole + 1) % OUTER, span, :]
            out_ref[device, 1, span, lanes] = jnp.where(lane < LANES - part, now, after)


def transform(received, offset, blend, fields):
    high, low = mode_tables()
    count, _, rows, cols = received.shape
    vmem = pl.BlockSpec(memory_space=pltpu.VMEM)
    return pl.pallas_call(
        functools.partial(transform_kernel, fields),
        out_shape=jax.ShapeDtypeStruct(received.shape, jnp.float32),
        in_specs=[pl.BlockSpec(memory_space=pltpu.SMEM)] + [vmem] * 4,
        out_specs=vmem,
        scratch_shapes=[
            pltpu.VMEM((OUTER, rows, LANES), jnp.float32),
            pltpu.VMEM((PAIRS, rows, 2 * LANES), jnp.float32),
        ],
        compiler_params=pltpu.CompilerParams(vmem_limit_bytes=NARROW),
        cost_estimate=pl.CostEstimate(
            flops=12 * rows * PAIRS * 4 * LANES * LANES, bytes_accessed=5_000_000, transcendentals=0
        ),
        name="modes",
    )(offset, received, blend, jnp.asarray(high), jnp.asarray(low))


def planes_kernel(stator, rotor, out):
    count, _, _, _, step, _ = out.shape
    for q in range(count):
        span = slice(q * step, (q + 1) * step)
        for ghost in range(2):
            out[q, 0, :, ghost] = stator[:, 1 - ghost, span, :]
            out[q, 1, :, ghost] = rotor[:, ghost, span, :]


def interface_planes(stator, rotor, count):
    fields, layers, rows, cols = stator.shape
    step = rows // count
    group = max(1, count // 2)
    block = (fields, 2, group * step, cols)
    return pl.pallas_call(
        planes_kernel,
        grid=(count // group,),
        out_shape=jax.ShapeDtypeStruct((count, 2, fields, 2, step, cols), jnp.float32),
        in_specs=[
            pl.BlockSpec(block, lambda q: (0, layers // 2 - 1, q, 0)),
            pl.BlockSpec(block, lambda q: (0, 0, q, 0)),
        ],
        out_specs=pl.BlockSpec((group, 2, fields, 2, step, cols), lambda q: (q, 0, 0, 0, 0, 0)),
        compiler_params=pltpu.CompilerParams(vmem_limit_bytes=WIDE),
        name="planes",
    )(stator, rotor)


def pack_kernel(stator_ref, rotor_ref, low_ref, high_ref, left_ref, right_ref):
    fields, layers, rows, cols = stator_ref.shape
    lane = lax.broadcasted_iota(jnp.int32, (rows, LANES), 1)
    for layer in range(layers):
        for side, ref in enumerate((stator_ref, rotor_ref)):
            taken = layer if side == 0 else layers - 1 - layer
            unit = 2 * (pl.program_id(0) * layers + layer) + side
            place, first = unit // UNITS, unit % UNITS * (2 * fields)
            left = jnp.zeros((rows, LANES), jnp.float32)
            right = jnp.zeros((rows, LANES), jnp.float32)
            for f in range(fields):
                low_ref[side, layer, f] = ref[f, taken, :2, :]
                high_ref[side, layer, f] = ref[f, taken, rows - 2 :, :]
                ends = jnp.where(
                    lane < LANES // 2, ref[f, taken, :, :LANES], ref[f, taken, :, cols - LANES :]
                )
                ends = pltpu.roll(ends, 2 * f, 1) if f else ends
                left = jnp.where(lane // 2 == f, ends, left)
                right = jnp.where(lane // 2 == (f - 1) % (LANES // 2), ends, right)
            fresh = (lane >= first) & (lane < first + 2 * fields)
            left_ref[place] = jnp.where(fresh, pltpu.roll(left, first, 1), left_ref[place])
            after = jnp.where(lane < LANES - 2, lane + 2, lane + 2 - LANES)
            fresh = (after >= first) & (after < first + 2 * fields)
            right_ref[place] = jnp.where(fresh, pltpu.roll(right, first, 1), right_ref[place])


def pack_edges(stator, rotor):
    fields, layers, rows, cols = stator.shape
    blocks = -(-2 * layers // UNITS)
    each = max(n for n in (4, 2, 1) if layers % n == 0)
    steps = layers // each
    block = (fields, each, rows, cols)
    edge = jax.ShapeDtypeStruct((2, layers, fields, 2, cols), jnp.float32)
    side = jax.ShapeDtypeStruct((blocks, rows, LANES), jnp.float32)
    edge_spec = pl.BlockSpec((2, each, fields, 2, cols), lambda t: (0, t, 0, 0, 0))
    side_spec = pl.BlockSpec((blocks, rows, LANES), lambda t: (0, 0, 0))
    return pl.pallas_call(
        pack_kernel,
        grid=(steps,),
        out_shape=(edge, edge, side, side),
        in_specs=[
            pl.BlockSpec(block, lambda t: (0, t, 0, 0)),
            pl.BlockSpec(block, lambda t: (0, steps - 1 - t, 0, 0)),
        ],
        out_specs=(edge_spec, edge_spec, side_spec, side_spec),
        compiler_params=pltpu.CompilerParams(vmem_limit_bytes=WIDE),
        cost_estimate=pl.CostEstimate(
            flops=0, bytes_accessed=2 * 4 * stator.size, transcendentals=0
        ),
        name="edges",
    )(stator, rotor)


def difference_tables(rows, cols):
    scale = time_step * damping
    slope = {1: -0.5 * time_step, -1: 0.5 * time_step}
    smooth = {0: -6.0 * scale, 1: 4.0 * scale, -1: 4.0 * scale, 2: -scale, -2: -scale}

    def banded(extent, halo_places, halo_width):
        whole = np.zeros((2, extent, extent))
        halo = np.zeros((2, extent, halo_width))
        for which, taps in enumerate((slope, smooth)):
            for i in range(extent):
                for shift, value in taps.items():
                    j = i + shift
                    if 0 <= j < extent:
                        whole[which, i, j] += value
                    else:
                        halo[which, i, halo_places[j if j < 0 else j - extent]] += value
        return whole.reshape(2 * extent, extent), halo.reshape(2 * extent, halo_width)

    main, rim = banded(rows, {-2: 0, -1: 1, 0: 2, 1: 3}, 8)
    along_rows = np.concatenate([main, main, rim, rim], axis=1)
    main, rim = banded(cols, {0: 0, 1: 1, -2: LANES - 2, -1: LANES - 1}, LANES)
    along_cols = np.concatenate([main, main, rim, rim], axis=1).T
    return along_rows.astype(ml_dtypes.bfloat16), along_cols.astype(ml_dtypes.bfloat16)


def halves(x):
    high = x.astype(jnp.bfloat16)
    return high, (x - high.astype(jnp.float32)).astype(jnp.bfloat16)


def stencil_kernel(
    layers, jac_ref, mix_ref, stator_hbm, rotor_hbm, low_ref, high_ref, left_ref, right_ref, rows_ref,
    cols_ref, stator_out, rotor_out, state, radial, pitch, parts, mixer, slopes, sems,
):
    fields, _, rows, cols = stator_out.shape
    chunk, wide = 16, 2 * LANES
    steps = layers // 2
    step = pl.program_id(0)
    sources = (stator_hbm, rotor_hbm)

    def load(side, layer):
        taken = layer if side == 0 else layers - 1 - layer
        return pltpu.make_async_copy(
            sources[side].at[:, taken], state.at[side, :, layer + 2], sems.at[side, layer]
        )

    @pl.when(step == 0)
    def _():
        for side in range(2):
            for layer in range(layers):
                load(side, layer).start()
        state[:, :, 0:2] = jnp.zeros((2, fields, 2, rows, cols), jnp.float32)
        spot = lax.broadcasted_iota(jnp.int32, (chunk, wide), 1)
        own = spot % chunk == lax.broadcasted_iota(jnp.int32, (chunk, wide), 0)
        for f in range(fields):
            axial = jnp.zeros((chunk, wide), jnp.float32)
            others = jnp.zeros((chunk, wide), jnp.float32)
            for d in range(3):
                for g in range(fields):
                    here = own & (spot // chunk == d * fields + g)
                    entry = jnp.where(here, jac_ref[(d * fields + f) * fields + g], 0.0)
                    if d == 0:
                        axial = axial + entry
                    else:
                        others = others + entry
            band = slice(f * chunk, (f + 1) * chunk)
            for side in range(2):
                high, low = halves(others + axial * ((0.5 if side else -0.5) * time_step))
                mixer[side, band, :wide] = high
                mixer[side, band, wide : 2 * wide] = high
                mixer[side, band, 2 * wide :] = low
        used = 3 * fields * chunk
        blank = jnp.zeros((2, rows // chunk, wide - used, cols), jnp.bfloat16)
        slopes[:, :, used:wide, :] = blank
        slopes[:, :, wide + used :, :] = blank

    for side, out in enumerate((stator_out, rotor_out)):

        @pl.when(step // steps == side)
        def _():
            stencil_step(
                side, step - side * steps, layers, functools.partial(load, side), mix_ref, low_ref.at[side],
                high_ref.at[side], left_ref, right_ref, rows_ref, cols_ref, out, state.at[side], radial,
                pitch, parts, mixer.at[side], slopes,
            )


def stencil_step(
    side, step, layers, load, mix_ref, low_ref, high_ref, left_ref, right_ref, rows_ref, cols_ref,
    out, state, radial, pitch, parts, mixer, slopes,
):
    fields, _, rows, cols = out.shape
    chunk, wide = 16, 2 * LANES
    scale = time_step * damping
    lane = lax.broadcasted_iota(jnp.int32, (rows, LANES), 1)

    def products(t, slot):
        unit = 2 * t + side
        place, first = unit // UNITS, unit % UNITS * (2 * fields)
        from_left, from_right = left_ref[place], right_ref[place]
        for f in range(fields):
            at = first + 2 * f
            before = jnp.where(lane < LANES - 2, lane + 2, lane + 2 - LANES)
            rim = jnp.where((before >= at) & (before < at + 2), from_left, from_right)
            rim = pltpu.roll(rim, (LANES - at) % LANES, 1)
            rim = jnp.where((lane < 2) | (lane >= LANES - 2), rim, 0.0)
            span = slice(f * rows, (f + 1) * rows)
            x_high, x_low = halves(state[f, t + 2])
            rim_high, rim_low = halves(rim)
            parts[span, :cols] = x_high
            parts[span, cols : 2 * cols] = x_low
            parts[span, 2 * cols : 2 * cols + LANES] = rim_high
            parts[span, 2 * cols + LANES :] = rim_low
            halo = jnp.concatenate(
                [low_ref[t, f], high_ref[t, f], jnp.zeros((4, cols), jnp.float32)], axis=0
            )
            halo_high = halo.astype(jnp.bfloat16).astype(jnp.float32)
            halo = jnp.concatenate([halo_high, halo - halo_high], axis=0).astype(jnp.bfloat16)
            radial[slot, f] = jnp.dot(
                rows_ref[...],
                jnp.concatenate([x_high, x_low, halo], axis=0),
                preferred_element_type=jnp.float32,
            )
        pitch[slot] = jnp.dot(parts[...], cols_ref[...], preferred_element_type=jnp.float32)

    def advance(t, slot):
        here = t + 2
        for at in range(0, rows, chunk):
            span = slice(at, at + chunk)
            totals = []
            for f in range(fields):
                near = state[f, here + 1, span, :] + state[f, here - 1, span, :]
                far = state[f, here + 2, span, :] + state[f, here - 2, span, :]
                totals.append(
                    (state[f, here, span, :] * (1.0 - 6.0 * scale) + (near * 4.0 - far) * scale)
                    + (
                        radial[slot, f, rows + at : rows + at + chunk, :]
                        + pitch[slot, f * rows + at : f * rows + at + chunk, cols:]
                    )
                )
            place = at // chunk
            for g in range(fields):
                for d, slope in enumerate(
                    (
                        state[g, here + 1, span, :] - state[g, here - 1, span, :],
                        radial[slot, g, span, :],
                        pitch[slot, g * rows + at : g * rows + at + chunk, :cols],
                    )
                ):
                    first = (d * fields + g) * chunk
                    high, low = halves(slope)
                    slopes[slot, place, first : first + chunk, :] = high
                    slopes[slot, place, wide + first : wide + first + chunk, :] = low
            mixed = jnp.dot(
                mixer[:, : 2 * wide], slopes[slot, place], preferred_element_type=jnp.float32
            ) + jnp.dot(
                mixer[:, 2 * wide :], slopes[slot, place, :wide, :], preferred_element_type=jnp.float32
            )
            for f in range(fields):
                out[f, slot if side == 0 else 1 - slot, span, :] = (
                    totals[f] + mixed[f * chunk : (f + 1) * chunk]
                )

    @pl.when(step == 0)
    def _():
        load(0).wait()
        load(1).wait()

    @pl.when(2 * step + 2 < layers)
    def _():
        load(2 * step + 2).wait()
        load(2 * step + 3).wait()

    @pl.when(2 * step == layers - 2)
    def _():
        for ghost in range(2):
            for at in range(0, rows, chunk):
                span = slice(at, at + chunk)
                planes = [state[g, layers + 1 - ghost, span, :] for g in range(fields)]
                for f in range(fields):
                    total = mix_ref[f, 0] * planes[0]
                    for g in range(1, fields):
                        total = total + mix_ref[f, g] * planes[g]
                    state[f, layers + 2 + ghost, span, :] = total

    for slot in range(2):
        products(2 * step + slot, slot)
    for slot in range(2):
        advance(2 * step + slot, slot)


def stencil(stator, rotor, low, high, left, right, jacobians, mix):
    fields, layers, rows, cols = stator.shape
    along_rows, along_cols = difference_tables(rows, cols)
    steps = layers // 2
    block = (fields, 2, rows, cols)
    smem = pl.BlockSpec(memory_space=pltpu.SMEM)
    vmem = pl.BlockSpec(memory_space=pltpu.VMEM)
    hbm = pl.BlockSpec(memory_space=pl.ANY)
    shape = jax.ShapeDtypeStruct(stator.shape, jnp.float32)
    return pl.pallas_call(
        functools.partial(stencil_kernel, layers),
        grid=(2 * steps,),
        out_shape=(shape, shape),
        in_specs=[smem, smem, hbm, hbm] + [vmem] * 6,
        out_specs=(
            pl.BlockSpec(block, lambda t: (0, jnp.minimum(t, steps - 1), 0, 0)),
            pl.BlockSpec(block, lambda t: (0, steps - 1 - jnp.maximum(t - steps, 0), 0, 0)),
        ),
        scratch_shapes=[
            pltpu.VMEM((2, fields, layers + 4, rows, cols), jnp.float32),
            pltpu.VMEM((2, fields, 2 * rows, cols), jnp.float32),
            pltpu.VMEM((2, fields * rows, 2 * cols), jnp.float32),
            pltpu.VMEM((fields * rows, 2 * cols + 2 * LANES), jnp.bfloat16),
            pltpu.VMEM((2, fields * 16, 6 * LANES), jnp.bfloat16),
            pltpu.VMEM((2, rows // 16, 4 * LANES, cols), jnp.bfloat16),
            pltpu.SemaphoreType.DMA((2, layers)),
        ],
        compiler_params=pltpu.CompilerParams(vmem_limit_bytes=WIDE),
        cost_estimate=pl.CostEstimate(
            flops=120 * stator.size, bytes_accessed=32 * stator.size, transcendentals=0
        ),
        name="stencil",
    )(jacobians, mix, stator, rotor, low, high, left, right, jnp.asarray(along_rows), jnp.asarray(along_cols))


def close_kernel(
    jac_ref, mix_ref, modes_ref, stator_ref, rotor_ref, stator_out, rotor_out, before, after, sems
):
    count, _, fields, _, step, cols = modes_ref.shape
    layers = stator_ref.shape[1]
    pieces, _, _, _, height, _ = before.shape
    group = height // step
    scale = time_step * damping
    refs = ((stator_ref, stator_out, layers - 2), (rotor_ref, rotor_out, 0))

    def spot(side, piece):
        return slice(None), pl.ds(refs[side][2], 2), pl.ds(piece * height, height)

    def fetch(side, piece):
        given = refs[side][0].at[spot(side, piece)]
        return pltpu.make_async_copy(given, before.at[piece, side], sems.at[0, piece, side])

    def store(side, piece):
        out = refs[side][1].at[spot(side, piece)]
        return pltpu.make_async_copy(after.at[piece, side], out, sems.at[1, piece, side])

    def combine(row, sources):
        total = row(0) * sources[0]
        for g in range(1, fields):
            total = total + row(g) * sources[g]
        return total

    order = [(side, piece) for piece in range(pieces) for side in range(2)]
    for side, piece in order:
        fetch(side, piece).start()
    for side, piece in order:
        near, far = (1, 0) if side == 0 else (0, 1)
        sign = -1.0 if side else 1.0

        def plane(g, ghost):
            return modes_ref[piece * group : (piece + 1) * group, side, g, ghost].reshape(height, cols)

        planes = [plane(g, 0) for g in range(fields)]
        first = [combine(lambda g: mix_ref[f, g], planes) for f in range(fields)]
        fetch(side, piece).wait()
        planes = [plane(g, 1) for g in range(fields)]
        for f in range(fields):
            second = combine(lambda g: mix_ref[f, g], planes)
            slope = combine(lambda g: jac_ref[f * fields + g], first) * (-0.5 * time_step)
            bend = first[f] * 4.0 - second
            after[piece, side, f, near] = before[piece, side, f, near] + (slope + bend * (sign * scale))
            after[piece, side, f, far] = before[piece, side, f, far] - first[f] * (sign * scale)
        store(side, piece).start()
    for side, piece in order:
        store(side, piece).wait()


def close(modes, stator, rotor, jacobians, field_mix):
    fields, layers, rows, cols = stator.shape
    pieces = max(n for n in (4, 2, 1) if rows % (8 * n) == 0 and modes.shape[0] % n == 0)
    smem = pl.BlockSpec(memory_space=pltpu.SMEM)
    hbm = pl.BlockSpec(memory_space=pl.ANY)
    shape = jax.ShapeDtypeStruct(stator.shape, jnp.float32)
    buffer = pltpu.VMEM((pieces, 2, fields, 2, rows // pieces, cols), jnp.float32)
    return pl.pallas_call(
        close_kernel,
        out_shape=(shape, shape),
        in_specs=[smem, smem, pl.BlockSpec(memory_space=pltpu.VMEM), hbm, hbm],
        out_specs=(hbm, hbm),
        scratch_shapes=[buffer, buffer, pltpu.SemaphoreType.DMA((2, pieces, 2))],
        input_output_aliases={3: 0, 4: 1},
        compiler_params=pltpu.CompilerParams(vmem_limit_bytes=NARROW),
        cost_estimate=pl.CostEstimate(
            flops=30 * modes.size, bytes_accessed=12 * modes.size, transcendentals=0
        ),
        name="interface",
    )(jacobians, field_mix, modes, stator, rotor)


def shards(stator, rotor, jacobians, field_mix, mode_blend, rotor_offset):
    fields, layers, rows, cols = stator.shape
    count = lax.axis_size("pitch")
    spans = lax.axis_size("span")
    step = rows // count

    planes = interface_planes(stator, rotor, count).reshape(count, 2, fields * 2 * step, cols)

    planes, *states = lax.optimization_barrier((planes, stator, rotor))
    received = lax.all_to_all(planes, "pitch", 0, 0, tiled=True)
    low, high, left, right = pack_edges(*states)
    ring = [(i, (i + 1) % count) for i in range(count)]
    line = [(i, i + 1) for i in range(spans - 1)]
    from_left = lax.ppermute(right, "pitch", ring)
    from_right = lax.ppermute(left, "pitch", [(b, a) for a, b in ring])
    from_below = lax.ppermute(high, "span", line)
    from_above = lax.ppermute(low, "span", [(b, a) for a, b in line])

    edges = (from_below, from_above, from_left, from_right)
    blend = mode_blend.reshape(fields, LANES, OUTER) * (1.0 / NP)
    blend = jnp.moveaxis(blend, 2, 0)[outer_order().reshape(-1)]
    blend = blend.reshape(PAIRS, 2, fields, LANES).transpose(0, 2, 1, 3).reshape(PAIRS, fields, 2 * LANES)
    received, edges, flat = lax.optimization_barrier((received, edges, jacobians.reshape(-1)))
    sent = transform(received, rotor_offset, blend, fields)
    sent, edges, flat = lax.optimization_barrier((sent, edges, flat))
    modes = lax.all_to_all(sent, "pitch", 0, 0, tiled=True)
    modes = modes.reshape(count, 2, fields, 2, step, cols)
    stator_mid, rotor_mid = stencil(stator, rotor, *edges, flat, field_mix)
    return close(modes, stator_mid, rotor_mid, flat, field_mix)


def solution(mesh):
    block = P(None, None, "span", "pitch")
    in_specs = (block, block, P(), P(), P(), P())
    return jax.shard_map(
        shards, mesh=mesh, in_specs=in_specs, out_specs=(block, block), check_vma=False
    )
```

```python
import functools
import math

import jax
import jax.numpy as jnp
import ml_dtypes
import numpy as np
from jax import lax
from jax.experimental import pallas as pl
from jax.experimental.pallas import tpu as pltpu
from jax.sharding import PartitionSpec as P

NP = 2048
LANES = 128
OUTER = NP // LANES
PAIRS = OUTER // 2
UNITS = 12

time_step = 0.5
damping = 1.0 / 32.0
WIDE = 56 * 1024 * 1024
NARROW = 16 * 1024 * 1024


def mode_tables():
    inner = np.arange(LANES)
    out = np.zeros((PAIRS, 2 * LANES, 2 * LANES))

    def angles(outer):
        return 2.0 * math.pi * (np.outer(inner, outer + OUTER * inner) % NP) / NP

    for m in range(PAIRS):
        first, second = (0, PAIRS) if m == 0 else (m, OUTER - m)
        a, b = angles(first), angles(second)
        if m == 0:
            out[m, :LANES, :LANES] = np.cos(a) + np.sin(a)
            out[m, LANES:, LANES:] = np.cos(b) + np.sin(b)
        else:
            out[m, :LANES, :LANES] = np.cos(a)
            out[m, LANES:, :LANES] = np.sin(a)
            out[m, :LANES, LANES:] = np.sin(b)
            out[m, LANES:, LANES:] = np.cos(b)
    high = out.astype(ml_dtypes.bfloat16)
    low = (out - high.astype(np.float64)).astype(ml_dtypes.bfloat16)
    return high, low


def outer_order():
    order = [(0, PAIRS)] + [(m, OUTER - m) for m in range(1, PAIRS)]
    return np.array(order)


def fast_hartley(parts):
    count = len(parts)
    if count == 1:
        return parts
    half = count // 2
    even = fast_hartley(parts[0::2])
    odd = fast_hartley(parts[1::2])
    turned = []
    for k in range(half):
        if k == 0:
            turned.append(odd[0])
        elif 4 * k == count:
            turned.append(odd[half - k])
        else:
            angle = 2.0 * math.pi * k / count
            turned.append(odd[k] * math.cos(angle) + odd[half - k] * math.sin(angle))
    return [even[k] + turned[k] for k in range(half)] + [even[k] - turned[k] for k in range(half)]


def split_dot(x, high, low, dims):
    x_high = x.astype(jnp.bfloat16)
    x_low = (x - x_high.astype(jnp.float32)).astype(jnp.bfloat16)
    dot = functools.partial(
        lax.dot_general, dimension_numbers=(dims, ((), ())), preferred_element_type=jnp.float32
    )
    rows = x.shape[0]
    both = dot(jnp.concatenate([x_high, x_low], axis=0), high)
    return both[:rows] + (both[rows:] + dot(x_high, low))


def transform_kernel(fields, offset_ref, got_ref, blend_ref, high_ref, low_ref, out_ref, turn, work):
    rows, cols = got_ref.shape[2:]
    per = cols // LANES
    offset = offset_ref[0]
    whole, part = offset // LANES, offset % LANES
    chunk = 8 if rows % 8 == 0 else rows
    lane = lax.broadcasted_iota(jnp.int32, (chunk, LANES), 1)
    pairs = outer_order()

    def block(i):
        return i // per, slice((i % per) * LANES, (i % per + 1) * LANES)

    for i in range(OUTER):
        device, lanes = block(i)
        turn[i] = pltpu.roll(got_ref[device, 1, :, lanes], part, 1)
    for at in range(0, rows, chunk):
        span = slice(at, at + chunk)
        parts = []
        for i in range(OUTER):
            device, lanes = block(i)
            now = turn[(i - whole + OUTER) % OUTER, span, :]
            before = turn[(i - whole - 1 + OUTER) % OUTER, span, :]
            parts.append(jnp.where(lane >= part, now, before) - got_ref[device, 0, span, lanes])
        modes = fast_hartley(parts)
        for m in range(PAIRS):
            work[m, span, :LANES] = modes[pairs[m, 0]]
            work[m, span, LANES:] = modes[pairs[m, 1]]
    for m in range(PAIRS):
        got = split_dot(work[m], high_ref[m], low_ref[m], ((1,), (0,)))
        per_field = rows // fields
        got = jnp.concatenate(
            [
                got[f * per_field : (f + 1) * per_field] * blend_ref[m, f : f + 1, :]
                for f in range(fields)
            ],
            axis=0,
        )
        work[m] = split_dot(got, high_ref[m], low_ref[m], ((1,), (1,)))
    back = (LANES - part) % LANES
    for at in range(0, rows, chunk):
        span = slice(at, at + chunk)
        modes = [None] * OUTER
        for m in range(PAIRS):
            modes[pairs[m, 0]] = work[m, span, :LANES]
            modes[pairs[m, 1]] = work[m, span, LANES:]
        parts = fast_hartley(modes)
        for i in range(OUTER):
            device, lanes = block(i)
            out_ref[device, 0, span, lanes] = parts[i]
            turn[i, span, :] = pltpu.roll(parts[i], back, 1)
        for i in range(OUTER):
            device, lanes = block(i)
            now = turn[(i + whole) % OUTER, span, :]
            after = turn[(i + whole + 1) % OUTER, span, :]
            out_ref[device, 1, span, lanes] = jnp.where(lane < LANES - part, now, after)


def transform(received, offset, blend, fields):
    high, low = mode_tables()
    count, _, rows, cols = received.shape
    vmem = pl.BlockSpec(memory_space=pltpu.VMEM)
    return pl.pallas_call(
        functools.partial(transform_kernel, fields),
        out_shape=jax.ShapeDtypeStruct(received.shape, jnp.float32),
        in_specs=[pl.BlockSpec(memory_space=pltpu.SMEM)] + [vmem] * 4,
        out_specs=vmem,
        scratch_shapes=[
            pltpu.VMEM((OUTER, rows, LANES), jnp.float32),
            pltpu.VMEM((PAIRS, rows, 2 * LANES), jnp.float32),
        ],
        compiler_params=pltpu.CompilerParams(vmem_limit_bytes=NARROW),
        cost_estimate=pl.CostEstimate(
            flops=12 * rows * PAIRS * 4 * LANES * LANES, bytes_accessed=5_000_000, transcendentals=0
        ),
        name="modes",
    )(offset, received, blend, jnp.asarray(high), jnp.asarray(low))


def planes_kernel(stator, rotor, out):
    count, _, _, _, step, _ = out.shape
    for q in range(count):
        span = slice(q * step, (q + 1) * step)
        for ghost in range(2):
            out[q, 0, :, ghost] = stator[:, 1 - ghost, span, :]
            out[q, 1, :, ghost] = rotor[:, ghost, span, :]


def planes_copy_kernel(stator, rotor, out, held, sems, stores):
    count, _, _, _, step, _ = out.shape
    layers = stator.shape[1]

    def load(side, ghost):
        source = stator.at[:, layers - 1 - ghost] if side == 0 else rotor.at[:, ghost]
        return pltpu.make_async_copy(source, held.at[side, ghost], sems.at[side, ghost])

    def store(side, ghost, q):
        source = held.at[side, ghost, :, pl.ds(q * step, step)]
        return pltpu.make_async_copy(source, out.at[q, side, :, ghost], stores.at[side, ghost, q])

    order = [(side, ghost) for side in range(2) for ghost in range(2)]
    for plane in order:
        load(*plane).start()
    for plane in order:
        load(*plane).wait()
        for q in range(count):
            store(*plane, q).start()
    for plane in order:
        for q in range(count):
            store(*plane, q).wait()


def interface_planes(stator, rotor, count):
    fields, layers, rows, cols = stator.shape
    step = rows // count
    if step % 8 == 0:
        hbm = pl.BlockSpec(memory_space=pl.ANY)
        return pl.pallas_call(
            planes_copy_kernel,
            out_shape=jax.ShapeDtypeStruct((count, 2, fields, 2, step, cols), jnp.float32),
            in_specs=[hbm, hbm],
            out_specs=hbm,
            scratch_shapes=[
                pltpu.VMEM((2, 2, fields, rows, cols), jnp.float32),
                pltpu.SemaphoreType.DMA((2, 2)),
                pltpu.SemaphoreType.DMA((2, 2, count)),
            ],
            compiler_params=pltpu.CompilerParams(vmem_limit_bytes=WIDE),
            name="planes",
        )(stator, rotor)
    group = max(1, count // 2)
    block = (fields, 2, group * step, cols)
    return pl.pallas_call(
        planes_kernel,
        grid=(count // group,),
        out_shape=jax.ShapeDtypeStruct((count, 2, fields, 2, step, cols), jnp.float32),
        in_specs=[
            pl.BlockSpec(block, lambda q: (0, layers // 2 - 1, q, 0)),
            pl.BlockSpec(block, lambda q: (0, 0, q, 0)),
        ],
        out_specs=pl.BlockSpec((group, 2, fields, 2, step, cols), lambda q: (q, 0, 0, 0, 0, 0)),
        compiler_params=pltpu.CompilerParams(vmem_limit_bytes=WIDE),
        name="planes",
    )(stator, rotor)


def pack_kernel(stator_ref, rotor_ref, low_ref, high_ref, left_ref, right_ref):
    fields, layers, rows, cols = stator_ref.shape
    lane = lax.broadcasted_iota(jnp.int32, (rows, LANES), 1)
    for layer in range(layers):
        for side, ref in enumerate((stator_ref, rotor_ref)):
            taken = layer if side == 0 else layers - 1 - layer
            unit = 2 * (pl.program_id(0) * layers + layer) + side
            place, first = unit // UNITS, unit % UNITS * (2 * fields)
            left = jnp.zeros((rows, LANES), jnp.float32)
            right = jnp.zeros((rows, LANES), jnp.float32)
            for f in range(fields):
                low_ref[side, layer, f] = ref[f, taken, :2, :]
                high_ref[side, layer, f] = ref[f, taken, rows - 2 :, :]
                ends = jnp.where(
                    lane < LANES // 2, ref[f, taken, :, :LANES], ref[f, taken, :, cols - LANES :]
                )
                ends = pltpu.roll(ends, 2 * f, 1) if f else ends
                left = jnp.where(lane // 2 == f, ends, left)
                right = jnp.where(lane // 2 == (f - 1) % (LANES // 2), ends, right)
            fresh = (lane >= first) & (lane < first + 2 * fields)
            left_ref[place] = jnp.where(fresh, pltpu.roll(left, first, 1), left_ref[place])
            after = jnp.where(lane < LANES - 2, lane + 2, lane + 2 - LANES)
            fresh = (after >= first) & (after < first + 2 * fields)
            right_ref[place] = jnp.where(fresh, pltpu.roll(right, first, 1), right_ref[place])


def pack_edges(stator, rotor):
    fields, layers, rows, cols = stator.shape
    blocks = -(-2 * layers // UNITS)
    each = max(n for n in (4, 2, 1) if layers % n == 0)
    steps = layers // each
    block = (fields, each, rows, cols)
    edge = jax.ShapeDtypeStruct((2, layers, fields, 2, cols), jnp.float32)
    side = jax.ShapeDtypeStruct((blocks, rows, LANES), jnp.float32)
    edge_spec = pl.BlockSpec((2, each, fields, 2, cols), lambda t: (0, t, 0, 0, 0))
    side_spec = pl.BlockSpec((blocks, rows, LANES), lambda t: (0, 0, 0))
    return pl.pallas_call(
        pack_kernel,
        grid=(steps,),
        out_shape=(edge, edge, side, side),
        in_specs=[
            pl.BlockSpec(block, lambda t: (0, t, 0, 0)),
            pl.BlockSpec(block, lambda t: (0, steps - 1 - t, 0, 0)),
        ],
        out_specs=(edge_spec, edge_spec, side_spec, side_spec),
        compiler_params=pltpu.CompilerParams(vmem_limit_bytes=WIDE),
        cost_estimate=pl.CostEstimate(
            flops=0, bytes_accessed=2 * 4 * stator.size, transcendentals=0
        ),
        name="edges",
    )(stator, rotor)


def difference_tables(rows, cols):
    scale = time_step * damping
    slope = {1: -0.5 * time_step, -1: 0.5 * time_step}
    smooth = {0: -6.0 * scale, 1: 4.0 * scale, -1: 4.0 * scale, 2: -scale, -2: -scale}

    def banded(extent, halo_places, halo_width):
        whole = np.zeros((2, extent, extent))
        halo = np.zeros((2, extent, halo_width))
        for which, taps in enumerate((slope, smooth)):
            for i in range(extent):
                for shift, value in taps.items():
                    j = i + shift
                    if 0 <= j < extent:
                        whole[which, i, j] += value
                    else:
                        halo[which, i, halo_places[j if j < 0 else j - extent]] += value
        return whole.reshape(2 * extent, extent), halo.reshape(2 * extent, halo_width)

    main, rim = banded(rows, {-2: 0, -1: 1, 0: 2, 1: 3}, 8)
    along_rows = np.concatenate([main, main, rim, rim], axis=1)
    main, rim = banded(cols, {0: 0, 1: 1, -2: LANES - 2, -1: LANES - 1}, LANES)
    along_cols = np.concatenate([main, main, rim, rim], axis=1).T
    return along_rows.astype(ml_dtypes.bfloat16), along_cols.astype(ml_dtypes.bfloat16)


def halves(x):
    high = x.astype(jnp.bfloat16)
    return high, (x - high.astype(jnp.float32)).astype(jnp.bfloat16)


def stencil_kernel(
    layers, jac_ref, mix_ref, stator_hbm, rotor_hbm, low_ref, high_ref, left_ref, right_ref, rows_ref,
    cols_ref, stator_out, rotor_out, state, radial, pitch, parts, mixer, slopes, sems,
):
    fields, _, rows, cols = stator_out.shape
    chunk, wide = 16, 2 * LANES
    steps = layers // 2
    step = pl.program_id(0)
    sources = (stator_hbm, rotor_hbm)

    def load(side, layer):
        taken = layer if side == 0 else layers - 1 - layer
        return pltpu.make_async_copy(
            sources[side].at[:, taken], state.at[side, :, layer + 2], sems.at[side, layer]
        )

    @pl.when(step == 0)
    def _():
        for side in range(2):
            for layer in range(layers):
                load(side, layer).start()
        state[:, :, 0:2] = jnp.zeros((2, fields, 2, rows, cols), jnp.float32)
        spot = lax.broadcasted_iota(jnp.int32, (chunk, wide), 1)
        own = spot % chunk == lax.broadcasted_iota(jnp.int32, (chunk, wide), 0)
        for f in range(fields):
            axial = jnp.zeros((chunk, wide), jnp.float32)
            others = jnp.zeros((chunk, wide), jnp.float32)
            for d in range(3):
                for g in range(fields):
                    here = own & (spot // chunk == d * fields + g)
                    entry = jnp.where(here, jac_ref[(d * fields + f) * fields + g], 0.0)
                    if d == 0:
                        axial = axial + entry
                    else:
                        others = others + entry
            band = slice(f * chunk, (f + 1) * chunk)
            for side in range(2):
                high, low = halves(others + axial * ((0.5 if side else -0.5) * time_step))
                mixer[side, band, :wide] = high
                mixer[side, band, wide : 2 * wide] = high
                mixer[side, band, 2 * wide :] = low
        used = 3 * fields * chunk
        blank = jnp.zeros((2, rows // chunk, wide - used, cols), jnp.bfloat16)
        slopes[:, :, used:wide, :] = blank
        slopes[:, :, wide + used :, :] = blank

    for side, out in enumerate((stator_out, rotor_out)):

        @pl.when(step // steps == side)
        def _():
            stencil_step(
                side, step - side * steps, layers, functools.partial(load, side), mix_ref, low_ref.at[side],
                high_ref.at[side], left_ref, right_ref, rows_ref, cols_ref, out, state.at[side], radial,
                pitch, parts, mixer.at[side], slopes,
            )


def stencil_step(
    side, step, layers, load, mix_ref, low_ref, high_ref, left_ref, right_ref, rows_ref, cols_ref,
    out, state, radial, pitch, parts, mixer, slopes,
):
    fields, _, rows, cols = out.shape
    chunk, wide = 16, 2 * LANES
    scale = time_step * damping
    lane = lax.broadcasted_iota(jnp.int32, (rows, LANES), 1)

    def products(t, slot):
        unit = 2 * t + side
        place, first = unit // UNITS, unit % UNITS * (2 * fields)
        from_left, from_right = left_ref[place], right_ref[place]
        for f in range(fields):
            at = first + 2 * f
            before = jnp.where(lane < LANES - 2, lane + 2, lane + 2 - LANES)
            rim = jnp.where((before >= at) & (before < at + 2), from_left, from_right)
            rim = pltpu.roll(rim, (LANES - at) % LANES, 1)
            rim = jnp.where((lane < 2) | (lane >= LANES - 2), rim, 0.0)
            span = slice(f * rows, (f + 1) * rows)
            x_high, x_low = halves(state[f, t + 2])
            rim_high, rim_low = halves(rim)
            parts[span, :cols] = x_high
            parts[span, cols : 2 * cols] = x_low
            parts[span, 2 * cols : 2 * cols + LANES] = rim_high
            parts[span, 2 * cols + LANES :] = rim_low
            halo = jnp.concatenate(
                [low_ref[t, f], high_ref[t, f], jnp.zeros((4, cols), jnp.float32)], axis=0
            )
            halo_high = halo.astype(jnp.bfloat16).astype(jnp.float32)
            halo = jnp.concatenate([halo_high, halo - halo_high], axis=0).astype(jnp.bfloat16)
            radial[slot, f] = jnp.dot(
                rows_ref[...],
                jnp.concatenate([x_high, x_low, halo], axis=0),
                preferred_element_type=jnp.float32,
            )
        pitch[slot] = jnp.dot(parts[...], cols_ref[...], preferred_element_type=jnp.float32)

    def advance(t, slot):
        here = t + 2
        for at in range(0, rows, chunk):
            span = slice(at, at + chunk)
            totals = []
            for f in range(fields):
                near = state[f, here + 1, span, :] + state[f, here - 1, span, :]
                far = state[f, here + 2, span, :] + state[f, here - 2, span, :]
                totals.append(
                    (state[f, here, span, :] * (1.0 - 6.0 * scale) + (near * 4.0 - far) * scale)
                    + (
                        radial[slot, f, rows + at : rows + at + chunk, :]
                        + pitch[slot, f * rows + at : f * rows + at + chunk, cols:]
                    )
                )
            place = at // chunk
            for g in range(fields):
                for d, slope in enumerate(
                    (
                        state[g, here + 1, span, :] - state[g, here - 1, span, :],
                        radial[slot, g, span, :],
                        pitch[slot, g * rows + at : g * rows + at + chunk, :cols],
                    )
                ):
                    first = (d * fields + g) * chunk
                    high, low = halves(slope)
                    slopes[slot, place, first : first + chunk, :] = high
                    slopes[slot, place, wide + first : wide + first + chunk, :] = low
            mixed = jnp.dot(
                mixer[:, : 2 * wide], slopes[slot, place], preferred_element_type=jnp.float32
            ) + jnp.dot(
                mixer[:, 2 * wide :], slopes[slot, place, :wide, :], preferred_element_type=jnp.float32
            )
            for f in range(fields):
                out[f, slot if side == 0 else 1 - slot, span, :] = (
                    totals[f] + mixed[f * chunk : (f + 1) * chunk]
                )

    @pl.when(step == 0)
    def _():
        load(0).wait()
        load(1).wait()

    @pl.when(2 * step + 2 < layers)
    def _():
        load(2 * step + 2).wait()
        load(2 * step + 3).wait()

    @pl.when(2 * step == layers - 2)
    def _():
        for ghost in range(2):
            for at in range(0, rows, chunk):
                span = slice(at, at + chunk)
                planes = [state[g, layers + 1 - ghost, span, :] for g in range(fields)]
                for f in range(fields):
                    total = mix_ref[f, 0] * planes[0]
                    for g in range(1, fields):
                        total = total + mix_ref[f, g] * planes[g]
                    state[f, layers + 2 + ghost, span, :] = total

    for slot in range(2):
        products(2 * step + slot, slot)
    for slot in range(2):
        advance(2 * step + slot, slot)


def stencil(stator, rotor, low, high, left, right, jacobians, mix):
    fields, layers, rows, cols = stator.shape
    along_rows, along_cols = difference_tables(rows, cols)
    steps = layers // 2
    block = (fields, 2, rows, cols)
    smem = pl.BlockSpec(memory_space=pltpu.SMEM)
    vmem = pl.BlockSpec(memory_space=pltpu.VMEM)
    hbm = pl.BlockSpec(memory_space=pl.ANY)
    shape = jax.ShapeDtypeStruct(stator.shape, jnp.float32)
    return pl.pallas_call(
        functools.partial(stencil_kernel, layers),
        grid=(2 * steps,),
        out_shape=(shape, shape),
        in_specs=[smem, smem, hbm, hbm] + [vmem] * 6,
        out_specs=(
            pl.BlockSpec(block, lambda t: (0, jnp.minimum(t, steps - 1), 0, 0)),
            pl.BlockSpec(block, lambda t: (0, steps - 1 - jnp.maximum(t - steps, 0), 0, 0)),
        ),
        scratch_shapes=[
            pltpu.VMEM((2, fields, layers + 4, rows, cols), jnp.float32),
            pltpu.VMEM((2, fields, 2 * rows, cols), jnp.float32),
            pltpu.VMEM((2, fields * rows, 2 * cols), jnp.float32),
            pltpu.VMEM((fields * rows, 2 * cols + 2 * LANES), jnp.bfloat16),
            pltpu.VMEM((2, fields * 16, 6 * LANES), jnp.bfloat16),
            pltpu.VMEM((2, rows // 16, 4 * LANES, cols), jnp.bfloat16),
            pltpu.SemaphoreType.DMA((2, layers)),
        ],
        compiler_params=pltpu.CompilerParams(vmem_limit_bytes=WIDE),
        cost_estimate=pl.CostEstimate(
            flops=120 * stator.size, bytes_accessed=32 * stator.size, transcendentals=0
        ),
        name="stencil",
    )(jacobians, mix, stator, rotor, low, high, left, right, jnp.asarray(along_rows), jnp.asarray(along_cols))


def close_kernel(
    jac_ref, mix_ref, modes_ref, stator_ref, rotor_ref, stator_out, rotor_out, before, after, sems
):
    count, _, fields, _, step, cols = modes_ref.shape
    layers = stator_ref.shape[1]
    pieces, _, _, _, height, _ = before.shape
    group = height // step
    scale = time_step * damping
    refs = ((stator_ref, stator_out, layers - 2), (rotor_ref, rotor_out, 0))

    def spot(side, piece):
        return slice(None), pl.ds(refs[side][2], 2), pl.ds(piece * height, height)

    def fetch(side, piece):
        given = refs[side][0].at[spot(side, piece)]
        return pltpu.make_async_copy(given, before.at[piece, side], sems.at[0, piece, side])

    def store(side, piece):
        out = refs[side][1].at[spot(side, piece)]
        return pltpu.make_async_copy(after.at[piece, side], out, sems.at[1, piece, side])

    def combine(row, sources):
        total = row(0) * sources[0]
        for g in range(1, fields):
            total = total + row(g) * sources[g]
        return total

    order = [(side, piece) for piece in range(pieces) for side in range(2)]
    for side, piece in order:
        fetch(side, piece).start()
    for side, piece in order:
        near, far = (1, 0) if side == 0 else (0, 1)
        sign = -1.0 if side else 1.0

        def plane(g, ghost):
            return modes_ref[piece * group : (piece + 1) * group, side, g, ghost].reshape(height, cols)

        planes = [plane(g, 0) for g in range(fields)]
        first = [combine(lambda g: mix_ref[f, g], planes) for f in range(fields)]
        fetch(side, piece).wait()
        planes = [plane(g, 1) for g in range(fields)]
        for f in range(fields):
            second = combine(lambda g: mix_ref[f, g], planes)
            slope = combine(lambda g: jac_ref[f * fields + g], first) * (-0.5 * time_step)
            bend = first[f] * 4.0 - second
            after[piece, side, f, near] = before[piece, side, f, near] + (slope + bend * (sign * scale))
            after[piece, side, f, far] = before[piece, side, f, far] - first[f] * (sign * scale)
        store(side, piece).start()
    for side, piece in order:
        store(side, piece).wait()


def close(modes, stator, rotor, jacobians, field_mix):
    fields, layers, rows, cols = stator.shape
    pieces = max(n for n in (4, 2, 1) if rows % (8 * n) == 0 and modes.shape[0] % n == 0)
    smem = pl.BlockSpec(memory_space=pltpu.SMEM)
    hbm = pl.BlockSpec(memory_space=pl.ANY)
    shape = jax.ShapeDtypeStruct(stator.shape, jnp.float32)
    buffer = pltpu.VMEM((pieces, 2, fields, 2, rows // pieces, cols), jnp.float32)
    return pl.pallas_call(
        close_kernel,
        out_shape=(shape, shape),
        in_specs=[smem, smem, pl.BlockSpec(memory_space=pltpu.VMEM), hbm, hbm],
        out_specs=(hbm, hbm),
        scratch_shapes=[buffer, buffer, pltpu.SemaphoreType.DMA((2, pieces, 2))],
        input_output_aliases={3: 0, 4: 1},
        compiler_params=pltpu.CompilerParams(vmem_limit_bytes=NARROW),
        cost_estimate=pl.CostEstimate(
            flops=30 * modes.size, bytes_accessed=12 * modes.size, transcendentals=0
        ),
        name="interface",
    )(jacobians, field_mix, modes, stator, rotor)


def shards(stator, rotor, jacobians, field_mix, mode_blend, rotor_offset):
    fields, layers, rows, cols = stator.shape
    count = lax.axis_size("pitch")
    spans = lax.axis_size("span")
    step = rows // count

    planes = interface_planes(stator, rotor, count).reshape(count, 2, fields * 2 * step, cols)

    planes, *states = lax.optimization_barrier((planes, stator, rotor))
    received = lax.all_to_all(planes, "pitch", 0, 0, tiled=True)
    low, high, left, right = pack_edges(*states)
    ring = [(i, (i + 1) % count) for i in range(count)]
    line = [(i, i + 1) for i in range(spans - 1)]
    from_left = lax.ppermute(right, "pitch", ring)
    from_right = lax.ppermute(left, "pitch", [(b, a) for a, b in ring])
    from_below = lax.ppermute(high, "span", line)
    from_above = lax.ppermute(low, "span", [(b, a) for a, b in line])

    edges = (from_below, from_above, from_left, from_right)
    blend = mode_blend.reshape(fields, LANES, OUTER) * (1.0 / NP)
    blend = jnp.moveaxis(blend, 2, 0)[outer_order().reshape(-1)]
    blend = blend.reshape(PAIRS, 2, fields, LANES).transpose(0, 2, 1, 3).reshape(PAIRS, fields, 2 * LANES)
    received, edges, flat = lax.optimization_barrier((received, edges, jacobians.reshape(-1)))
    sent = transform(received, rotor_offset, blend, fields)
    sent, edges, flat = lax.optimization_barrier((sent, edges, flat))
    modes = lax.all_to_all(sent, "pitch", 0, 0, tiled=True)
    modes = modes.reshape(count, 2, fields, 2, step, cols)
    stator_mid, rotor_mid = stencil(stator, rotor, *edges, flat, field_mix)
    return close(modes, stator_mid, rotor_mid, flat, field_mix)


def solution(mesh):
    block = P(None, None, "span", "pitch")
    in_specs = (block, block, P(), P(), P(), P())
    return jax.shard_map(
        shards, mesh=mesh, in_specs=in_specs, out_specs=(block, block), check_vma=False
    )
```
